128 devices in a mesh: row: 16 (over z, x), col: 8 (over y, core).
Axes of the slice: x: 4, y: 4, z: 4, core: 2. Of those that a mesh axis runs over, the one named last changes fastest.
Arguments:
- template_pair: bfloat16 [4, 64, 1024, 1024], P(None, None, 'row', 'col'), may hold values from -6 to 6
- template_feat: bfloat16 [128, 64, 128], P(('row', 'col')), may hold values from -6 to 6
- block_map: int32 [4, 8], replicated, may hold values from 0 to 127
- block_count: int32 [4, 8], replicated, may hold values from 1 to 128
- residue_mask: int32 [4, 1024], replicated, may hold values 0 or 1
- row_embed: bfloat16 [64, 64], replicated, may hold values from -0.75 to 0.75
- col_embed: bfloat16 [64, 64], replicated, may hold values from -0.75 to 0.75
- norm_gain: bfloat16 [64], replicated, may hold values from 0.25 to 1.75
- left_proj: bfloat16 [64, 64], replicated, may hold values from -0.75 to 0.75
- right_proj: bfloat16 [64, 64], replicated, may hold values from -0.75 to 0.75
- gate_proj: bfloat16 [64, 64], replicated, may hold values from -0.75 to 0.75
- out_proj: bfloat16 [64, 64], replicated, may hold values from -0.75 to 0.75
- embed_grad: bfloat16 [64, 1024, 1024], P(None, 'row', 'col'), may hold values from -0.29882812 to 0.29882812
Outputs:
- embedding: bfloat16 [64, 1024, 1024], P(None, 'row', 'col')
- feat_grad: float32 [128, 64, 128], P(('row', 'col'))
The draws below stay inside these ranges and needn't reach their ends.
All inputs are finite; a program needn't handle non-finite values.
Results may differ from the reference program's by a relative error of at most 0.013.
Values may be sent and summed in bfloat16 or wider, within the bound.
No kernel may reach another device: no remote copies, remote signals or barrier semaphores. Data moves between devices by JAX's collectives and lax.ppermute only.
A program may use at most 192 MiB of HBM per device.

```python
import jax
import jax.numpy as jnp
from jax import lax

C = 64
F = 64
BLK = 128
TPL = 4
QB = 8
N = 1024
TB_ALL = 128


def plant(array, own_key, low, largest):
    longest = array.shape.index(max(array.shape))
    spots = []
    for shift in (0, 1):
        where = [jax.random.randint(jax.random.fold_in(own_key, axis), (), 0, length) for axis, length in enumerate(array.shape)]
        where[longest] = (where[longest] + shift) % array.shape[longest]
        spots.append(tuple(where))
    return array.at[spots[0]].set(low).at[spots[1]].set(largest)


def block_scale(rng, extent, split, least, top_value):
    factor_of = 1.0
    for axis_at, parts in split:
        draws = jax.random.uniform(jax.random.fold_in(jax.random.fold_in(rng, 6), axis_at), (parts,), jnp.float32, least / len(split), top_value / len(split))
        factor_of = factor_of * jnp.repeat(jnp.exp(draws), extent[axis_at] // parts).reshape((-1,) + (1,) * (len(extent) - 1 - axis_at))
    return factor_of


def bell_draw(rng, dims, deviation, bound, pieces=(), kind=jnp.bfloat16):
    level = block_scale(rng, dims, pieces, -0.22, 0.18) if pieces else 1.0
    drawn = jax.random.normal(rng, dims, jnp.float32) * deviation * level
    return jnp.minimum(jnp.maximum(drawn, -bound), bound).astype(kind)


def setup_inputs(seed: int = 0) -> dict:
    key_list = jax.random.split(jax.random.key(seed), 14)
    return {
        "template_pair": bell_draw(key_list[0], (TPL, C, N, N), 1.0, 6.0, ((2, 16), (3, 8))),
        "template_feat": bell_draw(key_list[1], (TB_ALL, F, BLK), 1.0, 6.0, ((0, 128),)),
        "block_map": plant(jax.random.randint(key_list[2], (TPL, QB), 0, TB_ALL), jax.random.fold_in(key_list[2], 1), 0, TB_ALL - 1).astype(jnp.int32),
        "block_count": plant(jax.random.randint(key_list[3], (TPL, QB), 1, BLK + 1), jax.random.fold_in(key_list[3], 1), 1, BLK).astype(jnp.int32),
        "residue_mask": plant((jax.random.randint(key_list[4], (TPL, N), 0, 8) < 7).astype(jnp.int32), jax.random.fold_in(key_list[4], 1), 0, 1),
        "row_embed": bell_draw(key_list[5], (F, C), F ** -0.5, 0.75),
        "col_embed": bell_draw(key_list[6], (F, C), F ** -0.5, 0.75),
        "norm_gain": jnp.clip(1.0 + 0.15 * jax.random.normal(key_list[7], (C,), jnp.float32), 0.25, 1.75).astype(jnp.bfloat16),
        "left_proj": bell_draw(key_list[8], (C, C), C ** -0.5, 0.75),
        "right_proj": bell_draw(key_list[9], (C, C), C ** -0.5, 0.75),
        "gate_proj": bell_draw(key_list[10], (C, C), C ** -0.5, 0.75),
        "out_proj": bell_draw(key_list[11], (C, C), C ** -0.5, 0.75),
        "embed_grad": bell_draw(key_list[12], (C, N, N), 0.05, 0.29882812, ((1, 16), (2, 8))),
    }


EPS = 1e-05

def normalize(values, axis):
    center = lax.optimization_barrier(jnp.mean(values, axis=axis, keepdims=True))
    shifted = values - center
    inverse = lax.rsqrt(lax.optimization_barrier(jnp.mean(shifted * shifted, axis=axis, keepdims=True)) + EPS)
    return (shifted * inverse, inverse)

def normalize_back(grad_hat, normed, inverse, axis):
    first_mean = lax.optimization_barrier(jnp.mean(grad_hat, axis=axis, keepdims=True))
    second_mean = lax.optimization_barrier(jnp.mean(grad_hat * normed, axis=axis, keepdims=True))
    return (grad_hat - first_mean - normed * second_mean) * inverse

def project(weight, values):
    return jnp.einsum('dc,dij->cij', weight.astype(jnp.float32), values.astype(jnp.float32))

def project_back(weight, values):
    return jnp.einsum('dc,cij->dij', weight.astype(jnp.float32), values.astype(jnp.float32))

def reference(template_pair, template_feat, block_map, block_count, residue_mask, row_embed, col_embed, norm_gain, left_proj, right_proj, gate_proj, out_proj, embed_grad):
    positions = jnp.arange(N, dtype=jnp.int32)
    block_of = (positions // BLK).astype(jnp.int32)
    offsets = (positions % BLK).astype(jnp.int32)
    gain = norm_gain.astype(jnp.float32)[:, None, None]
    grad_out = embed_grad.astype(jnp.float32) / TPL

    def one_template(carry, inputs):
        emb_sum, grad_sum = carry
        pair_slice, map_row, count_row, mask_row = inputs
        blocks = map_row[block_of]
        valid = ((offsets < count_row[block_of]) & (mask_row == 1)).astype(jnp.float32)
        fetched = template_feat[blocks, :, offsets]
        feat = (fetched.T.astype(jnp.float32) * valid[None, :]).astype(jnp.bfloat16)
        left_terms = jnp.dot(row_embed.T, feat, preferred_element_type=jnp.float32)
        right_terms = jnp.dot(col_embed.T, feat, preferred_element_type=jnp.float32)
        pair = pair_slice.astype(jnp.float32) + left_terms[:, :, None] + right_terms[:, None, :]
        normed, inverse = normalize(pair, 0)
        scaled = (normed * gain).astype(jnp.bfloat16)
        left_pair = project(left_proj, scaled).astype(jnp.bfloat16)
        right_pair = project(right_proj, scaled).astype(jnp.bfloat16)
        gate = jax.nn.sigmoid(project(gate_proj, scaled))
        product = jnp.einsum('cik,cjk->cij', left_pair.astype(jnp.float32), right_pair.astype(jnp.float32)).astype(jnp.bfloat16)
        prod_norm, prod_inv = normalize(product.astype(jnp.float32), 0)
        projected = project(out_proj, prod_norm.astype(jnp.bfloat16))
        emb_sum = emb_sum + (pair + gate * projected)
        grad_proj = (grad_out * gate).astype(jnp.bfloat16)
        grad_gate = (grad_out * projected * gate * (1.0 - gate)).astype(jnp.bfloat16)
        grad_norm = project_back(out_proj, grad_proj)
        grad_prod = normalize_back(grad_norm, prod_norm, prod_inv, 0).astype(jnp.bfloat16)
        grad_left = jnp.einsum('cij,cjk->cik', grad_prod.astype(jnp.float32), right_pair.astype(jnp.float32)).astype(jnp.bfloat16)
        grad_right = jnp.einsum('cij,cik->cjk', grad_prod.astype(jnp.float32), left_pair.astype(jnp.float32)).astype(jnp.bfloat16)
        grad_scaled = project_back(left_proj, grad_left) + project_back(right_proj, grad_right) + project_back(gate_proj, grad_gate)
        grad_pair = grad_out + normalize_back(grad_scaled * gain, normed, inverse, 0)
        row_sums = lax.optimization_barrier(jnp.sum(grad_pair, axis=2))
        col_sums = lax.optimization_barrier(jnp.sum(grad_pair, axis=1))
        grad_query = jnp.dot(row_embed.astype(jnp.float32), row_sums, precision=lax.Precision.HIGHEST)
        grad_query = grad_query + jnp.dot(col_embed.astype(jnp.float32), col_sums, precision=lax.Precision.HIGHEST)
        grad_query = grad_query * valid[None, :]
        grad_sum = grad_sum.at[blocks, :, offsets].add(grad_query.T)
        return ((emb_sum, grad_sum), None)
    start = (jnp.zeros((C, N, N), jnp.float32), jnp.zeros((TB_ALL, F, BLK), jnp.float32))
    (emb_sum, grad_sum), _ = lax.scan(one_template, start, (template_pair, block_map, block_count, residue_mask))
    return ((emb_sum / TPL).astype(jnp.bfloat16), grad_sum)
```

```python
import jax
import jax.numpy as jnp
import numpy as np
from jax import lax
from jax.experimental import pallas as pl
from jax.experimental.pallas import tpu as pltpu
from jax.sharding import PartitionSpec as P

EPS = 1e-05
HIGHEST = lax.Precision.HIGHEST
F32 = jnp.float32
BF = jnp.bfloat16
AXES = ("row", "col")
VMEM = 60 * 2**20

C = 64
T = 4
H = 64
W = 128
N = 1024
K8 = C * 8
ROWS = 288


def params():
    return pltpu.CompilerParams(vmem_limit_bytes=VMEM)


def stack_rows(top, bottom):
    return jnp.concatenate([top.reshape(K8, W), bottom.reshape(K8, W)], axis=1)


def unstack_rows(wide):
    return wide[:, :W].reshape(C, 8, W), wide[:, W:].reshape(C, 8, W)


def join_rows(top, bottom):
    return jnp.concatenate([top, bottom], axis=1)


def norm_kernel(
    pair_ref, left_ref, right_ref, gain_ref, kl_ref, kr_ref, pay_ref, scaled_ref, inv_ref, sum_ref
):
    step = pl.program_id(0)
    right = right_ref[0]
    for g in range(4):
        rows = slice(g * 16, g * 16 + 16)
        pairs, scaleds, invs = [], [], []
        for part in range(2):
            first = g * 16 + part * 8
            raw = pair_ref[0, :, rows, :].astype(F32)[:, part * 8 : part * 8 + 8, :]
            lane = 2 * g + part
            left = jnp.broadcast_to(left_ref[0, :, lane : lane + 1], (K8, W)).reshape(C, 8, W)
            pair = raw + left + right
            center = jnp.sum(pair, axis=0, keepdims=True) * (1.0 / C)
            shifted = pair - center
            inverse = lax.rsqrt(
                jnp.sum(shifted * shifted, axis=0, keepdims=True) * (1.0 / C) + EPS
            )
            inv_ref[0, first : first + 8, :] = inverse[0]
            scaleds.append(shifted * inverse * gain_ref[...])
            invs.append(inverse[0])
            where = (slice(None), slice(first, first + 8), slice(None))

            @pl.when(step == 0)
            def _():
                sum_ref[where] = pair

            @pl.when(step > 0)
            def _():
                sum_ref[where] += pair

        scaled_ref[0, :, rows, :] = join_rows(*scaleds).astype(BF)
        wide = stack_rows(*scaleds).astype(BF)
        for k, weight in enumerate((kl_ref, kr_ref)):
            out = jnp.dot(weight[...], wide, preferred_element_type=F32)
            out = join_rows(*unstack_rows(out)).astype(BF).reshape(C // 2, 2, 16, W)
            for s in range(2):
                first = k * 128 + s * 64 + g * 16
                pay_ref[0, :, first : first + 16, :] = out[:, s]
        both = jnp.concatenate(invs, axis=0).astype(BF)
        first = 256 + (g % 2) * 16
        for q in range(g // 2, C // 2, 2):
            pay_ref[0, q, first : first + 16, :] = both


def run_norm(pair, left, right, gain, kl, kr):
    whole = lambda *shape: pl.BlockSpec(shape, lambda t: (0,) * len(shape))
    return pl.pallas_call(
        norm_kernel,
        grid=(T,),
        in_specs=[
            pl.BlockSpec((1, C, H, W), lambda t: (t, 0, 0, 0)),
            pl.BlockSpec((1, K8, 8), lambda t: (t, 0, 0)),
            pl.BlockSpec((1, C, 8, W), lambda t: (t, 0, 0, 0)),
            whole(C, 8, W),
            whole(K8, K8),
            whole(K8, K8),
        ],
        out_specs=[
            pl.BlockSpec((1, C // 2, ROWS, W), lambda t: (t, 0, 0, 0)),
            pl.BlockSpec((1, C, H, W), lambda t: (t, 0, 0, 0)),
            pl.BlockSpec((1, H, W), lambda t: (t, 0, 0)),
            whole(C, H, W),
        ],
        out_shape=[
            jax.ShapeDtypeStruct((T, C // 2, ROWS, W), BF),
            jax.ShapeDtypeStruct((T, C, H, W), BF),
            jax.ShapeDtypeStruct((T, H, W), F32),
            jax.ShapeDtypeStruct((C, H, W), F32),
        ],
        compiler_params=params(),
        name="pair_norm",
    )(pair, left, right, gain, kl, kr)


def spread(blocks_ref, full_ref):
    @pl.loop(0, 16)
    def _(r):
        for c in range(8):
            full_ref[pl.ds(r * H, H), c * W : (c + 1) * W] = blocks_ref[r * 8 + c]


def product_kernel(left_ref, right_ref, out_ref, left, right):
    spread(left_ref, left)
    spread(right_ref, right)

    @pl.loop(0, 4)
    def _(b):
        out = lax.dot_general(
            left[pl.ds(b * 256, 256), :],
            right[...],
            (((1,), (1,)), ((), ())),
            preferred_element_type=F32,
        ).astype(BF)
        for r in range(4):
            for c in range(8):
                out_ref[(b * 4 + r) * 8 + c] = out[r * H : (r + 1) * H, c * W : (c + 1) * W]


def run_product(factors):
    spec = lambda first: pl.BlockSpec((128, H, W), lambda s: (0, first + s, 0))
    return pl.pallas_call(
        product_kernel,
        grid=(2,),
        in_specs=[spec(0), spec(2)],
        out_specs=pl.BlockSpec((128, H, W), lambda s: (0, s, 0)),
        out_shape=jax.ShapeDtypeStruct((128, 2 * H, W), BF),
        scratch_shapes=[pltpu.VMEM((N, N), BF), pltpu.VMEM((N, N), BF)],
        compiler_params=params(),
        name="triangle_product",
    )(factors, factors)


def gate_kernel(
    prod_ref, scaled_ref, grad_ref, sum_ref, inv_ref, kg_ref, ko_ref, kb_ref, pick_ref,
    emb_ref, out_ref, mean_ref, rows_ref, cols_ref, grows_ref, gcols_ref, total,
):
    step = pl.program_id(0)
    halves = lambda v: (v[:, :8, :], v[:, 8:, :])
    row_sums = jnp.zeros((K8, W), F32)
    col_sums = jnp.zeros((C, 8, W), F32)
    for g in range(4):
        rows = slice(g * 16, g * 16 + 16)
        scaled = stack_rows(*halves(scaled_ref[0, :, rows, :].astype(F32))).astype(BF)
        opened = unstack_rows(jnp.dot(kg_ref[...], scaled, preferred_element_type=F32))
        normed, prod_invs = [], []
        for product in halves(prod_ref[0, :, rows, :].astype(F32)):
            center = jnp.sum(product, axis=0, keepdims=True) * (1.0 / C)
            shifted = product - center
            inverse = lax.rsqrt(
                jnp.sum(shifted * shifted, axis=0, keepdims=True) * (1.0 / C) + EPS
            )
            normed.append(shifted * inverse)
            prod_invs.append(inverse)
        projected = unstack_rows(
            jnp.dot(ko_ref[...], stack_rows(*normed).astype(BF), preferred_element_type=F32)
        )
        grads = halves(grad_ref[:, rows, :].astype(F32))
        grad_projs, weighted = [], []
        for part in range(2):
            first = g * 16 + part * 8
            where = (slice(None), slice(first, first + 8), slice(None))
            gate = jax.nn.sigmoid(opened[part])
            gated = gate * projected[part]

            @pl.when(step == 0)
            def _():
                total[where] = sum_ref[where] + gated

            @pl.when(step > 0)
            def _():
                total[where] += gated

            grad_out = grads[part] * (1.0 / T)
            grad_projs.append(grad_out * gate)
            grad_gate = grad_out * gated * (1.0 - gate)
            mean_ref[0, first : first + 8, :] = jnp.sum(grad_gate * opened[part], axis=0)
            term = grad_gate * inv_ref[0, first : first + 8, :][None]
            col_sums = col_sums + term
            weighted.append(term)
        row_sums = row_sums + jnp.dot(
            stack_rows(*weighted).astype(BF), pick_ref[g], preferred_element_type=F32
        )
        grad_norms = unstack_rows(
            jnp.dot(kb_ref[...], stack_rows(*grad_projs).astype(BF), preferred_element_type=F32)
        )
        outs = []
        for part in range(2):
            grad_norm = grad_norms[part]
            first_mean = jnp.sum(grad_norm, axis=0, keepdims=True) * (1.0 / C)
            second_mean = jnp.sum(grad_norm * normed[part], axis=0, keepdims=True) * (1.0 / C)
            outs.append((grad_norm - first_mean - normed[part] * second_mean) * prod_invs[part])
        out_ref[0, :, rows, :] = join_rows(*outs).astype(BF)
    rows_ref[0] = row_sums
    cols_ref[0] = col_sums.reshape(K8, W)

    @pl.when(step == 0)
    def _():
        grad_rows = jnp.zeros((K8, W), F32)
        grad_cols = jnp.zeros((C, 8, W), F32)
        for g in range(4):
            top, bottom = halves(grad_ref[:, g * 16 : g * 16 + 16, :].astype(F32))
            grad_cols = grad_cols + top + bottom
            grad_rows = grad_rows + jnp.dot(
                stack_rows(top, bottom).astype(BF), pick_ref[g], preferred_element_type=F32
            )
        grows_ref[...] = grad_rows
        gcols_ref[...] = grad_cols.reshape(K8, W)

    @pl.when(step == T - 1)
    def _():
        emb_ref[...] = (total[...] * (1.0 / T)).astype(BF)


def run_gate(prod, scaled, grad, pair_sum, inv, kg, ko, kb, pick):
    whole = lambda *shape: pl.BlockSpec(shape, lambda t: (0,) * len(shape))
    each = lambda *shape: pl.BlockSpec((1, *shape), lambda t: (t,) + (0,) * len(shape))
    return pl.pallas_call(
        gate_kernel,
        grid=(T,),
        in_specs=[
            each(C, H, W), each(C, H, W), whole(C, H, W), whole(C, H, W), each(H, W),
            whole(K8, K8), whole(K8, K8), whole(K8, K8), whole(4, 2 * W, W),
        ],
        out_specs=[
            whole(C, H, W), each(C, H, W), each(H, W), each(K8, W), each(K8, W),
            whole(K8, W), whole(K8, W),
        ],
        out_shape=[
            jax.ShapeDtypeStruct((C, H, W), BF),
            jax.ShapeDtypeStruct((T, C, H, W), BF),
            jax.ShapeDtypeStruct((T, H, W), F32),
            jax.ShapeDtypeStruct((T, K8, W), F32),
            jax.ShapeDtypeStruct((T, K8, W), F32),
            jax.ShapeDtypeStruct((K8, W), F32),
            jax.ShapeDtypeStruct((K8, W), F32),
        ],
        scratch_shapes=[pltpu.VMEM((C, H, W), F32)],
        compiler_params=params(),
        name="gate_and_grad",
    )(prod, scaled, grad, pair_sum, inv, kg, ko, kb, pick)


def factor_kernel(
    left_ref, right_ref, grad_ref, inv_ref, out_ref, sums_ref, left, right, grad, inv, mean
):
    step = pl.program_id(0)
    spread(left_ref, left)
    spread(right_ref, right)
    spread(grad_ref, grad)

    @pl.when(step == 0)
    def _():
        spread(inv_ref, inv)
        mean[...] = jnp.zeros_like(mean)

    sums_ref[...] = jnp.zeros_like(sums_ref)
    ones = jnp.full((8, W), 0.125, F32)

    def finish(value, rows, factor, kind):
        mean[rows, :] += value * factor[rows, :].astype(F32)
        term = value * inv[rows, :].astype(F32)
        sums_ref[0, 2 * kind + 1] += jnp.sum(term.reshape(32, 8, N), axis=0)
        lanes = term[:, :W]
        for c in range(1, 8):
            lanes = lanes + term[:, c * W : (c + 1) * W]
        sums_ref[0, 2 * kind, :, rows] = lax.dot_general(
            ones, lanes, (((1,), (1,)), ((), ())), precision=HIGHEST, preferred_element_type=F32
        )

    for b in range(4):
        rows = slice(b * 256, b * 256 + 256)
        value = jnp.dot(grad[rows, :], right[...], preferred_element_type=F32)
        finish(value, rows, left, 0)
    for b in range(4):
        rows = slice(b * 256, b * 256 + 256)
        value = lax.dot_general(
            grad[:, rows], left[...], (((0,), (0,)), ((), ())), preferred_element_type=F32
        )
        finish(value, rows, right, 1)

    @pl.when(step == 1)
    def _():
        @pl.loop(0, 16)
        def _(r):
            for c in range(8):
                out_ref[r * 8 + c] = mean[pl.ds(r * H, H), c * W : (c + 1) * W].astype(BF)


def run_factor(factors, grad, inv):
    spec = lambda first: pl.BlockSpec((128, H, W), lambda s: (0, first + s, 0))
    return pl.pallas_call(
        factor_kernel,
        grid=(2,),
        in_specs=[spec(0), spec(2), spec(0), pl.BlockSpec((128, H, W), lambda s: (0, 0, 0))],
        out_specs=[
            pl.BlockSpec((128, H, W), lambda s: (0, 0, 0)),
            pl.BlockSpec((1, 4, 8, N), lambda s: (s, 0, 0, 0)),
        ],
        out_shape=[
            jax.ShapeDtypeStruct((128, H, W), BF),
            jax.ShapeDtypeStruct((2, 4, 8, N), F32),
        ],
        scratch_shapes=[
            pltpu.VMEM((N, N), BF),
            pltpu.VMEM((N, N), BF),
            pltpu.VMEM((N, N), BF),
            pltpu.VMEM((N, N), BF),
            pltpu.VMEM((N, N), F32),
        ],
        compiler_params=params(),
        name="factor_grads",
    )(factors, factors, grad, inv)


def close_kernel(recv_ref, mean_ref, inv_ref, scaled_ref, pick_ref, rows_ref, cols_ref):
    got = recv_ref[0].astype(F32)
    total = got[0]
    for k in range(1, 16):
        total = total + got[k]
    weight = (total.reshape(H, W) + mean_ref[0]) * inv_ref[0] * (1.0 / C)
    row_sums = jnp.zeros((K8, W), F32)
    col_sums = jnp.zeros((C, 8, W), F32)
    for g in range(4):
        scaled = scaled_ref[0, :, g * 16 : g * 16 + 16, :].astype(F32)
        terms = []
        for part in range(2):
            first = g * 16 + part * 8
            term = scaled[:, part * 8 : part * 8 + 8, :] * weight[first : first + 8, :][None]
            col_sums = col_sums + term
            terms.append(term)
        row_sums = row_sums + jnp.dot(
            stack_rows(*terms).astype(BF), pick_ref[g], preferred_element_type=F32
        )
    rows_ref[0] = row_sums
    cols_ref[0] = col_sums.reshape(K8, W)


def run_close(recv, mean, inv, scaled, pick):
    each = lambda *shape: pl.BlockSpec((1, *shape), lambda t: (t,) + (0,) * len(shape))
    return pl.pallas_call(
        close_kernel,
        grid=(T,),
        in_specs=[
            each(16, 2, H // 2, W), each(H, W), each(H, W), each(C, H, W),
            pl.BlockSpec((4, 2 * W, W), lambda t: (0, 0, 0)),
        ],
        out_specs=[each(K8, W), each(K8, W)],
        out_shape=[jax.ShapeDtypeStruct((T, K8, W), F32)] * 2,
        compiler_params=params(),
        name="close_sums",
    )(recv, mean, inv, scaled, pick)


def swap_cores(value):
    return lax.ppermute(value, "col", [(i, i ^ 1) for i in range(8)])


def exchange(value):
    return lax.all_to_all(value, AXES, split_axis=0, concat_axis=0, tiled=True)


def in_order(core, mine, other, axis):
    first = jnp.where(core == 0, mine, other)
    second = jnp.where(core == 0, other, mine)
    return jnp.concatenate([first, second], axis=axis)


def lane_rows(sums):
    lead = sums.shape[:-2]
    cut = sums[..., :8].reshape(*lead, C, 8, 8)
    return jnp.swapaxes(cut, -1, -2).reshape(*lead, C, H)


def lane_cols(sums):
    lead = sums.shape[:-2]
    return jnp.sum(sums.reshape(*lead, C, 8, W), axis=-2)


def expand(weights):
    to = jnp.asarray(np.kron(np.eye(C), np.ones((8, 1))), BF)
    tall = jnp.einsum("ac,ncd->nad", to, weights, preferred_element_type=F32).astype(BF)
    wide = jnp.einsum("nad,bd->nab", tall, to, preferred_element_type=F32)
    index = jnp.arange(K8, dtype=jnp.int32) % 8
    return jnp.where(index[:, None] == index[None, :], wide, 0.0).astype(BF)


def per_device(
    template_pair,
    template_feat,
    block_map,
    block_count,
    residue_mask,
    row_embed,
    col_embed,
    norm_gain,
    left_proj,
    right_proj,
    gate_proj,
    out_proj,
    embed_grad,
):
    row = lax.axis_index("row")
    col = lax.axis_index("col")
    core = col % 2
    me = row * 8 + col
    own = me // 32
    pair_at = me % 32
    blocks = jnp.arange(128, dtype=jnp.int32)
    half = row % 2
    row_block = row // 2

    feat_halves = jnp.stack([template_feat[0, :32], template_feat[0, 32:]])
    sent_feat = jnp.broadcast_to(feat_halves[None], (64, 2, 32, W)).reshape(128, 32, W)
    pool = exchange(sent_feat)
    column_ids = lambda m, at: lax.dynamic_index_in_dim(m, at, axis=1, keepdims=False)
    row_ids = column_ids(block_map, row_block)
    col_ids = column_ids(block_map, col)
    other_ids = column_ids(block_map, col ^ 1)
    wanted = jnp.concatenate([col_ids, row_ids, other_ids, row_ids])
    choose = (wanted[:, None] == blocks[None, :]).astype(BF)
    picked = jnp.einsum(
        "eb,bx->ex", choose, pool.reshape(128, 32 * W), preferred_element_type=F32
    ).astype(BF)
    picked = picked.reshape(16, 32, W)
    arrived = swap_cores(picked[8:])
    feats = in_order(core, picked[:8], arrived, 1).astype(F32)

    offsets = jnp.arange(W, dtype=jnp.int32)
    col_marks = lax.dynamic_slice_in_dim(residue_mask, col * W, W, axis=1)
    col_valid = (
        (offsets[None, :] < column_ids(block_count, col)[:, None]) & (col_marks == 1)
    ).astype(F32)
    row_offsets = half * H + jnp.arange(H, dtype=jnp.int32)
    row_marks = lax.dynamic_slice_in_dim(residue_mask, row * H, H, axis=1)
    row_valid = (
        (row_offsets[None, :] < column_ids(block_count, row_block)[:, None]) & (row_marks == 1)
    ).astype(F32)
    feat_cols = (feats[:4] * col_valid[:, None, :]).astype(BF)
    feat_rows = jnp.where(half == 0, feats[4:, :, :H], feats[4:, :, H:])
    feat_rows = (feat_rows * row_valid[:, None, :]).astype(BF)
    left_terms = jnp.einsum("fc,tfi->tci", row_embed, feat_rows, preferred_element_type=F32)
    right_terms = jnp.einsum("fc,tfj->tcj", col_embed, feat_cols, preferred_element_type=F32)
    left_cut = left_terms.reshape(T, C, 8, 8).transpose(0, 1, 3, 2).reshape(T, K8, 8)
    right_wide = jnp.broadcast_to(right_terms[:, :, None, :], (T, C, 8, W))
    gain = norm_gain.astype(F32)
    gain_wide = jnp.broadcast_to(gain[:, None, None], (C, 8, W))
    kl, kr, kg, ko, kb = expand(
        jnp.stack([left_proj.T, right_proj.T, gate_proj.T, out_proj.T, out_proj])
    )
    pick = jnp.asarray(
        np.arange(W)[None, None, :]
        == 2 * np.arange(4)[:, None, None] + (np.arange(2 * W) // W)[None, :, None],
        BF,
    )

    sent, scaled, inv, pair_sum = run_norm(template_pair, left_cut, right_wide, gain_wide, kl, kr)
    factors = exchange(sent.reshape(128, ROWS, W))
    my_inv = factors[:, 256:]
    inv_all = in_order(core, my_inv, swap_cores(my_inv), 1)
    prod = exchange(run_product(factors)).reshape(T, C, H, W)
    embedding, grad_prod, gate_mean, gate_rows, gate_cols, out_rows, out_cols = run_gate(
        prod, scaled, embed_grad, pair_sum, inv, kg, ko, kb, pick
    )
    grads = exchange(grad_prod.reshape(128, 2 * H, W))
    part_mean, sums = run_factor(factors, grads, inv_all)
    kept = jnp.where(core == 0, part_mean[:, :32], part_mean[:, 32:])
    given = jnp.where(core == 0, part_mean[:, 32:], part_mean[:, :32])
    mean_half = (kept.astype(F32) + swap_cores(given).astype(F32)).astype(BF)
    recv = exchange(mean_half).reshape(T, 16, 2, H // 2, W)
    close_rows, close_cols = run_close(recv, gate_mean, inv, scaled, pick)

    def center(weights):
        scaled_weights = gain[:, None] * weights.astype(F32)
        return scaled_weights - jnp.mean(scaled_weights, axis=0, keepdims=True)

    embeds = jnp.stack([row_embed, col_embed]).astype(F32)
    mixed = jnp.einsum(
        "efd,kdc->kefc",
        embeds,
        jnp.stack([center(left_proj), center(right_proj), center(gate_proj)]),
        precision=HIGHEST,
    )
    closing = -embeds / gain[None, None, :]
    opening = embeds * (1.0 / T)

    def finish(side, gated, closed, out, valid):
        total = jnp.einsum("fc,tci->tfi", mixed[2, side], gated, precision=HIGHEST)
        total = total + jnp.einsum("fc,tci->tfi", closing[side], closed, precision=HIGHEST)
        total = total + jnp.einsum("fc,ci->fi", opening[side], out, precision=HIGHEST)[None]
        return total * valid[:, None, :]

    grad_rows = finish(
        0, lane_rows(gate_rows), lane_rows(close_rows), lane_rows(out_rows), row_valid
    )
    grad_cols = finish(
        1, lane_cols(gate_cols), lane_cols(close_cols), lane_cols(out_cols), col_valid
    )
    owned = jnp.sum(sums, axis=2).reshape(2, 2, 2, N)
    weights = lax.dynamic_slice_in_dim(mixed[:2], 2 * pair_at, 2, axis=3)
    grad_own = jnp.einsum("kefs,sken->fn", weights, owned, precision=HIGHEST)
    all_offsets = jnp.arange(N, dtype=jnp.int32)
    own_map = lax.dynamic_index_in_dim(block_map, own, axis=0, keepdims=False)
    own_count = lax.dynamic_index_in_dim(block_count, own, axis=0, keepdims=False)
    own_marks = lax.dynamic_index_in_dim(residue_mask, own, axis=0, keepdims=False)
    own_valid = (
        (all_offsets % W).reshape(8, W) < own_count[:, None]
    ) & (own_marks.reshape(8, W) == 1)
    grad_own = grad_own.reshape(C, 8, W).transpose(1, 0, 2) * own_valid.astype(F32)[:, None, :]
    blank = jnp.zeros_like(grad_rows)
    grad_rows = jnp.concatenate(
        [jnp.where(half == 0, grad_rows, blank), jnp.where(half == 0, blank, grad_rows)], axis=2
    )
    entries = jnp.concatenate([grad_own, grad_rows, grad_cols], axis=0).astype(BF)
    kept = jnp.where(core == 0, entries[:, :32], entries[:, 32:])
    given = jnp.where(core == 0, entries[:, 32:], entries[:, :32])
    entries = jnp.concatenate([kept, swap_cores(given)], axis=0)
    targets = jnp.concatenate([own_map, row_ids, col_ids, own_map, row_ids, other_ids])
    place = (targets[None, :] == blocks[:, None]).astype(BF)
    placed = jnp.einsum(
        "be,ex->bx", place, entries.reshape(32, 32 * W), preferred_element_type=F32
    ).astype(BF)
    back = exchange(placed.reshape(128, 32, W)).reshape(64, 2 * 32, W)
    feat_grad = jnp.sum(back.astype(F32), axis=0)[None]
    return (embedding, feat_grad)


def solution(mesh):
    return jax.shard_map(
        per_device,
        mesh=mesh,
        in_specs=(
            P(None, None, "row", "col"),
            P(("row", "col"), None, None),
            P(),
            P(),
            P(),
            P(),
            P(),
            P(),
            P(),
            P(),
            P(),
            P(),
            P(None, "row", "col"),
        ),
        out_specs=(P(None, "row", "col"), P(("row", "col"), None, None)),
        check_vma=False,
    )
```

```python
import jax
import jax.numpy as jnp
import numpy as np
from jax import lax
from jax.experimental import pallas as pl
from jax.experimental.pallas import tpu as pltpu
from jax.sharding import PartitionSpec as P

EPS = 1e-05
HIGHEST = lax.Precision.HIGHEST
F32 = jnp.float32
BF = jnp.bfloat16
AXES = ("row", "col")
VMEM = 60 * 2**20

C = 64
T = 4
H = 64
W = 128
N = 1024
K8 = C * 8
ROWS = 288


def params():
    return pltpu.CompilerParams(vmem_limit_bytes=VMEM)


def stack_rows(top, bottom):
    return jnp.concatenate([top.reshape(K8, W), bottom.reshape(K8, W)], axis=1)


def unstack_rows(wide):
    return wide[:, :W].reshape(C, 8, W), wide[:, W:].reshape(C, 8, W)


def join_rows(top, bottom):
    return jnp.concatenate([top, bottom], axis=1)


def norm_kernel(
    pair_ref, left_ref, right_ref, gain_ref, kl_ref, kr_ref, pay_ref, scaled_ref, inv_ref, sum_ref
):
    step = pl.program_id(0)
    right = right_ref[0]
    for g in range(4):
        rows = slice(g * 16, g * 16 + 16)
        pairs, scaleds, invs = [], [], []
        for part in range(2):
            first = g * 16 + part * 8
            raw = pair_ref[0, :, rows, :].astype(F32)[:, part * 8 : part * 8 + 8, :]
            lane = 2 * g + part
            left = jnp.broadcast_to(left_ref[0, :, lane : lane + 1], (K8, W)).reshape(C, 8, W)
            pair = raw + left + right
            center = jnp.sum(pair, axis=0, keepdims=True) * (1.0 / C)
            shifted = pair - center
            inverse = lax.rsqrt(
                jnp.sum(shifted * shifted, axis=0, keepdims=True) * (1.0 / C) + EPS
            )
            inv_ref[0, first : first + 8, :] = inverse[0]
            scaleds.append(shifted * inverse * gain_ref[...])
            invs.append(inverse[0])
            where = (slice(None), slice(first, first + 8), slice(None))

            @pl.when(step == 0)
            def _():
                sum_ref[where] = pair

            @pl.when(step > 0)
            def _():
                sum_ref[where] += pair

        scaled_ref[0, :, rows, :] = join_rows(*scaleds).astype(BF)
        wide = stack_rows(*scaleds).astype(BF)
        for k, weight in enumerate((kl_ref, kr_ref)):
            out = jnp.dot(weight[...], wide, preferred_element_type=F32)
            out = join_rows(*unstack_rows(out)).astype(BF).reshape(C // 2, 2, 16, W)
            for s in range(2):
                first = k * 128 + s * 64 + g * 16
                pay_ref[0, :, first : first + 16, :] = out[:, s]
        both = jnp.concatenate(invs, axis=0).astype(BF)
        first = 256 + (g % 2) * 16
        for q in range(g // 2, C // 2, 2):
            pay_ref[0, q, first : first + 16, :] = both


def run_norm(pair, left, right, gain, kl, kr):
    whole = lambda *shape: pl.BlockSpec(shape, lambda t: (0,) * len(shape))
    return pl.pallas_call(
        norm_kernel,
        grid=(T,),
        in_specs=[
            pl.BlockSpec((1, C, H, W), lambda t: (t, 0, 0, 0)),
            pl.BlockSpec((1, K8, 8), lambda t: (t, 0, 0)),
            pl.BlockSpec((1, C, 8, W), lambda t: (t, 0, 0, 0)),
            whole(C, 8, W),
            whole(K8, K8),
            whole(K8, K8),
        ],
        out_specs=[
            pl.BlockSpec((1, C // 2, ROWS, W), lambda t: (t, 0, 0, 0)),
            pl.BlockSpec((1, C, H, W), lambda t: (t, 0, 0, 0)),
            pl.BlockSpec((1, H, W), lambda t: (t, 0, 0)),
            whole(C, H, W),
        ],
        out_shape=[
            jax.ShapeDtypeStruct((T, C // 2, ROWS, W), BF),
            jax.ShapeDtypeStruct((T, C, H, W), BF),
            jax.ShapeDtypeStruct((T, H, W), F32),
            jax.ShapeDtypeStruct((C, H, W), F32),
        ],
        compiler_params=params(),
        name="pair_norm",
    )(pair, left, right, gain, kl, kr)


def spread(blocks_ref, full_ref):
    @pl.loop(0, 16)
    def _(r):
        for c in range(8):
            full_ref[pl.ds(r * H, H), c * W : (c + 1) * W] = blocks_ref[r * 8 + c]


def product_kernel(left_ref, right_ref, out_ref, left, right):
    spread(left_ref, left)
    spread(right_ref, right)

    @pl.loop(0, 4)
    def _(b):
        out = lax.dot_general(
            left[pl.ds(b * 256, 256), :],
            right[...],
            (((1,), (1,)), ((), ())),
            preferred_element_type=F32,
        ).astype(BF)
        for r in range(4):
            for c in range(8):
                out_ref[(b * 4 + r) * 8 + c] = out[r * H : (r + 1) * H, c * W : (c + 1) * W]


def run_product(factors):
    spec = lambda first: pl.BlockSpec((128, H, W), lambda s: (0, first + s, 0))
    return pl.pallas_call(
        product_kernel,
        grid=(2,),
        in_specs=[spec(0), spec(2)],
        out_specs=pl.BlockSpec((128, H, W), lambda s: (0, s, 0)),
        out_shape=jax.ShapeDtypeStruct((128, 2 * H, W), BF),
        scratch_shapes=[pltpu.VMEM((N, N), BF), pltpu.VMEM((N, N), BF)],
        compiler_params=params(),
        name="triangle_product",
    )(factors, factors)


def halves(value):
    return value[:, :8, :], value[:, 8:, :]


def mean_channels(value):
    return jnp.sum(value, axis=0, keepdims=True) * (1.0 / C)


def back_kernel(scaled_ref, grad_ref, kg_ref, kb_ref, out_ref):
    for g in range(4):
        rows = slice(g * 16, g * 16 + 16)
        scaled = stack_rows(*halves(scaled_ref[0, :, rows, :].astype(F32))).astype(BF)
        opened = unstack_rows(jnp.dot(kg_ref[...], scaled, preferred_element_type=F32))
        grads = halves(grad_ref[:, rows, :].astype(F32))
        grad_projs = [
            grads[part] * (1.0 / T) * jax.nn.sigmoid(opened[part]) for part in range(2)
        ]
        grad_norms = unstack_rows(
            jnp.dot(kb_ref[...], stack_rows(*grad_projs).astype(BF), preferred_element_type=F32)
        )
        outs = [grad_norm - mean_channels(grad_norm) for grad_norm in grad_norms]
        out_ref[0, :, rows, :] = join_rows(*outs).astype(BF)


def whole_spec(*shape):
    return pl.BlockSpec(shape, lambda t: (0,) * len(shape))


def each_spec(*shape):
    return pl.BlockSpec((1, *shape), lambda t: (t,) + (0,) * len(shape))


def run_back(scaled, grad, kg, kb):
    return pl.pallas_call(
        back_kernel,
        grid=(T,),
        in_specs=[each_spec(C, H, W), whole_spec(C, H, W), whole_spec(K8, K8), whole_spec(K8, K8)],
        out_specs=each_spec(C, H, W),
        out_shape=jax.ShapeDtypeStruct((T, C, H, W), BF),
        compiler_params=params(),
        cost_estimate=pl.CostEstimate(flops=4 * 2**31, bytes_accessed=9 * 2**20, transcendentals=2**21),
        name="back_project",
    )(scaled, grad, kg, kb)


def product_norm(product):
    shifted = product - mean_channels(product)
    return shifted, lax.rsqrt(mean_channels(shifted * shifted) + EPS)


def grad_kernel(prod_ref, back_ref, out_ref):
    for g in range(8):
        rows = slice(g * 8, g * 8 + 8)
        shifted, inverse = product_norm(prod_ref[0, :, rows, :].astype(F32))
        back = back_ref[0, :, rows, :].astype(F32)
        slope = mean_channels(back * shifted) * inverse * inverse
        out_ref[0, :, rows, :] = ((back - shifted * slope) * inverse).astype(BF)


def run_grad(prod, back):
    return pl.pallas_call(
        grad_kernel,
        grid=(T,),
        in_specs=[each_spec(C, H, W), each_spec(C, H, W)],
        out_specs=each_spec(C, H, W),
        out_shape=jax.ShapeDtypeStruct((T, C, H, W), BF),
        compiler_params=params(),
        cost_estimate=pl.CostEstimate(flops=2**25, bytes_accessed=12 * 2**20, transcendentals=0),
        name="product_grad",
    )(prod, back)


def gate_kernel(
    prod_ref, scaled_ref, grad_ref, sum_ref, inv_ref, kg_ref, ko_ref, pick_ref,
    emb_ref, mean_ref, rows_ref, cols_ref, grows_ref, gcols_ref, total,
):
    step = pl.program_id(0)
    row_sums = jnp.zeros((K8, W), F32)
    col_sums = jnp.zeros((C, 8, W), F32)
    for g in range(4):
        rows = slice(g * 16, g * 16 + 16)
        scaled = stack_rows(*halves(scaled_ref[0, :, rows, :].astype(F32))).astype(BF)
        opened = unstack_rows(jnp.dot(kg_ref[...], scaled, preferred_element_type=F32))
        normed = []
        for product in halves(prod_ref[0, :, rows, :].astype(F32)):
            shifted, inverse = product_norm(product)
            normed.append(shifted * inverse)
        projected = unstack_rows(
            jnp.dot(ko_ref[...], stack_rows(*normed).astype(BF), preferred_element_type=F32)
        )
        grads = halves(grad_ref[:, rows, :].astype(F32))
        weighted = []
        for part in range(2):
            first = g * 16 + part * 8
            where = (slice(None), slice(first, first + 8), slice(None))
            gate = jax.nn.sigmoid(opened[part])
            gated = gate * projected[part]

            @pl.when(step == 0)
            def _():
                total[where] = sum_ref[where] + gated

            @pl.when(step > 0)
            def _():
                total[where] += gated

            grad_gate = grads[part] * (1.0 / T) * gated * (1.0 - gate)
            mean_ref[0, first : first + 8, :] = jnp.sum(grad_gate * opened[part], axis=0)
            term = grad_gate * inv_ref[0, first : first + 8, :][None]
            col_sums = col_sums + term
            weighted.append(term)
        row_sums = row_sums + jnp.dot(
            stack_rows(*weighted).astype(BF), pick_ref[g], preferred_element_type=F32
        )
    rows_ref[0] = row_sums
    cols_ref[0] = col_sums.reshape(K8, W)

    @pl.when(step == 0)
    def _():
        grad_rows = jnp.zeros((K8, W), F32)
        grad_cols = jnp.zeros((C, 8, W), F32)
        for g in range(4):
            top, bottom = halves(grad_ref[:, g * 16 : g * 16 + 16, :].astype(F32))
            grad_cols = grad_cols + top + bottom
            grad_rows = grad_rows + jnp.dot(
                stack_rows(top, bottom).astype(BF), pick_ref[g], preferred_element_type=F32
            )
        grows_ref[...] = grad_rows
        gcols_ref[...] = grad_cols.reshape(K8, W)

    @pl.when(step == T - 1)
    def _():
        emb_ref[...] = (total[...] * (1.0 / T)).astype(BF)


def run_gate(prod, scaled, grad, pair_sum, inv, kg, ko, pick):
    return pl.pallas_call(
        gate_kernel,
        grid=(T,),
        in_specs=[
            each_spec(C, H, W), each_spec(C, H, W), whole_spec(C, H, W), whole_spec(C, H, W),
            each_spec(H, W), whole_spec(K8, K8), whole_spec(K8, K8), whole_spec(4, 2 * W, W),
        ],
        out_specs=[
            whole_spec(C, H, W), each_spec(H, W), each_spec(K8, W), each_spec(K8, W),
            whole_spec(K8, W), whole_spec(K8, W),
        ],
        out_shape=[
            jax.ShapeDtypeStruct((C, H, W), BF),
            jax.ShapeDtypeStruct((T, H, W), F32),
            jax.ShapeDtypeStruct((T, K8, W), F32),
            jax.ShapeDtypeStruct((T, K8, W), F32),
            jax.ShapeDtypeStruct((K8, W), F32),
            jax.ShapeDtypeStruct((K8, W), F32),
        ],
        scratch_shapes=[pltpu.VMEM((C, H, W), F32)],
        compiler_params=params(),
        cost_estimate=pl.CostEstimate(flops=4 * 2**31, bytes_accessed=12 * 2**20, transcendentals=2**21),
        name="gate_and_embed",
    )(prod, scaled, grad, pair_sum, inv, kg, ko, pick)


def square_kernel(left_ref, right_ref, inv_ref, left, right, inv):
    step = pl.program_id(0)
    spread(left_ref, left.at[0])
    spread(right_ref, right.at[0])

    @pl.when(step == 0)
    def _():
        spread(inv_ref, inv)


def run_square(factors, inv):
    spec = lambda first: pl.BlockSpec((128, H, W), lambda s: (0, first + s, 0))
    out = pl.BlockSpec((1, N, N), lambda s: (s, 0, 0))
    return pl.pallas_call(
        square_kernel,
        grid=(2,),
        in_specs=[spec(0), spec(2), pl.BlockSpec((128, H, W), lambda s: (0, 0, 0))],
        out_specs=[out, out, pl.BlockSpec((N, N), lambda s: (0, 0))],
        out_shape=[jax.ShapeDtypeStruct((2, N, N), BF)] * 2 + [jax.ShapeDtypeStruct((N, N), BF)],
        compiler_params=params(),
        cost_estimate=pl.CostEstimate(flops=2**20, bytes_accessed=20 * 2**20, transcendentals=0),
        name="to_matrices",
    )(factors, factors, inv)


def factor_kernel(
    core_ref, left_ref, right_ref, grad_ref, inv_ref, kept_ref, given_ref, sums_ref, grad, mean
):
    step = pl.program_id(0)
    core = core_ref[0]
    left, right = left_ref.at[0], right_ref.at[0]
    spread(grad_ref, grad)

    @pl.when(step == 0)
    def _():
        mean[...] = jnp.zeros_like(mean)

    sums_ref[...] = jnp.zeros_like(sums_ref)
    ones = jnp.full((8, W), 0.125, F32)

    def finish(value, rows, factor, kind):
        mean[rows, :] += value * factor[rows, :].astype(F32)
        term = value * inv_ref[rows, :].astype(F32)
        sums_ref[0, 2 * kind + 1] += jnp.sum(term.reshape(32, 8, N), axis=0)
        lanes = term[:, :W]
        for c in range(1, 8):
            lanes = lanes + term[:, c * W : (c + 1) * W]
        sums_ref[0, 2 * kind, :, rows] = lax.dot_general(
            ones, lanes, (((1,), (1,)), ((), ())), precision=HIGHEST, preferred_element_type=F32
        )

    for b in range(4):
        rows = slice(b * 256, b * 256 + 256)
        value = jnp.dot(grad[rows, :], right[...], preferred_element_type=F32)
        finish(value, rows, left, 0)
    for b in range(4):
        rows = slice(b * 256, b * 256 + 256)
        value = lax.dot_general(
            grad[:, rows], left[...], (((0,), (0,)), ((), ())), preferred_element_type=F32
        )
        finish(value, rows, right, 1)

    @pl.when(step == 1)
    def _():
        @pl.loop(0, 16)
        def _(r):
            mine = pl.ds(pl.multiple_of(r * H + core * 32, 32), 32)
            other = pl.ds(pl.multiple_of(r * H + (1 - core) * 32, 32), 32)
            for c in range(8):
                kept_ref[r * 8 + c] = mean[mine, c * W : (c + 1) * W].astype(BF)
                given_ref[r * 8 + c] = mean[other, c * W : (c + 1) * W].astype(BF)


def run_factor(core, left, right, grad, inv):
    matrix = pl.BlockSpec((1, N, N), lambda s: (s, 0, 0))
    return pl.pallas_call(
        factor_kernel,
        grid=(2,),
        in_specs=[
            pl.BlockSpec(memory_space=pltpu.SMEM),
            matrix,
            matrix,
            pl.BlockSpec((128, H, W), lambda s: (0, s, 0)),
            pl.BlockSpec((N, N), lambda s: (0, 0)),
        ],
        out_specs=[
            pl.BlockSpec((128, H // 2, W), lambda s: (0, 0, 0)),
            pl.BlockSpec((128, H // 2, W), lambda s: (0, 0, 0)),
            pl.BlockSpec((1, 4, 8, N), lambda s: (s, 0, 0, 0)),
        ],
        out_shape=[
            jax.ShapeDtypeStruct((128, H // 2, W), BF),
            jax.ShapeDtypeStruct((128, H // 2, W), BF),
            jax.ShapeDtypeStruct((2, 4, 8, N), F32),
        ],
        scratch_shapes=[pltpu.VMEM((N, N), BF), pltpu.VMEM((N, N), F32)],
        compiler_params=params(),
        name="factor_grads",
    )(core.reshape(1), left, right, grad, inv)


def close_kernel(recv_ref, mean_ref, inv_ref, scaled_ref, pick_ref, rows_ref, cols_ref):
    got = recv_ref[0].astype(F32)
    total = got[0]
    for k in range(1, 16):
        total = total + got[k]
    weight = (total.reshape(H, W) + mean_ref[0]) * inv_ref[0] * (1.0 / C)
    row_sums = jnp.zeros((K8, W), F32)
    col_sums = jnp.zeros((C, 8, W), F32)
    for g in range(4):
        scaled = scaled_ref[0, :, g * 16 : g * 16 + 16, :].astype(F32)
        terms = []
        for part in range(2):
            first = g * 16 + part * 8
            term = scaled[:, part * 8 : part * 8 + 8, :] * weight[first : first + 8, :][None]
            col_sums = col_sums + term
            terms.append(term)
        row_sums = row_sums + jnp.dot(
            stack_rows(*terms).astype(BF), pick_ref[g], preferred_element_type=F32
        )
    rows_ref[0] = row_sums
    cols_ref[0] = col_sums.reshape(K8, W)


def run_close(recv, mean, inv, scaled, pick):
    each = lambda *shape: pl.BlockSpec((1, *shape), lambda t: (t,) + (0,) * len(shape))
    return pl.pallas_call(
        close_kernel,
        grid=(T,),
        in_specs=[
            each(16, 2, H // 2, W), each(H, W), each(H, W), each(C, H, W),
            pl.BlockSpec((4, 2 * W, W), lambda t: (0, 0, 0)),
        ],
        out_specs=[each(K8, W), each(K8, W)],
        out_shape=[jax.ShapeDtypeStruct((T, K8, W), F32)] * 2,
        compiler_params=params(),
        name="close_sums",
    )(recv, mean, inv, scaled, pick)


def swap_cores(value):
    return lax.ppermute(value, "col", [(i, i ^ 1) for i in range(8)])


def exchange(value):
    return lax.all_to_all(value, AXES, split_axis=0, concat_axis=0, tiled=True)


def in_order(core, mine, other, axis):
    first = jnp.where(core == 0, mine, other)
    second = jnp.where(core == 0, other, mine)
    return jnp.concatenate([first, second], axis=axis)


def lane_rows(sums):
    lead = sums.shape[:-2]
    cut = sums[..., :8].reshape(*lead, C, 8, 8)
    return jnp.swapaxes(cut, -1, -2).reshape(*lead, C, H)


def lane_cols(sums):
    lead = sums.shape[:-2]
    return jnp.sum(sums.reshape(*lead, C, 8, W), axis=-2)


def expand(weights):
    to = jnp.asarray(np.kron(np.eye(C), np.ones((8, 1))), BF)
    tall = jnp.einsum("ac,ncd->nad", to, weights, preferred_element_type=F32).astype(BF)
    wide = jnp.einsum("nad,bd->nab", tall, to, preferred_element_type=F32)
    index = jnp.arange(K8, dtype=jnp.int32) % 8
    return jnp.where(index[:, None] == index[None, :], wide, 0.0).astype(BF)


def per_device(
    template_pair,
    template_feat,
    block_map,
    block_count,
    residue_mask,
    row_embed,
    col_embed,
    norm_gain,
    left_proj,
    right_proj,
    gate_proj,
    out_proj,
    embed_grad,
):
    row = lax.axis_index("row")
    col = lax.axis_index("col")
    core = col % 2
    me = row * 8 + col
    own = me // 32
    pair_at = me % 32
    blocks = jnp.arange(128, dtype=jnp.int32)
    half = row % 2
    row_block = row // 2

    feat_halves = jnp.stack([template_feat[0, :32], template_feat[0, 32:]])
    sent_feat = jnp.broadcast_to(feat_halves[None], (64, 2, 32, W)).reshape(128, 32, W)
    pool = exchange(sent_feat)
    column_ids = lambda m, at: lax.dynamic_index_in_dim(m, at, axis=1, keepdims=False)
    row_ids = column_ids(block_map, row_block)
    col_ids = column_ids(block_map, col)
    other_ids = column_ids(block_map, col ^ 1)
    wanted = jnp.concatenate([col_ids, row_ids, other_ids, row_ids])
    choose = (wanted[:, None] == blocks[None, :]).astype(BF)
    picked = jnp.einsum(
        "eb,bx->ex", choose, pool.reshape(128, 32 * W), preferred_element_type=F32
    ).astype(BF)
    picked = picked.reshape(16, 32, W)
    arrived = swap_cores(picked[8:])
    feats = in_order(core, picked[:8], arrived, 1).astype(F32)

    offsets = jnp.arange(W, dtype=jnp.int32)
    col_marks = lax.dynamic_slice_in_dim(residue_mask, col * W, W, axis=1)
    col_valid = (
        (offsets[None, :] < column_ids(block_count, col)[:, None]) & (col_marks == 1)
    ).astype(F32)
    row_offsets = half * H + jnp.arange(H, dtype=jnp.int32)
    row_marks = lax.dynamic_slice_in_dim(residue_mask, row * H, H, axis=1)
    row_valid = (
        (row_offsets[None, :] < column_ids(block_count, row_block)[:, None]) & (row_marks == 1)
    ).astype(F32)
    feat_cols = (feats[:4] * col_valid[:, None, :]).astype(BF)
    feat_rows = jnp.where(half == 0, feats[4:, :, :H], feats[4:, :, H:])
    feat_rows = (feat_rows * row_valid[:, None, :]).astype(BF)
    left_terms = jnp.einsum("fc,tfi->tci", row_embed, feat_rows, preferred_element_type=F32)
    right_terms = jnp.einsum("fc,tfj->tcj", col_embed, feat_cols, preferred_element_type=F32)
    left_cut = left_terms.reshape(T, C, 8, 8).transpose(0, 1, 3, 2).reshape(T, K8, 8)
    right_wide = jnp.broadcast_to(right_terms[:, :, None, :], (T, C, 8, W))
    gain = norm_gain.astype(F32)
    gain_wide = jnp.broadcast_to(gain[:, None, None], (C, 8, W))
    kl, kr, kg, ko, kb = expand(
        jnp.stack([left_proj.T, right_proj.T, gate_proj.T, out_proj.T, out_proj])
    )
    pick = jnp.asarray(
        np.arange(W)[None, None, :]
        == 2 * np.arange(4)[:, None, None] + (np.arange(2 * W) // W)[None, :, None],
        BF,
    )

    sent, scaled, inv, pair_sum = run_norm(template_pair, left_cut, right_wide, gain_wide, kl, kr)
    factors = exchange(sent.reshape(128, ROWS, W))
    back = run_back(scaled, embed_grad, kg, kb)
    factors, back = lax.optimization_barrier((factors, back))
    my_inv = factors[:, 256:]
    inv_all = in_order(core, my_inv, swap_cores(my_inv), 1)
    prod = exchange(run_product(factors)).reshape(T, C, H, W)
    left, right, inv_matrix = run_square(factors, inv_all)
    prod, left, right, inv_matrix = lax.optimization_barrier((prod, left, right, inv_matrix))
    grads = exchange(run_grad(prod, back).reshape(128, 2 * H, W))
    embedding, gate_mean, gate_rows, gate_cols, out_rows, out_cols = run_gate(
        prod, scaled, embed_grad, pair_sum, inv, kg, ko, pick
    )
    grads, embedding, gate_mean, gate_rows, gate_cols, out_rows, out_cols = (
        lax.optimization_barrier(
            (grads, embedding, gate_mean, gate_rows, gate_cols, out_rows, out_cols)
        )
    )
    kept, given, sums = run_factor(core, left, right, grads, inv_matrix)
    mean_half = (kept.astype(F32) + swap_cores(given).astype(F32)).astype(BF)
    sums, mean_half = lax.optimization_barrier((sums, mean_half))
    recv = exchange(mean_half).reshape(T, 16, 2, H // 2, W)
    close_rows, close_cols = run_close(recv, gate_mean, inv, scaled, pick)

    def center(weights):
        scaled_weights = gain[:, None] * weights.astype(F32)
        return scaled_weights - jnp.mean(scaled_weights, axis=0, keepdims=True)

    embeds = jnp.stack([row_embed, col_embed]).astype(F32)
    mixed = jnp.einsum(
        "efd,kdc->kefc",
        embeds,
        jnp.stack([center(left_proj), center(right_proj), center(gate_proj)]),
        precision=HIGHEST,
    )
    closing = -embeds / gain[None, None, :]
    opening = embeds * (1.0 / T)

    def finish(side, gated, closed, out, valid):
        total = jnp.einsum("fc,tci->tfi", mixed[2, side], gated, precision=HIGHEST)
        total = total + jnp.einsum("fc,tci->tfi", closing[side], closed, precision=HIGHEST)
        total = total + jnp.einsum("fc,ci->fi", opening[side], out, precision=HIGHEST)[None]
        return total * valid[:, None, :]

    grad_rows = finish(
        0, lane_rows(gate_rows), lane_rows(close_rows), lane_rows(out_rows), row_valid
    )
    grad_cols = finish(
        1, lane_cols(gate_cols), lane_cols(close_cols), lane_cols(out_cols), col_valid
    )
    owned = jnp.sum(sums, axis=2).reshape(2, 2, 2, N)
    weights = lax.dynamic_slice_in_dim(mixed[:2], 2 * pair_at, 2, axis=3)
    grad_own = jnp.einsum("kefs,sken->fn", weights, owned, precision=HIGHEST)
    all_offsets = jnp.arange(N, dtype=jnp.int32)
    own_map = lax.dynamic_index_in_dim(block_map, own, axis=0, keepdims=False)
    own_count = lax.dynamic_index_in_dim(block_count, own, axis=0, keepdims=False)
    own_marks = lax.dynamic_index_in_dim(residue_mask, own, axis=0, keepdims=False)
    own_valid = (
        (all_offsets % W).reshape(8, W) < own_count[:, None]
    ) & (own_marks.reshape(8, W) == 1)
    grad_own = grad_own.reshape(C, 8, W).transpose(1, 0, 2) * own_valid.astype(F32)[:, None, :]
    blank = jnp.zeros_like(grad_rows)
    grad_rows = jnp.concatenate(
        [jnp.where(half == 0, grad_rows, blank), jnp.where(half == 0, blank, grad_rows)], axis=2
    )
    entries = jnp.concatenate([grad_own, grad_rows, grad_cols], axis=0).astype(BF)
    kept = jnp.where(core == 0, entries[:, :32], entries[:, 32:])
    given = jnp.where(core == 0, entries[:, 32:], entries[:, :32])
    entries = jnp.concatenate([kept, swap_cores(given)], axis=0)
    targets = jnp.concatenate([own_map, row_ids, col_ids, own_map, row_ids, other_ids])
    place = (targets[None, :] == blocks[:, None]).astype(BF)
    placed = jnp.einsum(
        "be,ex->bx", place, entries.reshape(32, 32 * W), preferred_element_type=F32
    ).astype(BF)
    back = exchange(placed.reshape(128, 32, W)).reshape(64, 2 * 32, W)
    feat_grad = jnp.sum(back.astype(F32), axis=0)[None]
    return (embedding, feat_grad)


def solution(mesh):
    return jax.shard_map(
        per_device,
        mesh=mesh,
        in_specs=(
            P(None, None, "row", "col"),
            P(("row", "col"), None, None),
            P(),
            P(),
            P(),
            P(),
            P(),
            P(),
            P(),
            P(),
            P(),
            P(),
            P(None, "row", "col"),
        ),
        out_specs=(P(None, "row", "col"), P(("row", "col"), None, None)),
        check_vma=False,
    )
```

```python
import jax
import jax.numpy as jnp
import numpy as np
from jax import lax
from jax.experimental import pallas as pl
from jax.experimental.pallas import tpu as pltpu
from jax.sharding import PartitionSpec as P

EPS = 1e-05
HIGHEST = lax.Precision.HIGHEST
F32 = jnp.float32
BF = jnp.bfloat16
AXES = ("row", "col")
VMEM = 60 * 2**20

C = 64
T = 4
H = 64
W = 128
N = 1024
K8 = C * 8
ROWS = 288


def params():
    return pltpu.CompilerParams(vmem_limit_bytes=VMEM)


def stack_rows(top, bottom):
    return jnp.concatenate([top.reshape(K8, W), bottom.reshape(K8, W)], axis=1)


def unstack_rows(wide):
    return wide[:, :W].reshape(C, 8, W), wide[:, W:].reshape(C, 8, W)


def join_rows(top, bottom):
    return jnp.concatenate([top, bottom], axis=1)


def halves(value):
    return value[:, :8, :], value[:, 8:, :]


def mean_channels(value):
    return jnp.sum(value, axis=0, keepdims=True) * (1.0 / C)


def whole_spec(*shape):
    return pl.BlockSpec(shape, lambda t: (0,) * len(shape))


def each_spec(*shape):
    return pl.BlockSpec((1, *shape), lambda t: (t,) + (0,) * len(shape))


def row_mask(width):
    lane = lax.broadcasted_iota(jnp.int32, (8, width), 1)
    return (lane % 8 == lax.broadcasted_iota(jnp.int32, (8, width), 0)).astype(F32)


def spread_terms(left_ref, right_ref, right):
    mask = row_mask(W)
    rows = []
    for c in range(C):
        right[c] = jnp.broadcast_to(right_ref[0, c : c + 1, :], (8, W))
        rows.append(jnp.broadcast_to(left_ref[0, c : c + 1, :], (8, W)) * mask)
    value = jnp.concatenate(rows, axis=0)
    rest = value - value.astype(BF).astype(F32)
    lane = lax.broadcasted_iota(jnp.int32, (K8, W), 1)
    return jnp.where(lane < H, value, rest).astype(BF)


def make_pairs(pair_ref, left, lanes_ref, right, g):
    terms = unstack_rows(jnp.dot(left, lanes_ref[g], preferred_element_type=F32))
    raw = halves(pair_ref[0, :, g * 16 : g * 16 + 16, :].astype(F32))
    return [raw[part] + terms[part] + right[...] for part in range(2)]


def norm_kernel(
    pair_ref, left_ref, right_ref, lanes_ref, gain_ref, kl_ref, kr_ref, pay_ref, inv_ref, right
):
    left = spread_terms(left_ref, right_ref, right)
    for g in range(4):
        scaleds, invs = [], []
        for pair in make_pairs(pair_ref, left, lanes_ref, right, g):
            shifted = pair - mean_channels(pair)
            inverse = lax.rsqrt(mean_channels(shifted * shifted) + EPS)
            scaleds.append(shifted * inverse * gain_ref[...])
            invs.append(inverse[0])
        both = jnp.concatenate(invs, axis=0)
        inv_ref[0, g * 16 : g * 16 + 16, :] = both
        wide = stack_rows(*scaleds).astype(BF)
        for k, weight in enumerate((kl_ref, kr_ref)):
            out = jnp.dot(weight[...], wide, preferred_element_type=F32)
            out = join_rows(*unstack_rows(out)).astype(BF).reshape(C // 2, 2, 16, W)
            for s in range(2):
                first = k * 128 + s * 64 + g * 16
                pay_ref[0, :, first : first + 16, :] = out[:, s]
        first = 256 + (g % 2) * 16
        for q in range(g // 2, C // 2, 2):
            pay_ref[0, q, first : first + 16, :] = both.astype(BF)


TERM_SPECS = [each_spec(C, H, W), each_spec(C, W), each_spec(C, W), whole_spec(4, W, 2 * W), whole_spec(C, 8, W)]


def run_norm(pair, left, right, lanes, gain, kl, kr):
    return pl.pallas_call(
        norm_kernel,
        grid=(T,),
        in_specs=[*TERM_SPECS, whole_spec(K8, K8), whole_spec(K8, K8)],
        out_specs=[each_spec(C // 2, ROWS, W), each_spec(H, W)],
        out_shape=[
            jax.ShapeDtypeStruct((T, C // 2, ROWS, W), BF),
            jax.ShapeDtypeStruct((T, H, W), F32),
        ],
        scratch_shapes=[pltpu.VMEM((C, 8, W), F32)],
        compiler_params=params(),
        name="pair_norm",
    )(pair, left, right, lanes, gain, kl, kr)


def spread(blocks_ref, full_ref):
    @pl.loop(0, 16)
    def _(r):
        for c in range(8):
            full_ref[pl.ds(r * H, H), c * W : (c + 1) * W] = blocks_ref[r * 8 + c]


def product_kernel(left_ref, right_ref, out_ref, left, right):
    spread(left_ref, left)
    spread(right_ref, right)

    out = lax.dot_general(
        left[...], right[...], (((1,), (1,)), ((), ())), preferred_element_type=F32
    ).astype(BF)
    for r in range(16):
        for c in range(8):
            out_ref[r * 8 + c] = out[r * H : (r + 1) * H, c * W : (c + 1) * W]


def run_product(factors):
    spec = lambda first: pl.BlockSpec((128, H, W), lambda s: (0, first + s, 0))
    return pl.pallas_call(
        product_kernel,
        grid=(2,),
        in_specs=[spec(0), spec(2)],
        out_specs=pl.BlockSpec((128, H, W), lambda s: (0, s, 0)),
        out_shape=jax.ShapeDtypeStruct((128, 2 * H, W), BF),
        scratch_shapes=[pltpu.VMEM((N, N), BF), pltpu.VMEM((N, N), BF)],
        compiler_params=params(),
        name="triangle_product",
    )(factors, factors)


def back_kernel(
    pair_ref, left_ref, right_ref, lanes_ref, gain_ref, inv_ref, grad_ref, kg_ref, kb_ref,
    scaled_ref, out_ref, sum_ref, right,
):
    step = pl.program_id(0)
    left = spread_terms(left_ref, right_ref, right)

    @pl.when(step == 0)
    def _():
        sum_ref[...] = jnp.zeros_like(sum_ref)

    for g in range(4):
        rows = slice(g * 16, g * 16 + 16)
        pairs = make_pairs(pair_ref, left, lanes_ref, right, g)
        sum_ref[:, rows, :] += join_rows(*pairs)
        scaleds = []
        for part in range(2):
            first = g * 16 + part * 8
            inverse = inv_ref[0, first : first + 8, :][None]
            scaleds.append((pairs[part] - mean_channels(pairs[part])) * inverse * gain_ref[...])
        scaled_ref[0, :, rows, :] = join_rows(*scaleds).astype(BF)
        opened = unstack_rows(
            jnp.dot(kg_ref[...], stack_rows(*scaleds).astype(BF), preferred_element_type=F32)
        )
        grads = halves(grad_ref[:, rows, :].astype(F32))
        grad_projs = [
            grads[part] * (1.0 / T) * jax.nn.sigmoid(opened[part]) for part in range(2)
        ]
        grad_norms = unstack_rows(
            jnp.dot(kb_ref[...], stack_rows(*grad_projs).astype(BF), preferred_element_type=F32)
        )
        outs = [grad_norm - mean_channels(grad_norm) for grad_norm in grad_norms]
        out_ref[0, :, rows, :] = join_rows(*outs).astype(BF)


def run_back(pair, left, right, lanes, gain, inv, grad, kg, kb):
    return pl.pallas_call(
        back_kernel,
        grid=(T,),
        in_specs=[
            *TERM_SPECS, each_spec(H, W), whole_spec(C, H, W), whole_spec(K8, K8), whole_spec(K8, K8)
        ],
        out_specs=[each_spec(C, H, W), each_spec(C, H, W), whole_spec(C, H, W)],
        out_shape=[
            jax.ShapeDtypeStruct((T, C, H, W), BF),
            jax.ShapeDtypeStruct((T, C, H, W), BF),
            jax.ShapeDtypeStruct((C, H, W), F32),
        ],
        scratch_shapes=[pltpu.VMEM((C, 8, W), F32)],
        compiler_params=params(),
        cost_estimate=pl.CostEstimate(flops=4 * 2**31, bytes_accessed=16 * 2**20, transcendentals=2**21),
        name="back_project",
    )(pair, left, right, lanes, gain, inv, grad, kg, kb)


def product_norm(product):
    shifted = product - mean_channels(product)
    return shifted, lax.rsqrt(mean_channels(shifted * shifted) + EPS)


def grad_kernel(prod_ref, back_ref, out_ref):
    for g in range(4):
        rows = slice(g * 16, g * 16 + 16)
        shifted, inverse = product_norm(prod_ref[0, :, rows, :].astype(F32))
        back = back_ref[0, :, rows, :].astype(F32)
        slope = mean_channels(back * shifted) * inverse * inverse
        out_ref[0, :, rows, :] = ((back - shifted * slope) * inverse).astype(BF)


def run_grad(prod, back):
    return pl.pallas_call(
        grad_kernel,
        grid=(T,),
        in_specs=[each_spec(C, H, W), each_spec(C, H, W)],
        out_specs=each_spec(C, H, W),
        out_shape=jax.ShapeDtypeStruct((T, C, H, W), BF),
        compiler_params=params(),
        cost_estimate=pl.CostEstimate(flops=2**25, bytes_accessed=12 * 2**20, transcendentals=0),
        name="product_grad",
    )(prod, back)


def fold_rows(sums):
    return jnp.sum(sums.reshape(C, 8, W) * row_mask(W)[None], axis=1)


def gate_kernel(
    prod_ref, scaled_ref, grad_ref, sum_ref, inv_ref, kg_ref, ko_ref, pick_ref,
    emb_ref, mean_ref, rows_ref, cols_ref, grows_ref, gcols_ref, total,
):
    step = pl.program_id(0)
    row_sums = jnp.zeros((K8, W), F32)
    col_sums = jnp.zeros((C, 8, W), F32)
    for g in range(4):
        rows = slice(g * 16, g * 16 + 16)
        scaled = stack_rows(*halves(scaled_ref[0, :, rows, :].astype(F32))).astype(BF)
        opened = unstack_rows(jnp.dot(kg_ref[...], scaled, preferred_element_type=F32))
        normed = []
        for product in halves(prod_ref[0, :, rows, :].astype(F32)):
            shifted, inverse = product_norm(product)
            normed.append(shifted * inverse)
        projected = unstack_rows(
            jnp.dot(ko_ref[...], stack_rows(*normed).astype(BF), preferred_element_type=F32)
        )
        grads = halves(grad_ref[:, rows, :].astype(F32))
        weighted = []
        for part in range(2):
            first = g * 16 + part * 8
            where = (slice(None), slice(first, first + 8), slice(None))
            gate = jax.nn.sigmoid(opened[part])
            gated = gate * projected[part]

            @pl.when(step == 0)
            def _():
                total[where] = sum_ref[where] + gated

            @pl.when(step > 0)
            def _():
                total[where] += gated

            grad_gate = grads[part] * (1.0 / T) * gated * (1.0 - gate)
            mean_ref[0, first : first + 8, :] = jnp.sum(grad_gate * opened[part], axis=0)
            term = grad_gate * inv_ref[0, first : first + 8, :][None]
            col_sums = col_sums + term
            weighted.append(term)
        row_sums = row_sums + jnp.dot(
            stack_rows(*weighted).astype(BF), pick_ref[g], preferred_element_type=F32
        )
    rows_ref[0] = fold_rows(row_sums)
    cols_ref[0] = jnp.sum(col_sums, axis=1)

    @pl.when(step == 0)
    def _():
        grad_rows = jnp.zeros((K8, W), F32)
        grad_cols = jnp.zeros((C, 8, W), F32)
        for g in range(4):
            top, bottom = halves(grad_ref[:, g * 16 : g * 16 + 16, :].astype(F32))
            grad_cols = grad_cols + top + bottom
            grad_rows = grad_rows + jnp.dot(
                stack_rows(top, bottom).astype(BF), pick_ref[g], preferred_element_type=F32
            )
        grows_ref[...] = fold_rows(grad_rows)
        gcols_ref[...] = jnp.sum(grad_cols, axis=1)

    @pl.when(step == T - 1)
    def _():
        emb_ref[...] = (total[...] * (1.0 / T)).astype(BF)


def run_gate(prod, scaled, grad, pair_sum, inv, kg, ko, pick):
    return pl.pallas_call(
        gate_kernel,
        grid=(T,),
        in_specs=[
            each_spec(C, H, W), each_spec(C, H, W), whole_spec(C, H, W), whole_spec(C, H, W),
            each_spec(H, W), whole_spec(K8, K8), whole_spec(K8, K8), whole_spec(4, 2 * W, W),
        ],
        out_specs=[
            whole_spec(C, H, W), each_spec(H, W), each_spec(C, W), each_spec(C, W),
            whole_spec(C, W), whole_spec(C, W),
        ],
        out_shape=[
            jax.ShapeDtypeStruct((C, H, W), BF),
            jax.ShapeDtypeStruct((T, H, W), F32),
            jax.ShapeDtypeStruct((T, C, W), F32),
            jax.ShapeDtypeStruct((T, C, W), F32),
            jax.ShapeDtypeStruct((C, W), F32),
            jax.ShapeDtypeStruct((C, W), F32),
        ],
        scratch_shapes=[pltpu.VMEM((C, H, W), F32)],
        compiler_params=params(),
        cost_estimate=pl.CostEstimate(flops=4 * 2**31, bytes_accessed=12 * 2**20, transcendentals=2**21),
        name="gate_and_embed",
    )(prod, scaled, grad, pair_sum, inv, kg, ko, pick)


def square_kernel(left_ref, right_ref, inv_ref, left, right, inv):
    step = pl.program_id(0)
    spread(left_ref, left.at[0])
    spread(right_ref, right.at[0])

    @pl.when(step == 0)
    def _():
        spread(inv_ref, inv)


def run_square(factors, inv):
    spec = lambda first: pl.BlockSpec((128, H, W), lambda s: (0, first + s, 0))
    out = pl.BlockSpec((1, N, N), lambda s: (s, 0, 0))
    return pl.pallas_call(
        square_kernel,
        grid=(2,),
        in_specs=[spec(0), spec(2), pl.BlockSpec((128, H, W), lambda s: (0, 0, 0))],
        out_specs=[out, out, pl.BlockSpec((N, N), lambda s: (0, 0))],
        out_shape=[jax.ShapeDtypeStruct((2, N, N), BF)] * 2 + [jax.ShapeDtypeStruct((N, N), BF)],
        compiler_params=params(),
        cost_estimate=pl.CostEstimate(flops=2**20, bytes_accessed=20 * 2**20, transcendentals=0),
        name="to_matrices",
    )(factors, factors, inv)


def factor_kernel(
    core_ref, left_ref, right_ref, grad_ref, inv_ref,
    kept_ref, given_ref, cols_ref, rows_ref, grad, mean,
):
    step = pl.program_id(0)
    core = core_ref[0]
    left, right = left_ref.at[0], right_ref.at[0]
    spread(grad_ref, grad)

    @pl.when(step == 0)
    def _():
        mean[...] = jnp.zeros_like(mean)

    def finish(value, rows, factor, kind):
        mean[rows, :] += value * factor[rows, :].astype(F32)
        term = value * inv_ref[rows, :].astype(F32)
        part = jnp.sum(term.reshape(64, 8, N), axis=0)
        lanes = term[:, :W]
        for c in range(1, 8):
            lanes = lanes + term[:, c * W : (c + 1) * W]
        rows_ref[0, kind, rows, :] = lanes
        return part

    blocks = [slice(b * 512, b * 512 + 512) for b in range(2)]
    total = None
    for rows in blocks:
        value = jnp.dot(grad[rows, :], right[...], preferred_element_type=F32)
        part = finish(value, rows, left, 0)
        total = part if total is None else total + part
    cols_ref[0, 0] = total
    total = None
    for rows in blocks:
        value = lax.dot_general(
            grad[:, rows], left[...], (((0,), (0,)), ((), ())), preferred_element_type=F32
        )
        part = finish(value, rows, right, 1)
        total = part if total is None else total + part
    cols_ref[0, 1] = total

    @pl.when(step == 1)
    def _():
        @pl.loop(0, 16)
        def _(r):
            mine = pl.ds(pl.multiple_of(r * H + core * 32, 32), 32)
            other = pl.ds(pl.multiple_of(r * H + (1 - core) * 32, 32), 32)
            for c in range(8):
                kept_ref[r * 8 + c] = mean[mine, c * W : (c + 1) * W].astype(BF)
                given_ref[r * 8 + c] = mean[other, c * W : (c + 1) * W].astype(BF)


def run_factor(core, left, right, grad, inv):
    matrix = pl.BlockSpec((1, N, N), lambda s: (s, 0, 0))
    return pl.pallas_call(
        factor_kernel,
        grid=(2,),
        in_specs=[
            pl.BlockSpec(memory_space=pltpu.SMEM),
            matrix,
            matrix,
            pl.BlockSpec((128, H, W), lambda s: (0, s, 0)),
            pl.BlockSpec((N, N), lambda s: (0, 0)),
        ],
        out_specs=[
            pl.BlockSpec((128, H // 2, W), lambda s: (0, 0, 0)),
            pl.BlockSpec((128, H // 2, W), lambda s: (0, 0, 0)),
            pl.BlockSpec((1, 2, 8, N), lambda s: (s, 0, 0, 0)),
            pl.BlockSpec((1, 2, N, W), lambda s: (s, 0, 0, 0)),
        ],
        out_shape=[
            jax.ShapeDtypeStruct((128, H // 2, W), BF),
            jax.ShapeDtypeStruct((128, H // 2, W), BF),
            jax.ShapeDtypeStruct((2, 2, 8, N), F32),
            jax.ShapeDtypeStruct((2, 2, N, W), F32),
        ],
        scratch_shapes=[pltpu.VMEM((N, N), BF), pltpu.VMEM((N, N), F32)],
        compiler_params=params(),
        name="factor_grads",
    )(core.reshape(1), left, right, grad, inv)


def close_kernel(
    recv_ref, mean_ref, inv_ref, scaled_ref, pick_ref, weight_ref, valid_ref, base_ref, out_ref
):
    got = recv_ref[0].astype(F32)
    total = got[0]
    for k in range(1, 16):
        total = total + got[k]
    weight = (total.reshape(H, W) + mean_ref[0]) * inv_ref[0] * (1.0 / C)
    row_sums = jnp.zeros((K8, W), F32)
    col_sums = jnp.zeros((C, 8, W), F32)
    for g in range(4):
        scaled = scaled_ref[0, :, g * 16 : g * 16 + 16, :].astype(F32)
        terms = []
        for part in range(2):
            first = g * 16 + part * 8
            term = scaled[:, part * 8 : part * 8 + 8, :] * weight[first : first + 8, :][None]
            col_sums = col_sums + term
            terms.append(term)
        row_sums = row_sums + jnp.dot(
            stack_rows(*terms).astype(BF), pick_ref[g], preferred_element_type=F32
        )
    for side, sums in enumerate((fold_rows(row_sums), jnp.sum(col_sums, axis=1))):
        value = jnp.dot(weight_ref[side], sums, precision=HIGHEST, preferred_element_type=F32)
        out_ref[side, 0] = (base_ref[side, 0] + value * valid_ref[side, 0]).astype(BF)


def run_close(recv, mean, inv, scaled, pick, weights, valid, base):
    both = lambda *shape: pl.BlockSpec((2, 1, *shape), lambda t: (0, t) + (0,) * len(shape))
    return pl.pallas_call(
        close_kernel,
        grid=(T,),
        in_specs=[
            each_spec(16, 2, H // 2, W), each_spec(H, W), each_spec(H, W), each_spec(C, H, W),
            whole_spec(4, 2 * W, W), whole_spec(2, C, C), both(1, W), both(C, W),
        ],
        out_specs=both(C, W),
        out_shape=jax.ShapeDtypeStruct((2, T, C, W), BF),
        compiler_params=params(),
        name="close_sums",
    )(recv, mean, inv, scaled, pick, weights, valid, base)


def from_member(value, k):
    return lax.ppermute(value, "col", [(i, i ^ k) for i in range(8)])


def swap_cores(value):
    return from_member(value, 1)


def exchange(value):
    return lax.all_to_all(value, AXES, split_axis=0, concat_axis=0, tiled=True)


def in_order(core, mine, other, axis):
    first = jnp.where(core == 0, mine, other)
    second = jnp.where(core == 0, other, mine)
    return jnp.concatenate([first, second], axis=axis)


def by_member(value, member):
    lead, last = value.shape[:-2], value.shape[-1]
    cut = value.reshape(*lead, 2, 2, 16, last)
    cut = jnp.where(member % 2 == 1, cut[..., ::-1, :, :], cut)
    cut = jnp.where(member // 2 == 1, cut[..., ::-1, :, :, :], cut)
    return cut.reshape(*lead, 64, last)


def expand(weights):
    to = jnp.asarray(np.kron(np.eye(C), np.ones((8, 1))), BF)
    tall = jnp.einsum("ac,ncd->nad", to, weights, preferred_element_type=F32).astype(BF)
    wide = jnp.einsum("nad,bd->nab", tall, to, preferred_element_type=F32)
    index = jnp.arange(K8, dtype=jnp.int32) % 8
    return jnp.where(index[:, None] == index[None, :], wide, 0.0).astype(BF)


def per_device(
    template_pair,
    template_feat,
    block_map,
    block_count,
    residue_mask,
    row_embed,
    col_embed,
    norm_gain,
    left_proj,
    right_proj,
    gate_proj,
    out_proj,
    embed_grad,
):
    row = lax.axis_index("row")
    col = lax.axis_index("col")
    core = col % 2
    me = row * 8 + col
    own = me // 32
    pair_at = me % 32
    blocks = jnp.arange(128, dtype=jnp.int32)
    half = row % 2
    row_block = row // 2

    member = col % 4
    sent_feat = jnp.broadcast_to(template_feat.reshape(1, 4, 16, W), (32, 4, 16, W))
    pool = exchange(sent_feat.reshape(128, 16, W))
    column_ids = lambda m, at: lax.dynamic_index_in_dim(m, at, axis=1, keepdims=False)
    row_ids = column_ids(block_map, row_block)
    member_ids = [column_ids(block_map, col ^ k) for k in range(4)]
    wanted = jnp.concatenate([jnp.concatenate([ids, row_ids]) for ids in member_ids])
    choose = (wanted[:, None] == blocks[None, :]).astype(BF)
    picked = jnp.einsum(
        "eb,bx->ex", choose, pool.reshape(128, 16 * W), preferred_element_type=F32
    ).astype(BF)
    picked = picked.reshape(4, 8, 16, W)
    feats = jnp.concatenate(
        [picked[0]] + [from_member(picked[k], k) for k in range(1, 4)], axis=1
    )
    embeds = by_member(jnp.stack([row_embed, col_embed]), member)

    offsets = jnp.arange(W, dtype=jnp.int32)

    def marks(at):
        kept = lax.dynamic_slice_in_dim(residue_mask, at * W, W, axis=1) == 1
        return kept & (offsets[None, :] < column_ids(block_count, at)[:, None])

    col_valid = marks(col).astype(F32)
    row_valid = (marks(row_block) & (offsets // H == half)[None, :]).astype(F32)
    left_terms = jnp.einsum("fc,tfi->tci", embeds[0], feats[4:], preferred_element_type=F32)
    left_terms = left_terms * row_valid[:, None, :]
    near, far = left_terms[:, :, :H], left_terms[:, :, H:]
    left_twice = near + far
    left_twice = jnp.concatenate([left_twice, left_twice], axis=2)
    right_terms = jnp.einsum("fc,tfj->tcj", embeds[1], feats[:4], preferred_element_type=F32)
    right_terms = right_terms * col_valid[:, None, :]
    gain = norm_gain.astype(F32)
    gain_wide = jnp.broadcast_to(gain[:, None, None], (C, 8, W))
    kl, kr, kg, ko, kb = expand(
        jnp.stack([left_proj.T, right_proj.T, gate_proj.T, out_proj.T, out_proj])
    )
    group = 2 * np.arange(4)[:, None, None] + (np.arange(2 * W) // W)[None, :, None]
    lanes = np.arange(W)[None, None, :] % H // 8 == group
    terms_pick = jnp.asarray(lanes.transpose(0, 2, 1), BF)
    sums_pick = jnp.where((offsets // H == half)[None, None, :], jnp.asarray(lanes, BF), 0)

    terms = (template_pair, left_twice, right_terms, terms_pick, gain_wide)
    sent, inv = run_norm(*terms, kl, kr)
    factors = exchange(sent.reshape(128, ROWS, W))
    scaled, back, pair_sum = run_back(*terms, inv, embed_grad, kg, kb)
    factors, scaled, back, pair_sum = lax.optimization_barrier((factors, scaled, back, pair_sum))
    my_inv = factors[:, 256:]
    inv_all = in_order(core, my_inv, swap_cores(my_inv), 1)
    prod = exchange(run_product(factors)).reshape(T, C, H, W)
    left, right, inv_matrix = run_square(factors, inv_all)
    prod, left, right, inv_matrix = lax.optimization_barrier((prod, left, right, inv_matrix))
    grads = exchange(run_grad(prod, back).reshape(128, 2 * H, W))
    embedding, gate_mean, gate_rows, gate_cols, out_rows, out_cols = run_gate(
        prod, scaled, embed_grad, pair_sum, inv, kg, ko, sums_pick
    )
    grads, embedding, gate_mean, gate_rows, gate_cols, out_rows, out_cols = (
        lax.optimization_barrier(
            (grads, embedding, gate_mean, gate_rows, gate_cols, out_rows, out_cols)
        )
    )
    kept, given, col_sums, row_sums = run_factor(core, left, right, grads, inv_matrix)
    mean_half = (kept.astype(F32) + swap_cores(given).astype(F32)).astype(BF)
    col_sums, row_sums, mean_half = lax.optimization_barrier((col_sums, row_sums, mean_half))
    recv = exchange(mean_half).reshape(T, 16, 2, H // 2, W)

    def center(weights):
        scaled_weights = gain[:, None] * weights.astype(F32)
        return scaled_weights - jnp.mean(scaled_weights, axis=0, keepdims=True)

    embeds = embeds.astype(F32)
    mixed = jnp.einsum(
        "efd,kdc->kefc",
        embeds,
        jnp.stack([center(left_proj), center(right_proj), center(gate_proj)]),
        precision=HIGHEST,
    )
    closing = -embeds / gain[None, None, :]
    opening = embeds * (1.0 / T)
    valid = jnp.stack([row_valid, col_valid])[:, :, None, :]
    base = jnp.einsum(
        "efc,etcp->etfp", mixed[2], jnp.stack([gate_rows, gate_cols]), precision=HIGHEST
    )
    opened = jnp.einsum(
        "efc,ecp->efp", opening, jnp.stack([out_rows, out_cols]), precision=HIGHEST
    )
    base = (base + opened[:, None]) * valid
    owned = jnp.stack([jnp.sum(row_sums, axis=3), jnp.sum(col_sums, axis=2)], axis=2)
    weights = lax.dynamic_slice_in_dim(mixed[:2], 2 * pair_at, 2, axis=3)
    grad_own = jnp.einsum("kefs,sken->fn", weights, owned, precision=HIGHEST)
    own_map = lax.dynamic_index_in_dim(block_map, own, axis=0, keepdims=False)
    own_count = lax.dynamic_index_in_dim(block_count, own, axis=0, keepdims=False)
    own_marks = lax.dynamic_index_in_dim(residue_mask, own, axis=0, keepdims=False)
    own_valid = (offsets[None, :] < own_count[:, None]) & (own_marks.reshape(8, W) == 1)
    grad_own = grad_own.reshape(C, 8, W).transpose(1, 0, 2) * own_valid.astype(F32)[:, None, :]
    grad_own = grad_own.astype(BF)
    targets = jnp.concatenate([jnp.concatenate([own_map, row_ids, ids]) for ids in member_ids])
    place = (targets[None, :] == blocks[:, None]).astype(BF)
    recv, base, grad_own, place = lax.optimization_barrier((recv, base, grad_own, place))

    closed = run_close(recv, gate_mean, inv, scaled, sums_pick, closing, valid, base)
    entries = jnp.concatenate([grad_own, closed.reshape(2 * T, C, W)], axis=0)
    quarters = [entries[:, k * 16 : k * 16 + 16] for k in range(4)]
    entries = jnp.concatenate(
        [quarters[0]] + [from_member(quarters[k], k) for k in range(1, 4)], axis=0
    )
    placed = jnp.einsum(
        "be,ex->bx", place, entries.reshape(64, 16 * W), preferred_element_type=F32
    ).astype(BF)
    result = exchange(placed.reshape(128, 16, W)).reshape(32, 4 * 16, W)
    feat_grad = jnp.sum(result.astype(F32), axis=0)[None]
    return (embedding, feat_grad)


def solution(mesh):
    return jax.shard_map(
        per_device,
        mesh=mesh,
        in_specs=(
            P(None, None, "row", "col"),
            P(("row", "col"), None, None),
            P(),
            P(),
            P(),
            P(),
            P(),
            P(),
            P(),
            P(),
            P(),
            P(),
            P(None, "row", "col"),
        ),
        out_specs=(P(None, "row", "col"), P(("row", "col"), None, None)),
        check_vma=False,
    )
```

```python
import jax
import jax.numpy as jnp
import numpy as np
from jax import lax
from jax.experimental import pallas as pl
from jax.experimental.pallas import tpu as pltpu
from jax.sharding import PartitionSpec as P

EPS = 1e-05
HIGHEST = lax.Precision.HIGHEST
F32 = jnp.float32
BF = jnp.bfloat16
AXES = ("row", "col")

C = 64
T = 4
H = 64
W = 128
N = 1024
K8 = C * 8
ROWS = 288


def params(mib):
    return pltpu.CompilerParams(vmem_limit_bytes=mib * 2**20)


def stack_rows(top, bottom):
    return jnp.concatenate([top.reshape(K8, W), bottom.reshape(K8, W)], axis=1)


def unstack_rows(wide):
    return wide[:, :W].reshape(C, 8, W), wide[:, W:].reshape(C, 8, W)


def join_rows(top, bottom):
    return jnp.concatenate([top, bottom], axis=1)


def halves(value):
    return value[:, :8, :], value[:, 8:, :]


def mean_channels(value):
    return jnp.sum(value, axis=0, keepdims=True) * (1.0 / C)


def whole_spec(*shape):
    return pl.BlockSpec(shape, lambda t: (0,) * len(shape))


def each_spec(*shape):
    return pl.BlockSpec((1, *shape), lambda t: (t,) + (0,) * len(shape))


def row_mask(width):
    lane = lax.broadcasted_iota(jnp.int32, (8, width), 1)
    return (lane % 8 == lax.broadcasted_iota(jnp.int32, (8, width), 0)).astype(F32)


def spread_terms(left_ref, right_ref, right):
    mask = row_mask(W)
    rows = []
    for c in range(C):
        right[c] = jnp.broadcast_to(right_ref[0, c : c + 1, :], (8, W))
        rows.append(jnp.broadcast_to(left_ref[0, c : c + 1, :], (8, W)) * mask)
    value = jnp.concatenate(rows, axis=0)
    rest = value - value.astype(BF).astype(F32)
    lane = lax.broadcasted_iota(jnp.int32, (K8, W), 1)
    return jnp.where(lane < H, value, rest).astype(BF)


def make_pairs(pair_ref, left, lanes_ref, right, g):
    terms = unstack_rows(jnp.dot(left, lanes_ref[g], preferred_element_type=F32))
    raw = halves(pair_ref[0, :, g * 16 : g * 16 + 16, :].astype(F32))
    return [raw[part] + terms[part] + right[...] for part in range(2)]


def norm_kernel(
    pair_ref, left_ref, right_ref, lanes_ref, gain_ref, kl_ref, kr_ref, pay_ref, inv_ref,
    right, terms, wide,
):
    left = spread_terms(left_ref, right_ref, right)
    for g in range(4):
        terms[g] = jnp.dot(left, lanes_ref[g], preferred_element_type=F32)
    for g in range(4):
        scaleds, invs = [], []
        left_terms = unstack_rows(terms[g])
        raw = halves(pair_ref[0, :, g * 16 : g * 16 + 16, :].astype(F32))
        for part in range(2):
            pair = raw[part] + left_terms[part] + right[...]
            shifted = pair - mean_channels(pair)
            inverse = lax.rsqrt(mean_channels(shifted * shifted) + EPS)
            scaleds.append(shifted * inverse * gain_ref[...])
            invs.append(inverse[0])
        both = jnp.concatenate(invs, axis=0)
        inv_ref[0, g * 16 : g * 16 + 16, :] = both
        wide[:, g * 256 : g * 256 + 256] = stack_rows(*scaleds).astype(BF)
        first = 256 + (g % 2) * 16
        for q in range(g // 2, C // 2, 2):
            pay_ref[0, q, first : first + 16, :] = both.astype(BF)
    for k, weight in enumerate((kl_ref, kr_ref)):
        outs = jnp.dot(weight[...], wide[...], preferred_element_type=F32)
        for g in range(4):
            out = join_rows(*unstack_rows(outs[:, g * 256 : g * 256 + 256])).astype(BF).reshape(C // 2, 2, 16, W)
            for s in range(2):
                first = k * 128 + s * 64 + g * 16
                pay_ref[0, :, first : first + 16, :] = out[:, s]


TERM_SPECS = [each_spec(C, H, W), each_spec(C, W), each_spec(C, W), whole_spec(4, W, 2 * W), whole_spec(C, 8, W)]


def run_norm(pair, left, right, lanes, gain, kl, kr):
    return pl.pallas_call(
        norm_kernel,
        grid=(T,),
        in_specs=[*TERM_SPECS, whole_spec(K8, K8), whole_spec(K8, K8)],
        out_specs=[each_spec(C // 2, ROWS, W), each_spec(H, W)],
        out_shape=[
            pltpu.HBM((T, C // 2, ROWS, W), BF),
            jax.ShapeDtypeStruct((T, H, W), F32),
        ],
        scratch_shapes=[
            pltpu.VMEM((C, 8, W), F32),
            pltpu.VMEM((4, K8, 2 * W), F32),
            pltpu.VMEM((K8, N), BF),
        ],
        compiler_params=params(24),
        name="pair_norm",
    )(pair, left, right, lanes, gain, kl, kr)


def spread(blocks_ref, full_ref):
    @pl.loop(0, 16)
    def _(r):
        for c in range(8):
            full_ref[pl.ds(r * H, H), c * W : (c + 1) * W] = blocks_ref[r * 8 + c]


def product_kernel(left_ref, right_ref, out_ref, left, right):
    spread(left_ref, left)
    spread(right_ref, right)

    out = lax.dot_general(
        left[...], right[...], (((1,), (1,)), ((), ())), preferred_element_type=F32
    ).astype(BF)
    for r in range(16):
        for c in range(8):
            out_ref[r * 8 + c] = out[r * H : (r + 1) * H, c * W : (c + 1) * W]


def run_product(factors):
    spec = lambda first: pl.BlockSpec((128, H, W), lambda s: (0, first + s, 0))
    return pl.pallas_call(
        product_kernel,
        grid=(2,),
        in_specs=[spec(0), spec(2)],
        out_specs=pl.BlockSpec((128, H, W), lambda s: (0, s, 0)),
        out_shape=pltpu.HBM((128, 2 * H, W), BF),
        scratch_shapes=[pltpu.VMEM((N, N), BF), pltpu.VMEM((N, N), BF)],
        compiler_params=params(28),
        name="triangle_product",
    )(factors, factors)


def back_kernel(
    pair_ref, left_ref, right_ref, lanes_ref, gain_ref, inv_ref, grad_ref, kg_ref, kb_ref,
    scaled_ref, out_ref, sum_ref, right,
):
    step = pl.program_id(0)
    left = spread_terms(left_ref, right_ref, right)

    @pl.when(step == 0)
    def _():
        sum_ref[...] = jnp.zeros_like(sum_ref)

    for g in range(4):
        rows = slice(g * 16, g * 16 + 16)
        pairs = make_pairs(pair_ref, left, lanes_ref, right, g)
        sum_ref[:, rows, :] += join_rows(*pairs)
        scaleds = []
        for part in range(2):
            first = g * 16 + part * 8
            inverse = inv_ref[0, first : first + 8, :][None]
            scaleds.append((pairs[part] - mean_channels(pairs[part])) * inverse * gain_ref[...])
        scaled_ref[0, :, rows, :] = join_rows(*scaleds).astype(BF)
        opened = unstack_rows(
            jnp.dot(kg_ref[...], stack_rows(*scaleds).astype(BF), preferred_element_type=F32)
        )
        grads = halves(grad_ref[:, rows, :].astype(F32))
        grad_projs = [
            grads[part] * (1.0 / T) * jax.nn.sigmoid(opened[part]) for part in range(2)
        ]
        grad_norms = unstack_rows(
            jnp.dot(kb_ref[...], stack_rows(*grad_projs).astype(BF), preferred_element_type=F32)
        )
        outs = [grad_norm - mean_channels(grad_norm) for grad_norm in grad_norms]
        out_ref[0, :, rows, :] = join_rows(*outs).astype(BF)


def run_back(pair, left, right, lanes, gain, inv, grad, kg, kb):
    return pl.pallas_call(
        back_kernel,
        grid=(T,),
        in_specs=[
            *TERM_SPECS, each_spec(H, W), whole_spec(C, H, W), whole_spec(K8, K8), whole_spec(K8, K8)
        ],
        out_specs=[each_spec(C, H, W), each_spec(C, H, W), whole_spec(C, H, W)],
        out_shape=[
            jax.ShapeDtypeStruct((T, C, H, W), BF),
            jax.ShapeDtypeStruct((T, C, H, W), BF),
            jax.ShapeDtypeStruct((C, H, W), F32),
        ],
        scratch_shapes=[pltpu.VMEM((C, 8, W), F32)],
        compiler_params=params(24),
        cost_estimate=pl.CostEstimate(flops=4 * 2**31, bytes_accessed=16 * 2**20, transcendentals=2**21),
        name="back_project",
    )(pair, left, right, lanes, gain, inv, grad, kg, kb)


def product_norm(product):
    shifted = product - mean_channels(product)
    return shifted, lax.rsqrt(mean_channels(shifted * shifted) + EPS)


def grad_kernel(prod_ref, back_ref, out_ref):
    for g in range(4):
        rows = slice(g * 16, g * 16 + 16)
        shifted, inverse = product_norm(prod_ref[0, :, rows, :].astype(F32))
        back = back_ref[0, :, rows, :].astype(F32)
        slope = mean_channels(back * shifted) * inverse * inverse
        out_ref[0, :, rows, :] = ((back - shifted * slope) * inverse).astype(BF)


def run_grad(prod, back):
    return pl.pallas_call(
        grad_kernel,
        grid=(T,),
        in_specs=[each_spec(C, H, W), each_spec(C, H, W)],
        out_specs=each_spec(C, H, W),
        out_shape=pltpu.HBM((T, C, H, W), BF),
        compiler_params=params(16),
        cost_estimate=pl.CostEstimate(flops=2**25, bytes_accessed=12 * 2**20, transcendentals=0),
        name="product_grad",
    )(prod, back)


def fold_rows(sums):
    return jnp.sum(sums.reshape(C, 8, W) * row_mask(W)[None], axis=1)


def gate_kernel(
    prod_ref, scaled_ref, grad_ref, sum_ref, inv_ref, kg_ref, ko_ref, pick_ref,
    emb_ref, mean_ref, rows_ref, cols_ref, grows_ref, gcols_ref, total,
):
    step = pl.program_id(0)
    row_sums = jnp.zeros((K8, W), F32)
    col_sums = jnp.zeros((C, 8, W), F32)
    for g in range(4):
        rows = slice(g * 16, g * 16 + 16)
        scaled = stack_rows(*halves(scaled_ref[0, :, rows, :].astype(F32))).astype(BF)
        opened = unstack_rows(jnp.dot(kg_ref[...], scaled, preferred_element_type=F32))
        normed = []
        for product in halves(prod_ref[0, :, rows, :].astype(F32)):
            shifted, inverse = product_norm(product)
            normed.append(shifted * inverse)
        projected = unstack_rows(
            jnp.dot(ko_ref[...], stack_rows(*normed).astype(BF), preferred_element_type=F32)
        )
        grads = halves(grad_ref[:, rows, :].astype(F32))
        weighted = []
        for part in range(2):
            first = g * 16 + part * 8
            where = (slice(None), slice(first, first + 8), slice(None))
            gate = jax.nn.sigmoid(opened[part])
            gated = gate * projected[part]

            @pl.when(step == 0)
            def _():
                total[where] = sum_ref[where] + gated

            @pl.when(step > 0)
            def _():
                total[where] += gated

            grad_gate = grads[part] * (1.0 / T) * gated * (1.0 - gate)
            mean_ref[0, first : first + 8, :] = jnp.sum(grad_gate * opened[part], axis=0)
            term = grad_gate * inv_ref[0, first : first + 8, :][None]
            col_sums = col_sums + term
            weighted.append(term)
        row_sums = row_sums + jnp.dot(
            stack_rows(*weighted).astype(BF), pick_ref[g], preferred_element_type=F32
        )
    rows_ref[0] = fold_rows(row_sums)
    cols_ref[0] = jnp.sum(col_sums, axis=1)

    @pl.when(step == 0)
    def _():
        grad_rows = jnp.zeros((K8, W), F32)
        grad_cols = jnp.zeros((C, 8, W), F32)
        for g in range(4):
            top, bottom = halves(grad_ref[:, g * 16 : g * 16 + 16, :].astype(F32))
            grad_cols = grad_cols + top + bottom
            grad_rows = grad_rows + jnp.dot(
                stack_rows(top, bottom).astype(BF), pick_ref[g], preferred_element_type=F32
            )
        grows_ref[...] = fold_rows(grad_rows)
        gcols_ref[...] = jnp.sum(grad_cols, axis=1)

    @pl.when(step == T - 1)
    def _():
        emb_ref[...] = (total[...] * (1.0 / T)).astype(BF)


def run_gate(prod, scaled, grad, pair_sum, inv, kg, ko, pick):
    return pl.pallas_call(
        gate_kernel,
        grid=(T,),
        in_specs=[
            each_spec(C, H, W), each_spec(C, H, W), whole_spec(C, H, W), whole_spec(C, H, W),
            each_spec(H, W), whole_spec(K8, K8), whole_spec(K8, K8), whole_spec(4, 2 * W, W),
        ],
        out_specs=[
            whole_spec(C, H, W), each_spec(H, W), each_spec(C, W), each_spec(C, W),
            whole_spec(C, W), whole_spec(C, W),
        ],
        out_shape=[
            jax.ShapeDtypeStruct((C, H, W), BF),
            jax.ShapeDtypeStruct((T, H, W), F32),
            jax.ShapeDtypeStruct((T, C, W), F32),
            jax.ShapeDtypeStruct((T, C, W), F32),
            jax.ShapeDtypeStruct((C, W), F32),
            jax.ShapeDtypeStruct((C, W), F32),
        ],
        scratch_shapes=[pltpu.VMEM((C, H, W), F32)],
        compiler_params=params(24),
        cost_estimate=pl.CostEstimate(flops=4 * 2**31, bytes_accessed=12 * 2**20, transcendentals=2**21),
        name="gate_and_embed",
    )(prod, scaled, grad, pair_sum, inv, kg, ko, pick)


def square_kernel(left_ref, right_ref, inv_ref, left, right, inv):
    step = pl.program_id(0)
    spread(left_ref, left.at[0])
    spread(right_ref, right.at[0])

    @pl.when(step == 0)
    def _():
        spread(inv_ref, inv)


def run_square(factors, inv):
    spec = lambda first: pl.BlockSpec((128, H, W), lambda s: (0, first + s, 0))
    out = pl.BlockSpec((1, N, N), lambda s: (s, 0, 0))
    return pl.pallas_call(
        square_kernel,
        grid=(2,),
        in_specs=[spec(0), spec(2), pl.BlockSpec((128, H, W), lambda s: (0, 0, 0))],
        out_specs=[out, out, pl.BlockSpec((N, N), lambda s: (0, 0))],
        out_shape=[jax.ShapeDtypeStruct((2, N, N), BF)] * 2 + [jax.ShapeDtypeStruct((N, N), BF)],
        compiler_params=params(28),
        cost_estimate=pl.CostEstimate(flops=2**20, bytes_accessed=20 * 2**20, transcendentals=0),
        name="to_matrices",
    )(factors, factors, inv)


def factor_kernel(
    core_ref, left_ref, right_ref, grad_ref, inv_ref,
    kept_ref, given_ref, cols_ref, rows_ref, grad, mean,
):
    step = pl.program_id(0)
    core = core_ref[0]
    left, right = left_ref.at[0], right_ref.at[0]
    spread(grad_ref, grad)

    @pl.when(step == 0)
    def _():
        mean[...] = jnp.zeros_like(mean)

    def finish(value, rows, factor, kind):
        mean[rows, :] += value * factor[rows, :].astype(F32)
        term = value * inv_ref[rows, :].astype(F32)
        part = jnp.sum(term.reshape(128, 8, N), axis=0)
        lanes = term[:, :W]
        for c in range(1, 8):
            lanes = lanes + term[:, c * W : (c + 1) * W]
        rows_ref[0, kind, rows, :] = lanes
        return part

    blocks = [slice(0, N)]
    total = None
    for rows in blocks:
        value = jnp.dot(grad[rows, :], right[...], preferred_element_type=F32)
        part = finish(value, rows, left, 0)
        total = part if total is None else total + part
    cols_ref[0, 0] = total
    total = None
    for rows in blocks:
        value = lax.dot_general(
            grad[:, rows], left[...], (((0,), (0,)), ((), ())), preferred_element_type=F32
        )
        part = finish(value, rows, right, 1)
        total = part if total is None else total + part
    cols_ref[0, 1] = total

    @pl.when(step == 1)
    def _():
        @pl.loop(0, 16)
        def _(r):
            mine = pl.ds(pl.multiple_of(r * H + core * 32, 32), 32)
            other = pl.ds(pl.multiple_of(r * H + (1 - core) * 32, 32), 32)
            for c in range(8):
                kept_ref[r * 8 + c] = mean[mine, c * W : (c + 1) * W].astype(BF)
                given_ref[r * 8 + c] = mean[other, c * W : (c + 1) * W].astype(BF)


def run_factor(core, left, right, grad, inv):
    matrix = pl.BlockSpec((1, N, N), lambda s: (s, 0, 0))
    return pl.pallas_call(
        factor_kernel,
        grid=(2,),
        in_specs=[
            pl.BlockSpec(memory_space=pltpu.SMEM),
            matrix,
            matrix,
            pl.BlockSpec((128, H, W), lambda s: (0, s, 0)),
            pl.BlockSpec((N, N), lambda s: (0, 0)),
        ],
        out_specs=[
            pl.BlockSpec((128, H // 2, W), lambda s: (0, 0, 0)),
            pl.BlockSpec((128, H // 2, W), lambda s: (0, 0, 0)),
            pl.BlockSpec((1, 2, 8, N), lambda s: (s, 0, 0, 0)),
            pl.BlockSpec((1, 2, N, W), lambda s: (s, 0, 0, 0)),
        ],
        out_shape=[
            jax.ShapeDtypeStruct((128, H // 2, W), BF),
            jax.ShapeDtypeStruct((128, H // 2, W), BF),
            jax.ShapeDtypeStruct((2, 2, 8, N), F32),
            jax.ShapeDtypeStruct((2, 2, N, W), F32),
        ],
        scratch_shapes=[pltpu.VMEM((N, N), BF), pltpu.VMEM((N, N), F32)],
        compiler_params=params(44),
        name="factor_grads",
    )(core.reshape(1), left, right, grad, inv)


def close_kernel(
    recv_ref, mean_ref, inv_ref, scaled_ref, pick_ref, weight_ref, valid_ref, base_ref, out_ref
):
    got = recv_ref[0].astype(F32)
    total = got[0]
    for k in range(1, 16):
        total = total + got[k]
    weight = (total.reshape(H, W) + mean_ref[0]) * inv_ref[0] * (1.0 / C)
    row_sums = jnp.zeros((K8, W), F32)
    col_sums = jnp.zeros((C, 8, W), F32)
    for g in range(4):
        scaled = scaled_ref[0, :, g * 16 : g * 16 + 16, :].astype(F32)
        terms = []
        for part in range(2):
            first = g * 16 + part * 8
            term = scaled[:, part * 8 : part * 8 + 8, :] * weight[first : first + 8, :][None]
            col_sums = col_sums + term
            terms.append(term)
        row_sums = row_sums + jnp.dot(
            stack_rows(*terms).astype(BF), pick_ref[g], preferred_element_type=F32
        )
    for side, sums in enumerate((fold_rows(row_sums), jnp.sum(col_sums, axis=1))):
        value = jnp.dot(weight_ref[side], sums, precision=HIGHEST, preferred_element_type=F32)
        out_ref[side, 0] = (base_ref[side, 0] + value * valid_ref[side, 0]).astype(BF)


def run_close(recv, mean, inv, scaled, pick, weights, valid, base):
    both = lambda *shape: pl.BlockSpec((2, 1, *shape), lambda t: (0, t) + (0,) * len(shape))
    return pl.pallas_call(
        close_kernel,
        grid=(T,),
        in_specs=[
            each_spec(16, 2, H // 2, W), each_spec(H, W), each_spec(H, W), each_spec(C, H, W),
            whole_spec(4, 2 * W, W), whole_spec(2, C, C), both(1, W), both(C, W),
        ],
        out_specs=both(C, W),
        out_shape=jax.ShapeDtypeStruct((2, T, C, W), BF),
        compiler_params=params(16),
        name="close_sums",
    )(recv, mean, inv, scaled, pick, weights, valid, base)


def from_member(value, k):
    return lax.ppermute(value, "col", [(i, i ^ k) for i in range(8)])


def swap_cores(value):
    return from_member(value, 1)


def exchange(value):
    return lax.all_to_all(value, AXES, split_axis=0, concat_axis=0, tiled=True)


def in_order(core, mine, other, axis):
    first = jnp.where(core == 0, mine, other)
    second = jnp.where(core == 0, other, mine)
    return jnp.concatenate([first, second], axis=axis)


def by_member(value, member):
    lead, last = value.shape[:-2], value.shape[-1]
    cut = value.reshape(*lead, 2, 2, 16, last)
    cut = jnp.where(member % 2 == 1, cut[..., ::-1, :, :], cut)
    cut = jnp.where(member // 2 == 1, cut[..., ::-1, :, :, :], cut)
    return cut.reshape(*lead, 64, last)


def expand(weights):
    to = jnp.asarray(np.kron(np.eye(C), np.ones((8, 1))), BF)
    tall = jnp.einsum("ac,ncd->nad", to, weights, preferred_element_type=F32).astype(BF)
    wide = jnp.einsum("nad,bd->nab", tall, to, preferred_element_type=F32)
    index = jnp.arange(K8, dtype=jnp.int32) % 8
    return jnp.where(index[:, None] == index[None, :], wide, 0.0).astype(BF)


def per_device(
    template_pair,
    template_feat,
    block_map,
    block_count,
    residue_mask,
    row_embed,
    col_embed,
    norm_gain,
    left_proj,
    right_proj,
    gate_proj,
    out_proj,
    embed_grad,
):
    row = lax.axis_index("row")
    col = lax.axis_index("col")
    core = col % 2
    me = row * 8 + col
    own = me // 32
    pair_at = me % 32
    blocks = jnp.arange(128, dtype=jnp.int32)
    half = row % 2
    row_block = row // 2

    member = col % 4
    sent_feat = jnp.broadcast_to(template_feat.reshape(1, 4, 16, W), (32, 4, 16, W))
    pool = exchange(sent_feat.reshape(128, 16, W))
    column_ids = lambda m, at: lax.dynamic_index_in_dim(m, at, axis=1, keepdims=False)
    row_ids = column_ids(block_map, row_block)
    member_ids = [column_ids(block_map, col ^ k) for k in range(4)]
    wanted = jnp.concatenate([jnp.concatenate([ids, row_ids]) for ids in member_ids])
    choose = (wanted[:, None] == blocks[None, :]).astype(BF)
    picked = jnp.einsum(
        "eb,bx->ex", choose, pool.reshape(128, 16 * W), preferred_element_type=F32
    ).astype(BF)
    picked = picked.reshape(4, 8, 16, W)
    feats = jnp.concatenate(
        [picked[0]] + [from_member(picked[k], k) for k in range(1, 4)], axis=1
    )
    embeds = by_member(jnp.stack([row_embed, col_embed]), member)

    offsets = jnp.arange(W, dtype=jnp.int32)

    def marks(at):
        kept = lax.dynamic_slice_in_dim(residue_mask, at * W, W, axis=1) == 1
        return kept & (offsets[None, :] < column_ids(block_count, at)[:, None])

    col_valid = marks(col).astype(F32)
    row_valid = (marks(row_block) & (offsets // H == half)[None, :]).astype(F32)
    left_terms = jnp.einsum("fc,tfi->tci", embeds[0], feats[4:], preferred_element_type=F32)
    left_terms = left_terms * row_valid[:, None, :]
    near, far = left_terms[:, :, :H], left_terms[:, :, H:]
    left_twice = near + far
    left_twice = jnp.concatenate([left_twice, left_twice], axis=2)
    right_terms = jnp.einsum("fc,tfj->tcj", embeds[1], feats[:4], preferred_element_type=F32)
    right_terms = right_terms * col_valid[:, None, :]
    gain = norm_gain.astype(F32)
    gain_wide = jnp.broadcast_to(gain[:, None, None], (C, 8, W))
    kl, kr, kg, ko, kb = expand(
        jnp.stack([left_proj.T, right_proj.T, gate_proj.T, out_proj.T, out_proj])
    )
    group = 2 * np.arange(4)[:, None, None] + (np.arange(2 * W) // W)[None, :, None]
    lanes = np.arange(W)[None, None, :] % H // 8 == group
    terms_pick = jnp.asarray(lanes.transpose(0, 2, 1), BF)
    sums_pick = jnp.where((offsets // H == half)[None, None, :], jnp.asarray(lanes, BF), 0)

    terms = (template_pair, left_twice, right_terms, terms_pick, gain_wide)
    sent, inv = run_norm(*terms, kl, kr)
    factors = exchange(sent.reshape(128, ROWS, W))
    scaled, back, pair_sum = run_back(*terms, inv, embed_grad, kg, kb)
    factors, scaled, back, pair_sum = lax.optimization_barrier((factors, scaled, back, pair_sum))
    my_inv = factors[:, 256:]
    inv_all = in_order(core, my_inv, swap_cores(my_inv), 1)
    prod = exchange(run_product(factors)).reshape(T, C, H, W)
    left, right, inv_matrix = run_square(factors, inv_all)
    prod, left, right, inv_matrix = lax.optimization_barrier((prod, left, right, inv_matrix))
    grads = exchange(run_grad(prod, back).reshape(128, 2 * H, W))
    embedding, gate_mean, gate_rows, gate_cols, out_rows, out_cols = run_gate(
        prod, scaled, embed_grad, pair_sum, inv, kg, ko, sums_pick
    )
    grads, embedding, gate_mean, gate_rows, gate_cols, out_rows, out_cols = (
        lax.optimization_barrier(
            (grads, embedding, gate_mean, gate_rows, gate_cols, out_rows, out_cols)
        )
    )
    kept, given, col_sums, row_sums = run_factor(core, left, right, grads, inv_matrix)
    mean_half = (kept.astype(F32) + swap_cores(given).astype(F32)).astype(BF)
    col_sums, row_sums, mean_half = lax.optimization_barrier((col_sums, row_sums, mean_half))
    recv = exchange(mean_half).reshape(T, 16, 2, H // 2, W)

    def center(weights):
        scaled_weights = gain[:, None] * weights.astype(F32)
        return scaled_weights - jnp.mean(scaled_weights, axis=0, keepdims=True)

    embeds = embeds.astype(F32)
    mixed = jnp.einsum(
        "efd,kdc->kefc",
        embeds,
        jnp.stack([center(left_proj), center(right_proj), center(gate_proj)]),
        precision=HIGHEST,
    )
    closing = -embeds / gain[None, None, :]
    opening = embeds * (1.0 / T)
    valid = jnp.stack([row_valid, col_valid])[:, :, None, :]
    base = jnp.einsum(
        "efc,etcp->etfp", mixed[2], jnp.stack([gate_rows, gate_cols]), precision=HIGHEST
    )
    opened = jnp.einsum(
        "efc,ecp->efp", opening, jnp.stack([out_rows, out_cols]), precision=HIGHEST
    )
    base = (base + opened[:, None]) * valid
    owned = jnp.stack([jnp.sum(row_sums, axis=3), jnp.sum(col_sums, axis=2)], axis=2)
    weights = lax.dynamic_slice_in_dim(mixed[:2], 2 * pair_at, 2, axis=3)
    grad_own = jnp.einsum("kefs,sken->fn", weights, owned, precision=HIGHEST)
    own_map = lax.dynamic_index_in_dim(block_map, own, axis=0, keepdims=False)
    own_count = lax.dynamic_index_in_dim(block_count, own, axis=0, keepdims=False)
    own_marks = lax.dynamic_index_in_dim(residue_mask, own, axis=0, keepdims=False)
    own_valid = (offsets[None, :] < own_count[:, None]) & (own_marks.reshape(8, W) == 1)
    grad_own = grad_own.reshape(C, 8, W).transpose(1, 0, 2) * own_valid.astype(F32)[:, None, :]
    grad_own = grad_own.astype(BF)
    targets = jnp.concatenate([jnp.concatenate([own_map, row_ids, ids]) for ids in member_ids])
    place = (targets[None, :] == blocks[:, None]).astype(BF)
    recv, base, grad_own, place = lax.optimization_barrier((recv, base, grad_own, place))

    closed = run_close(recv, gate_mean, inv, scaled, sums_pick, closing, valid, base)
    entries = jnp.concatenate([grad_own, closed.reshape(2 * T, C, W)], axis=0)
    quarters = [entries[:, k * 16 : k * 16 + 16] for k in range(4)]
    entries = jnp.concatenate(
        [quarters[0]] + [from_member(quarters[k], k) for k in range(1, 4)], axis=0
    )
    placed = jnp.einsum(
        "be,ex->bx", place, entries.reshape(64, 16 * W), preferred_element_type=F32
    ).astype(BF)
    result = exchange(placed.reshape(128, 16, W)).reshape(32, 4 * 16, W)
    feat_grad = jnp.sum(result.astype(F32), axis=0)[None]
    return (embedding, feat_grad)


def solution(mesh):
    return jax.shard_map(
        per_device,
        mesh=mesh,
        in_specs=(
            P(None, None, "row", "col"),
            P(("row", "col"), None, None),
            P(),
            P(),
            P(),
            P(),
            P(),
            P(),
            P(),
            P(),
            P(),
            P(),
            P(None, "row", "col"),
        ),
        out_specs=(P(None, "row", "col"), P(("row", "col"), None, None)),
        check_vma=False,
    )
```

```python
import jax
import jax.numpy as jnp
import numpy as np
from jax import lax
from jax.experimental import pallas as pl
from jax.experimental.pallas import tpu as pltpu
from jax.sharding import PartitionSpec as P

EPS = 1e-05
HIGHEST = lax.Precision.HIGHEST
F32 = jnp.float32
BF = jnp.bfloat16
AXES = ("row", "col")

C = 64
T = 4
H = 64
W = 128
N = 1024
K8 = C * 8
ROWS = 288


def params():
    return pltpu.CompilerParams(vmem_limit_bytes=60 * 2**20)


def stack_rows(top, bottom):
    return jnp.concatenate([top.reshape(K8, W), bottom.reshape(K8, W)], axis=1)


def unstack_rows(wide):
    return wide[:, :W].reshape(C, 8, W), wide[:, W:].reshape(C, 8, W)


def join_rows(top, bottom):
    return jnp.concatenate([top, bottom], axis=1)


def halves(value):
    return value[:, :8, :], value[:, 8:, :]


def mean_channels(value):
    return jnp.sum(value, axis=0, keepdims=True) * (1.0 / C)


def whole_spec(*shape):
    return pl.BlockSpec(shape, lambda t: (0,) * len(shape))


def each_spec(*shape):
    return pl.BlockSpec((1, *shape), lambda t: (t,) + (0,) * len(shape))


def row_mask(width):
    lane = lax.broadcasted_iota(jnp.int32, (8, width), 1)
    return (lane % 8 == lax.broadcasted_iota(jnp.int32, (8, width), 0)).astype(F32)


def spread_terms(left_ref, right_ref, right):
    mask = row_mask(W)
    rows = []
    for c in range(C):
        right[c] = jnp.broadcast_to(right_ref[0, c : c + 1, :], (8, W))
        rows.append(jnp.broadcast_to(left_ref[0, c : c + 1, :], (8, W)) * mask)
    value = jnp.concatenate(rows, axis=0)
    high = value.astype(BF)
    return jnp.concatenate([high, (value - high.astype(F32)).astype(BF)], axis=1)


def make_pairs(pair_ref, left, lanes_ref, right, g):
    terms = unstack_rows(jnp.dot(left, lanes_ref[g], preferred_element_type=F32))
    raw = halves(pair_ref[0, :, g * 16 : g * 16 + 16, :].astype(F32))
    return [raw[part] + terms[part] + right[...] for part in range(2)]


def norm_kernel(
    pair_ref, left_ref, right_ref, lanes_ref, gain_ref, kl_ref, kr_ref, pay_ref, inv_ref,
    right, terms, wide,
):
    left = spread_terms(left_ref, right_ref, right)
    for g in range(4):
        terms[g] = jnp.dot(left, lanes_ref[g], preferred_element_type=F32)
    for g in range(4):
        scaleds, invs = [], []
        left_terms = unstack_rows(terms[g])
        raw = halves(pair_ref[0, :, g * 16 : g * 16 + 16, :].astype(F32))
        for part in range(2):
            pair = raw[part] + left_terms[part] + right[...]
            shifted = pair - mean_channels(pair)
            inverse = lax.rsqrt(mean_channels(shifted * shifted) + EPS)
            scaleds.append(shifted * inverse * gain_ref[...])
            invs.append(inverse[0])
        both = jnp.concatenate(invs, axis=0)
        inv_ref[0, g * 16 : g * 16 + 16, :] = both
        wide[:, g * 256 : g * 256 + 256] = stack_rows(*scaleds).astype(BF)
        first = 256 + (g % 2) * 16
        for q in range(g // 2, C // 2, 2):
            pay_ref[0, q, first : first + 16, :] = both.astype(BF)
    for k, weight in enumerate((kl_ref, kr_ref)):
        outs = jnp.dot(weight[...], wide[...], preferred_element_type=F32)
        for g in range(4):
            out = join_rows(*unstack_rows(outs[:, g * 256 : g * 256 + 256])).astype(BF).reshape(C // 2, 2, 16, W)
            for s in range(2):
                first = k * 128 + s * 64 + g * 16
                pay_ref[0, :, first : first + 16, :] = out[:, s]


TERM_SPECS = [
    each_spec(C, H, W),
    each_spec(C, W),
    each_spec(C, W),
    whole_spec(4, 2 * W, 2 * W),
    whole_spec(C, 8, W),
]


def run_norm(pair, left, right, lanes, gain, kl, kr):
    return pl.pallas_call(
        norm_kernel,
        grid=(T,),
        in_specs=[*TERM_SPECS, whole_spec(K8, K8), whole_spec(K8, K8)],
        out_specs=[each_spec(C // 2, ROWS, W), each_spec(H, W)],
        out_shape=[
            pltpu.HBM((T, C // 2, ROWS, W), BF),
            jax.ShapeDtypeStruct((T, H, W), F32),
        ],
        scratch_shapes=[
            pltpu.VMEM((C, 8, W), F32),
            pltpu.VMEM((4, K8, 2 * W), F32),
            pltpu.VMEM((K8, N), BF),
        ],
        compiler_params=params(),
        name="pair_norm",
    )(pair, left, right, lanes, gain, kl, kr)


def spread(blocks_ref, full_ref):
    @pl.loop(0, 16)
    def _(r):
        for c in range(8):
            full_ref[pl.ds(r * H, H), c * W : (c + 1) * W] = blocks_ref[r * 8 + c]


def matrix(blocks_ref):
    rows = [
        jnp.concatenate([blocks_ref[r * 8 + c] for c in range(8)], axis=1) for r in range(16)
    ]
    return jnp.concatenate(rows, axis=0)


def product_kernel(left_ref, right_ref, out_ref):
    out = lax.dot_general(
        matrix(left_ref), matrix(right_ref), (((1,), (1,)), ((), ())), preferred_element_type=F32
    ).astype(BF)
    for r in range(16):
        for c in range(8):
            out_ref[r * 8 + c] = out[r * H : (r + 1) * H, c * W : (c + 1) * W]


def run_product(factors):
    spec = lambda first: pl.BlockSpec((128, H, W), lambda s: (0, first + s, 0))
    return pl.pallas_call(
        product_kernel,
        grid=(2,),
        in_specs=[spec(0), spec(2)],
        out_specs=pl.BlockSpec((128, H, W), lambda s: (0, s, 0)),
        out_shape=pltpu.HBM((128, 2 * H, W), BF),
        compiler_params=params(),
        name="triangle_product",
    )(factors, factors)


def back_kernel(
    pair_ref, left_ref, right_ref, lanes_ref, gain_ref, inv_ref, grad_ref, kg_ref, kb_ref,
    scaled_ref, out_ref, sum_ref, right,
):
    step = pl.program_id(0)
    left = spread_terms(left_ref, right_ref, right)

    @pl.when(step == 0)
    def _():
        sum_ref[...] = jnp.zeros_like(sum_ref)

    for g in range(4):
        rows = slice(g * 16, g * 16 + 16)
        pairs = make_pairs(pair_ref, left, lanes_ref, right, g)
        sum_ref[:, rows, :] += join_rows(*pairs)
        scaleds = []
        for part in range(2):
            first = g * 16 + part * 8
            inverse = inv_ref[0, first : first + 8, :][None]
            scaleds.append((pairs[part] - mean_channels(pairs[part])) * inverse * gain_ref[...])
        scaled_ref[0, :, rows, :] = join_rows(*scaleds).astype(BF)
        opened = unstack_rows(
            jnp.dot(kg_ref[...], stack_rows(*scaleds).astype(BF), preferred_element_type=F32)
        )
        grads = halves(grad_ref[:, rows, :].astype(F32))
        grad_projs = [
            grads[part] * (1.0 / T) * jax.nn.sigmoid(opened[part]) for part in range(2)
        ]
        grad_norms = unstack_rows(
            jnp.dot(kb_ref[...], stack_rows(*grad_projs).astype(BF), preferred_element_type=F32)
        )
        outs = [grad_norm - mean_channels(grad_norm) for grad_norm in grad_norms]
        out_ref[0, :, rows, :] = join_rows(*outs).astype(BF)


def run_back(pair, left, right, lanes, gain, inv, grad, kg, kb):
    return pl.pallas_call(
        back_kernel,
        grid=(T,),
        in_specs=[
            *TERM_SPECS, each_spec(H, W), whole_spec(C, H, W), whole_spec(K8, K8), whole_spec(K8, K8)
        ],
        out_specs=[each_spec(C, H, W), each_spec(C, H, W), whole_spec(C, H, W)],
        out_shape=[
            pltpu.HBM((T, C, H, W), BF),
            pltpu.HBM((T, C, H, W), BF),
            jax.ShapeDtypeStruct((C, H, W), F32),
        ],
        scratch_shapes=[pltpu.VMEM((C, 8, W), F32)],
        compiler_params=params(),
        cost_estimate=pl.CostEstimate(flops=4 * 2**31, bytes_accessed=16 * 2**20, transcendentals=2**21),
        name="back_project",
    )(pair, left, right, lanes, gain, inv, grad, kg, kb)


def product_norm(product):
    shifted = product - mean_channels(product)
    return shifted, lax.rsqrt(mean_channels(shifted * shifted) + EPS)


def grad_kernel(prod_ref, back_ref, out_ref):
    for g in range(4):
        rows = slice(g * 16, g * 16 + 16)
        shifted, inverse = product_norm(prod_ref[0, :, rows, :].astype(F32))
        back = back_ref[0, :, rows, :].astype(F32)
        slope = mean_channels(back * shifted) * inverse * inverse
        out_ref[0, :, rows, :] = ((back - shifted * slope) * inverse).astype(BF)


def run_grad(prod, back):
    return pl.pallas_call(
        grad_kernel,
        grid=(T,),
        in_specs=[each_spec(C, H, W), each_spec(C, H, W)],
        out_specs=each_spec(C, H, W),
        out_shape=pltpu.HBM((T, C, H, W), BF),
        compiler_params=params(),
        cost_estimate=pl.CostEstimate(flops=2**25, bytes_accessed=12 * 2**20, transcendentals=0),
        name="product_grad",
    )(prod, back)


def fold_rows(sums):
    return jnp.sum(sums.reshape(C, 8, W) * row_mask(W)[None], axis=1)


def gate_kernel(
    prod_ref, scaled_ref, grad_ref, sum_ref, inv_ref, kg_ref, ko_ref, pick_ref,
    emb_ref, mean_ref, rows_ref, cols_ref, grows_ref, gcols_ref, total,
):
    step = pl.program_id(0)
    row_sums = jnp.zeros((K8, W), F32)
    col_sums = jnp.zeros((C, 8, W), F32)
    for g in range(4):
        rows = slice(g * 16, g * 16 + 16)
        scaled = stack_rows(*halves(scaled_ref[0, :, rows, :].astype(F32))).astype(BF)
        opened = unstack_rows(jnp.dot(kg_ref[...], scaled, preferred_element_type=F32))
        normed = []
        for product in halves(prod_ref[0, :, rows, :].astype(F32)):
            shifted, inverse = product_norm(product)
            normed.append(shifted * inverse)
        projected = unstack_rows(
            jnp.dot(ko_ref[...], stack_rows(*normed).astype(BF), preferred_element_type=F32)
        )
        grads = halves(grad_ref[:, rows, :].astype(F32))
        weighted = []
        for part in range(2):
            first = g * 16 + part * 8
            where = (slice(None), slice(first, first + 8), slice(None))
            gate = jax.nn.sigmoid(opened[part])
            gated = gate * projected[part]

            @pl.when(step == 0)
            def _():
                total[where] = sum_ref[where] + gated

            @pl.when(step > 0)
            def _():
                total[where] += gated

            grad_gate = grads[part] * (1.0 / T) * gated * (1.0 - gate)
            mean_ref[0, first : first + 8, :] = jnp.sum(grad_gate * opened[part], axis=0)
            term = grad_gate * inv_ref[0, first : first + 8, :][None]
            col_sums = col_sums + term
            weighted.append(term)
        row_sums = row_sums + jnp.dot(
            stack_rows(*weighted).astype(BF), pick_ref[g], preferred_element_type=F32
        )
    rows_ref[0] = fold_rows(row_sums)
    cols_ref[0] = jnp.sum(col_sums, axis=1)

    @pl.when(step == 0)
    def _():
        grad_rows = jnp.zeros((K8, W), F32)
        grad_cols = jnp.zeros((C, 8, W), F32)
        for g in range(4):
            top, bottom = halves(grad_ref[:, g * 16 : g * 16 + 16, :].astype(F32))
            grad_cols = grad_cols + top + bottom
            grad_rows = grad_rows + jnp.dot(
                stack_rows(top, bottom).astype(BF), pick_ref[g], preferred_element_type=F32
            )
        grows_ref[...] = fold_rows(grad_rows)
        gcols_ref[...] = jnp.sum(grad_cols, axis=1)

    @pl.when(step == T - 1)
    def _():
        emb_ref[...] = (total[...] * (1.0 / T)).astype(BF)


def run_gate(prod, scaled, grad, pair_sum, inv, kg, ko, pick):
    return pl.pallas_call(
        gate_kernel,
        grid=(T,),
        in_specs=[
            each_spec(C, H, W), each_spec(C, H, W), whole_spec(C, H, W), whole_spec(C, H, W),
            each_spec(H, W), whole_spec(K8, K8), whole_spec(K8, K8), whole_spec(4, 2 * W, W),
        ],
        out_specs=[
            whole_spec(C, H, W), each_spec(H, W), each_spec(C, W), each_spec(C, W),
            whole_spec(C, W), whole_spec(C, W),
        ],
        out_shape=[
            jax.ShapeDtypeStruct((C, H, W), BF),
            jax.ShapeDtypeStruct((T, H, W), F32),
            jax.ShapeDtypeStruct((T, C, W), F32),
            jax.ShapeDtypeStruct((T, C, W), F32),
            jax.ShapeDtypeStruct((C, W), F32),
            jax.ShapeDtypeStruct((C, W), F32),
        ],
        scratch_shapes=[pltpu.VMEM((C, H, W), F32)],
        compiler_params=params(),
        cost_estimate=pl.CostEstimate(flops=4 * 2**31, bytes_accessed=12 * 2**20, transcendentals=2**21),
        name="gate_and_embed",
    )(prod, scaled, grad, pair_sum, inv, kg, ko, pick)


def square_kernel(left_ref, right_ref, inv_ref, left, right, inv):
    step = pl.program_id(0)
    spread(left_ref, left.at[0])
    spread(right_ref, right.at[0])

    @pl.when(step == 0)
    def _():
        spread(inv_ref, inv)


def run_square(factors, inv):
    spec = lambda first: pl.BlockSpec((128, H, W), lambda s: (0, first + s, 0))
    out = pl.BlockSpec((1, N, N), lambda s: (s, 0, 0))
    return pl.pallas_call(
        square_kernel,
        grid=(2,),
        in_specs=[spec(0), spec(2), pl.BlockSpec((128, H, W), lambda s: (0, 0, 0))],
        out_specs=[out, out, pl.BlockSpec((N, N), lambda s: (0, 0))],
        out_shape=[pltpu.HBM((2, N, N), BF), pltpu.HBM((2, N, N), BF), pltpu.HBM((N, N), BF)],
        compiler_params=params(),
        cost_estimate=pl.CostEstimate(flops=2**20, bytes_accessed=20 * 2**20, transcendentals=0),
        name="to_matrices",
    )(factors, factors, inv)


def factor_kernel(
    core_ref, left_ref, right_ref, grad_ref, inv_ref,
    kept_ref, given_ref, cols_ref, rows_ref, grad, mean,
):
    step = pl.program_id(0)
    core = core_ref[0]
    left, right = left_ref.at[0], right_ref.at[0]
    grad[...] = matrix(grad_ref)

    @pl.when(step == 0)
    def _():
        mean[...] = jnp.zeros_like(mean)

    def finish(value, rows, factor, kind):
        mean[rows, :] += value * factor[rows, :].astype(F32)
        term = value * inv_ref[rows, :].astype(F32)
        part = jnp.sum(term.reshape(128, 8, N), axis=0)
        lanes = term[:, :W]
        for c in range(1, 8):
            lanes = lanes + term[:, c * W : (c + 1) * W]
        rows_ref[0, kind, rows, :] = lanes
        return part

    blocks = [slice(0, N)]
    total = None
    for rows in blocks:
        value = jnp.dot(grad[rows, :], right[...], preferred_element_type=F32)
        part = finish(value, rows, left, 0)
        total = part if total is None else total + part
    cols_ref[0, 0] = total
    total = None
    for rows in blocks:
        value = lax.dot_general(
            grad[:, rows], left[...], (((0,), (0,)), ((), ())), preferred_element_type=F32
        )
        part = finish(value, rows, right, 1)
        total = part if total is None else total + part
    cols_ref[0, 1] = total

    @pl.when(step == 1)
    def _():
        @pl.loop(0, 16)
        def _(r):
            mine = pl.ds(pl.multiple_of(r * H + core * 32, 32), 32)
            other = pl.ds(pl.multiple_of(r * H + (1 - core) * 32, 32), 32)
            for c in range(8):
                kept_ref[r * 8 + c] = mean[mine, c * W : (c + 1) * W].astype(BF)
                given_ref[r * 8 + c] = mean[other, c * W : (c + 1) * W].astype(BF)


def run_factor(core, left, right, grad, inv):
    matrix = pl.BlockSpec((1, N, N), lambda s: (s, 0, 0))
    return pl.pallas_call(
        factor_kernel,
        grid=(2,),
        in_specs=[
            pl.BlockSpec(memory_space=pltpu.SMEM),
            matrix,
            matrix,
            pl.BlockSpec((128, H, W), lambda s: (0, s, 0)),
            pl.BlockSpec((N, N), lambda s: (0, 0)),
        ],
        out_specs=[
            pl.BlockSpec((128, H // 2, W), lambda s: (0, 0, 0)),
            pl.BlockSpec((128, H // 2, W), lambda s: (0, 0, 0)),
            pl.BlockSpec((1, 2, 8, N), lambda s: (s, 0, 0, 0)),
            pl.BlockSpec((1, 2, N, W), lambda s: (s, 0, 0, 0)),
        ],
        out_shape=[
            jax.ShapeDtypeStruct((128, H // 2, W), BF),
            jax.ShapeDtypeStruct((128, H // 2, W), BF),
            jax.ShapeDtypeStruct((2, 2, 8, N), F32),
            jax.ShapeDtypeStruct((2, 2, N, W), F32),
        ],
        scratch_shapes=[pltpu.VMEM((N, N), BF), pltpu.VMEM((N, N), F32)],
        compiler_params=params(),
        name="factor_grads",
    )(core.reshape(1), left, right, grad, inv)


def close_kernel(
    recv_ref, mean_ref, inv_ref, scaled_ref, pick_ref, weight_ref, valid_ref, base_ref, out_ref
):
    got = recv_ref[0].astype(F32)
    total = got[0]
    for k in range(1, 16):
        total = total + got[k]
    weight = (total.reshape(H, W) + mean_ref[0]) * inv_ref[0] * (1.0 / C)
    row_sums = jnp.zeros((K8, W), F32)
    col_sums = jnp.zeros((C, 8, W), F32)
    for g in range(4):
        scaled = scaled_ref[0, :, g * 16 : g * 16 + 16, :].astype(F32)
        terms = []
        for part in range(2):
            first = g * 16 + part * 8
            term = scaled[:, part * 8 : part * 8 + 8, :] * weight[first : first + 8, :][None]
            col_sums = col_sums + term
            terms.append(term)
        row_sums = row_sums + jnp.dot(
            stack_rows(*terms).astype(BF), pick_ref[g], preferred_element_type=F32
        )
    for side, sums in enumerate((fold_rows(row_sums), jnp.sum(col_sums, axis=1))):
        value = jnp.dot(weight_ref[side], sums, precision=HIGHEST, preferred_element_type=F32)
        out_ref[side, 0] = (base_ref[side, 0] + value * valid_ref[side, 0]).astype(BF)


def run_close(recv, mean, inv, scaled, pick, weights, valid, base):
    both = lambda *shape: pl.BlockSpec((2, 1, *shape), lambda t: (0, t) + (0,) * len(shape))
    return pl.pallas_call(
        close_kernel,
        grid=(T,),
        in_specs=[
            each_spec(16, 2, H // 2, W), each_spec(H, W), each_spec(H, W), each_spec(C, H, W),
            whole_spec(4, 2 * W, W), whole_spec(2, C, C), both(1, W), both(C, W),
        ],
        out_specs=both(C, W),
        out_shape=jax.ShapeDtypeStruct((2, T, C, W), BF),
        compiler_params=params(),
        name="close_sums",
    )(recv, mean, inv, scaled, pick, weights, valid, base)


def from_member(value, k):
    return lax.ppermute(value, "col", [(i, i ^ k) for i in range(8)])


def swap_cores(value):
    return from_member(value, 1)


def exchange(value):
    return lax.all_to_all(value, AXES, split_axis=0, concat_axis=0, tiled=True)


def in_order(core, mine, other, axis):
    first = jnp.where(core == 0, mine, other)
    second = jnp.where(core == 0, other, mine)
    return jnp.concatenate([first, second], axis=axis)


def by_member(value, member):
    lead, last = value.shape[:-2], value.shape[-1]
    cut = value.reshape(*lead, 2, 2, 16, last)
    cut = jnp.where(member % 2 == 1, cut[..., ::-1, :, :], cut)
    cut = jnp.where(member // 2 == 1, cut[..., ::-1, :, :, :], cut)
    return cut.reshape(*lead, 64, last)


def expand(weights):
    to = jnp.asarray(np.kron(np.eye(C), np.ones((8, 1))), BF)
    tall = jnp.einsum("ac,ncd->nad", to, weights, preferred_element_type=F32).astype(BF)
    wide = jnp.einsum("nad,bd->nab", tall, to, preferred_element_type=F32)
    index = jnp.arange(K8, dtype=jnp.int32) % 8
    return jnp.where(index[:, None] == index[None, :], wide, 0.0).astype(BF)


def per_device(
    template_pair,
    template_feat,
    block_map,
    block_count,
    residue_mask,
    row_embed,
    col_embed,
    norm_gain,
    left_proj,
    right_proj,
    gate_proj,
    out_proj,
    embed_grad,
):
    row = lax.axis_index("row")
    col = lax.axis_index("col")
    core = col % 2
    me = row * 8 + col
    own = me // 32
    pair_at = me % 32
    blocks = jnp.arange(128, dtype=jnp.int32)
    half = row % 2
    row_block = row // 2

    member = col % 4
    sent_feat = jnp.broadcast_to(template_feat.reshape(1, 4, 16, W), (32, 4, 16, W))
    pool = exchange(sent_feat.reshape(128, 16, W))
    gain = norm_gain.astype(F32)
    gain_wide = jnp.broadcast_to(gain[:, None, None], (C, 8, W))
    pool, gain_wide = lax.optimization_barrier((pool, gain_wide))
    column_ids = lambda m, at: lax.dynamic_index_in_dim(m, at, axis=1, keepdims=False)
    row_ids = column_ids(block_map, row_block)
    member_ids = [column_ids(block_map, col ^ k) for k in range(4)]
    wanted = jnp.concatenate([jnp.concatenate([ids, row_ids]) for ids in member_ids])
    choose = (wanted[:, None] == blocks[None, :]).astype(BF)
    picked = jnp.einsum(
        "eb,bx->ex", choose, pool.reshape(128, 16 * W), preferred_element_type=F32
    ).astype(BF)
    picked = picked.reshape(4, 8, 16, W)
    feats = jnp.concatenate(
        [picked[0]] + [from_member(picked[k], k) for k in range(1, 4)], axis=1
    )
    embeds = by_member(jnp.stack([row_embed, col_embed]), member)

    offsets = jnp.arange(W, dtype=jnp.int32)

    def marks(at):
        kept = lax.dynamic_slice_in_dim(residue_mask, at * W, W, axis=1) == 1
        return kept & (offsets[None, :] < column_ids(block_count, at)[:, None])

    col_valid = marks(col).astype(F32)
    row_valid = (marks(row_block) & (offsets // H == half)[None, :]).astype(F32)
    left_terms = jnp.einsum("fc,tfi->tci", embeds[0], feats[4:], preferred_element_type=F32)
    left_terms = left_terms * row_valid[:, None, :]
    right_terms = jnp.einsum("fc,tfj->tcj", embeds[1], feats[:4], preferred_element_type=F32)
    right_terms = right_terms * col_valid[:, None, :]
    kl, kr, kg, ko, kb = expand(
        jnp.stack([left_proj.T, right_proj.T, gate_proj.T, out_proj.T, out_proj])
    )
    group = 2 * np.arange(4)[:, None, None] + (np.arange(2 * W) // W)[None, :, None]
    lanes = np.arange(W)[None, None, :] % H // 8 == group
    terms_pick = jnp.asarray(np.tile(lanes.transpose(0, 2, 1), (1, 2, 1)), BF)
    sums_pick = jnp.where((offsets // H == half)[None, None, :], jnp.asarray(lanes, BF), 0)

    terms = (template_pair, left_terms, right_terms, terms_pick, gain_wide)
    sent, inv = run_norm(*terms, kl, kr)
    def center(weights):
        scaled_weights = gain[:, None] * weights.astype(F32)
        return scaled_weights - jnp.mean(scaled_weights, axis=0, keepdims=True)

    embeds = embeds.astype(F32)
    mixed = jnp.einsum(
        "efd,kdc->kefc",
        embeds,
        jnp.stack([center(left_proj), center(right_proj), center(gate_proj)]),
        precision=HIGHEST,
    )
    closing = -embeds / gain[None, None, :]
    opening = embeds * (1.0 / T)
    weights = lax.dynamic_slice_in_dim(mixed[:2], 2 * pair_at, 2, axis=3)
    own_map = lax.dynamic_index_in_dim(block_map, own, axis=0, keepdims=False)
    own_count = lax.dynamic_index_in_dim(block_count, own, axis=0, keepdims=False)
    own_marks = lax.dynamic_index_in_dim(residue_mask, own, axis=0, keepdims=False)
    own_valid = (offsets[None, :] < own_count[:, None]) & (own_marks.reshape(8, W) == 1)
    own_valid = own_valid.astype(F32)
    targets = jnp.concatenate(
        [own_map] * 4 + [jnp.concatenate([row_ids, ids]) for ids in member_ids]
    )
    place = (targets[None, :] == blocks[:, None]).astype(BF)
    factors = exchange(sent.reshape(128, ROWS, W))
    scaled, back, pair_sum = run_back(*terms, inv, embed_grad, kg, kb)
    factors, scaled, back, pair_sum, mixed, closing, opening, weights, own_valid, place = (
        lax.optimization_barrier(
            (factors, scaled, back, pair_sum, mixed, closing, opening, weights, own_valid, place)
        )
    )
    my_inv = factors[:, 256:]
    inv_all = in_order(core, my_inv, swap_cores(my_inv), 1)
    prod = exchange(run_product(factors)).reshape(T, C, H, W)
    left, right, inv_matrix = run_square(factors, inv_all)
    prod, left, right, inv_matrix = lax.optimization_barrier((prod, left, right, inv_matrix))
    grads = exchange(run_grad(prod, back).reshape(128, 2 * H, W))
    embedding, gate_mean, gate_rows, gate_cols, out_rows, out_cols = run_gate(
        prod, scaled, embed_grad, pair_sum, inv, kg, ko, sums_pick
    )
    grads, embedding, gate_mean, gate_rows, gate_cols, out_rows, out_cols = (
        lax.optimization_barrier(
            (grads, embedding, gate_mean, gate_rows, gate_cols, out_rows, out_cols)
        )
    )
    kept, given, col_sums, row_sums = run_factor(core, left, right, grads, inv_matrix)
    mean_half = (kept.astype(F32) + swap_cores(given).astype(F32)).astype(BF)
    col_sums, row_sums, mean_half = lax.optimization_barrier((col_sums, row_sums, mean_half))
    recv = exchange(mean_half).reshape(T, 16, 2, H // 2, W)

    valid = jnp.stack([row_valid, col_valid])[:, :, None, :]
    base = jnp.einsum(
        "efc,etcp->etfp", mixed[2], jnp.stack([gate_rows, gate_cols]), precision=HIGHEST
    )
    opened = jnp.einsum(
        "efc,ecp->efp", opening, jnp.stack([out_rows, out_cols]), precision=HIGHEST
    )
    base = (base + opened[:, None]) * valid
    owned = jnp.stack([jnp.sum(row_sums, axis=3), jnp.sum(col_sums, axis=2)], axis=2)
    grad_own = jnp.einsum("kefs,sken->fn", weights, owned, precision=HIGHEST)
    grad_own = grad_own.reshape(C, 8, W).transpose(1, 0, 2) * own_valid[:, None, :]
    grad_own = grad_own.astype(BF)
    def quarters(value):
        cut = [value[:, k * 16 : k * 16 + 16] for k in range(4)]
        return [cut[0]] + [from_member(cut[k], k) for k in range(1, 4)]

    own_parts = quarters(grad_own)
    recv, base, *own_parts = lax.optimization_barrier((recv, base, *own_parts))
    closed = run_close(recv, gate_mean, inv, scaled, sums_pick, closing, valid, base)
    parts = quarters(closed.reshape(2 * T, C, W))
    entries = jnp.concatenate([*own_parts, *parts], axis=0)
    placed = jnp.einsum(
        "be,ex->bx", place, entries.reshape(64, 16 * W), preferred_element_type=F32
    ).astype(BF)
    result = exchange(placed.reshape(128, 16, W)).reshape(32, 4 * 16, W)
    feat_grad = jnp.sum(result.astype(F32), axis=0)[None]
    return (embedding, feat_grad)


def solution(mesh):
    return jax.shard_map(
        per_device,
        mesh=mesh,
        in_specs=(
            P(None, None, "row", "col"),
            P(("row", "col"), None, None),
            P(),
            P(),
            P(),
            P(),
            P(),
            P(),
            P(),
            P(),
            P(),
            P(),
            P(None, "row", "col"),
        ),
        out_specs=(P(None, "row", "col"), P(("row", "col"), None, None)),
        check_vma=False,
    )
```

```python
import jax
import jax.numpy as jnp
import numpy as np
from jax import lax
from jax.experimental import pallas as pl
from jax.experimental.pallas import tpu as pltpu
from jax.sharding import PartitionSpec as P

EPS = 1e-05
HIGHEST = lax.Precision.HIGHEST
F32 = jnp.float32
BF = jnp.bfloat16
AXES = ("row", "col")

C = 64
T = 4
H = 64
W = 128
N = 1024
K8 = C * 8
ROWS = 272


def params(mib=60):
    return pltpu.CompilerParams(vmem_limit_bytes=mib * 2**20)


def stack_rows(top, bottom):
    return jnp.concatenate([top.reshape(K8, W), bottom.reshape(K8, W)], axis=1)


def unstack_rows(wide):
    return wide[:, :W].reshape(C, 8, W), wide[:, W:].reshape(C, 8, W)


def join_rows(top, bottom):
    return jnp.concatenate([top, bottom], axis=1)


def halves(value):
    return value[:, :8, :], value[:, 8:, :]


def mean_channels(value):
    return jnp.sum(value, axis=0, keepdims=True) * (1.0 / C)


def whole_spec(*shape):
    return pl.BlockSpec(shape, lambda t: (0,) * len(shape))


def each_spec(*shape):
    return pl.BlockSpec((1, *shape), lambda t: (t,) + (0,) * len(shape))


def row_mask(width):
    lane = lax.broadcasted_iota(jnp.int32, (8, width), 1)
    return (lane % 8 == lax.broadcasted_iota(jnp.int32, (8, width), 0)).astype(F32)


def spread_terms(left_ref, right_ref, gain_ref, right, gain):
    mask = row_mask(W)
    rows = []
    for c in range(C):
        right[c] = jnp.broadcast_to(right_ref[0, c : c + 1, :], (8, W))
        gain[c] = jnp.broadcast_to(gain_ref[c : c + 1, :], (8, W))
        rows.append(jnp.broadcast_to(left_ref[0, c : c + 1, :], (8, W)) * mask)
    value = jnp.concatenate(rows, axis=0)
    high = value.astype(BF)
    return jnp.concatenate([high, (value - high.astype(F32)).astype(BF)], axis=1)


def make_pairs(pair_ref, left, lanes_ref, right, g):
    terms = unstack_rows(jnp.dot(left, lanes_ref[g], preferred_element_type=F32))
    raw = halves(pair_ref[0, :, g * 16 : g * 16 + 16, :].astype(F32))
    return [raw[part] + terms[part] + right[...] for part in range(2)]


def norm_kernel(
    pair_ref, left_ref, right_ref, lanes_ref, gain_ref, kl_ref, kr_ref, pay_ref, inv_ref,
    right, gain, terms, wide,
):
    left = spread_terms(left_ref, right_ref, gain_ref, right, gain)
    for g in range(4):
        terms[g] = jnp.dot(left, lanes_ref[g], preferred_element_type=F32)
    for g in range(4):
        scaleds, invs = [], []
        left_terms = unstack_rows(terms[g])
        raw = halves(pair_ref[0, :, g * 16 : g * 16 + 16, :].astype(F32))
        for part in range(2):
            pair = raw[part] + left_terms[part] + right[...]
            shifted = pair - mean_channels(pair)
            inverse = lax.rsqrt(mean_channels(shifted * shifted) + EPS)
            scaleds.append(shifted * inverse * gain[...])
            invs.append(inverse[0])
        both = jnp.concatenate(invs, axis=0)
        inv_ref[0, g * 16 : g * 16 + 16, :] = both
        wide[:, g * 256 : g * 256 + 256] = stack_rows(*scaleds).astype(BF)
        for q in range(g, C // 2, 4):
            pay_ref[0, q, 256:272, :] = both.astype(BF)
    for k, weight in enumerate((kl_ref, kr_ref)):
        outs = jnp.dot(weight[...], wide[...], preferred_element_type=F32)
        for g in range(4):
            out = join_rows(*unstack_rows(outs[:, g * 256 : g * 256 + 256])).astype(BF).reshape(C // 2, 2, 16, W)
            for s in range(2):
                first = k * 128 + s * 64 + g * 16
                pay_ref[0, :, first : first + 16, :] = out[:, s]


TERM_SPECS = [
    each_spec(C, H, W),
    each_spec(C, W),
    each_spec(C, W),
    whole_spec(4, 2 * W, 2 * W),
    whole_spec(C, W),
]


def run_norm(pair, left, right, lanes, gain, kl, kr):
    return pl.pallas_call(
        norm_kernel,
        grid=(T,),
        in_specs=[*TERM_SPECS, whole_spec(K8, K8), whole_spec(K8, K8)],
        out_specs=[each_spec(C // 2, ROWS, W), each_spec(H, W)],
        out_shape=[
            pltpu.HBM((T, C // 2, ROWS, W), BF),
            jax.ShapeDtypeStruct((T, H, W), F32),
        ],
        scratch_shapes=[
            pltpu.VMEM((C, 8, W), F32),
            pltpu.VMEM((C, 8, W), F32),
            pltpu.VMEM((4, K8, 2 * W), F32),
            pltpu.VMEM((K8, N), BF),
        ],
        compiler_params=params(),
        name="pair_norm",
    )(pair, left, right, lanes, gain, kl, kr)


def spread(blocks_ref, full_ref):
    @pl.loop(0, 16)
    def _(r):
        for c in range(8):
            full_ref[pl.ds(r * H, H), c * W : (c + 1) * W] = blocks_ref[r * 8 + c]


def matrix(blocks_ref):
    rows = [
        jnp.concatenate([blocks_ref[r * 8 + c] for c in range(8)], axis=1) for r in range(16)
    ]
    return jnp.concatenate(rows, axis=0)


def product_kernel(left_ref, right_ref, out_ref):
    out = lax.dot_general(
        matrix(left_ref), matrix(right_ref), (((1,), (1,)), ((), ())), preferred_element_type=F32
    ).astype(BF)
    for r in range(16):
        for c in range(8):
            out_ref[r * 8 + c] = out[r * H : (r + 1) * H, c * W : (c + 1) * W]


def run_product(factors):
    spec = lambda first: pl.BlockSpec((128, H, W), lambda s: (0, first + s, 0))
    return pl.pallas_call(
        product_kernel,
        grid=(2,),
        in_specs=[spec(0), spec(2)],
        out_specs=pl.BlockSpec((128, H, W), lambda s: (0, s, 0)),
        out_shape=pltpu.HBM((128, 2 * H, W), BF),
        compiler_params=params(),
        name="triangle_product",
    )(factors, factors)


def back_kernel(
    pair_ref, left_ref, right_ref, lanes_ref, gain_ref, inv_ref, grad_ref, kg_ref, kb_ref,
    scaled_ref, out_ref, sum_ref, right, gain,
):
    step = pl.program_id(0)
    left = spread_terms(left_ref, right_ref, gain_ref, right, gain)

    @pl.when(step == 0)
    def _():
        sum_ref[...] = jnp.zeros_like(sum_ref)

    for g in range(4):
        rows = slice(g * 16, g * 16 + 16)
        pairs = make_pairs(pair_ref, left, lanes_ref, right, g)
        sum_ref[:, rows, :] += join_rows(*pairs)
        scaleds = []
        for part in range(2):
            first = g * 16 + part * 8
            inverse = inv_ref[0, first : first + 8, :][None]
            scaleds.append((pairs[part] - mean_channels(pairs[part])) * inverse * gain[...])
        scaled_ref[0, :, rows, :] = join_rows(*scaleds).astype(BF)
        opened = unstack_rows(
            jnp.dot(kg_ref[...], stack_rows(*scaleds).astype(BF), preferred_element_type=F32)
        )
        grads = halves(grad_ref[:, rows, :].astype(F32))
        grad_projs = [
            grads[part] * (1.0 / T) * jax.nn.sigmoid(opened[part]) for part in range(2)
        ]
        grad_norms = unstack_rows(
            jnp.dot(kb_ref[...], stack_rows(*grad_projs).astype(BF), preferred_element_type=F32)
        )
        outs = [grad_norm - mean_channels(grad_norm) for grad_norm in grad_norms]
        out_ref[0, :, rows, :] = join_rows(*outs).astype(BF)


def run_back(pair, left, right, lanes, gain, inv, grad, kg, kb):
    return pl.pallas_call(
        back_kernel,
        grid=(T,),
        in_specs=[
            *TERM_SPECS, each_spec(H, W), whole_spec(C, H, W), whole_spec(K8, K8), whole_spec(K8, K8)
        ],
        out_specs=[each_spec(C, H, W), each_spec(C, H, W), whole_spec(C, H, W)],
        out_shape=[
            pltpu.HBM((T, C, H, W), BF),
            pltpu.HBM((T, C, H, W), BF),
            jax.ShapeDtypeStruct((C, H, W), F32),
        ],
        scratch_shapes=[pltpu.VMEM((C, 8, W), F32), pltpu.VMEM((C, 8, W), F32)],
        compiler_params=params(),
        cost_estimate=pl.CostEstimate(flops=4 * 2**31, bytes_accessed=16 * 2**20, transcendentals=2**21),
        name="back_project",
    )(pair, left, right, lanes, gain, inv, grad, kg, kb)


def product_norm(product):
    shifted = product - mean_channels(product)
    return shifted, lax.rsqrt(mean_channels(shifted * shifted) + EPS)


def grad_kernel(prod_ref, back_ref, out_ref):
    for g in range(4):
        rows = slice(g * 16, g * 16 + 16)
        shifted, inverse = product_norm(prod_ref[0, :, rows, :].astype(F32))
        back = back_ref[0, :, rows, :].astype(F32)
        slope = mean_channels(back * shifted) * inverse * inverse
        out_ref[0, :, rows, :] = ((back - shifted * slope) * inverse).astype(BF)


def run_grad(prod, back):
    return pl.pallas_call(
        grad_kernel,
        grid=(T,),
        in_specs=[each_spec(C, H, W), each_spec(C, H, W)],
        out_specs=each_spec(C, H, W),
        out_shape=pltpu.HBM((T, C, H, W), BF),
        compiler_params=params(),
        cost_estimate=pl.CostEstimate(flops=2**25, bytes_accessed=12 * 2**20, transcendentals=0),
        name="product_grad",
    )(prod, back)


def fold_rows(sums):
    return jnp.sum(sums.reshape(C, 8, W) * row_mask(W)[None], axis=1)


def gate_kernel(
    prod_ref, scaled_ref, grad_ref, sum_ref, inv_ref, kg_ref, ko_ref, pick_ref,
    emb_ref, mean_ref, rows_ref, cols_ref, grows_ref, gcols_ref, total,
):
    step = pl.program_id(0)
    row_sums = jnp.zeros((K8, W), F32)
    col_sums = jnp.zeros((C, 8, W), F32)
    for g in range(4):
        rows = slice(g * 16, g * 16 + 16)
        scaled = stack_rows(*halves(scaled_ref[0, :, rows, :].astype(F32))).astype(BF)
        opened = unstack_rows(jnp.dot(kg_ref[...], scaled, preferred_element_type=F32))
        normed = []
        for product in halves(prod_ref[0, :, rows, :].astype(F32)):
            shifted, inverse = product_norm(product)
            normed.append(shifted * inverse)
        projected = unstack_rows(
            jnp.dot(ko_ref[...], stack_rows(*normed).astype(BF), preferred_element_type=F32)
        )
        grads = halves(grad_ref[:, rows, :].astype(F32))
        weighted = []
        for part in range(2):
            first = g * 16 + part * 8
            where = (slice(None), slice(first, first + 8), slice(None))
            gate = jax.nn.sigmoid(opened[part])
            gated = gate * projected[part]

            @pl.when(step == 0)
            def _():
                total[where] = sum_ref[where] + gated

            @pl.when(step > 0)
            def _():
                total[where] += gated

            grad_gate = grads[part] * (1.0 / T) * gated * (1.0 - gate)
            mean_ref[0, first : first + 8, :] = jnp.sum(grad_gate * opened[part], axis=0)
            term = grad_gate * inv_ref[0, first : first + 8, :][None]
            col_sums = col_sums + term
            weighted.append(term)
        row_sums = row_sums + jnp.dot(
            stack_rows(*weighted).astype(BF), pick_ref[g], preferred_element_type=F32
        )
    rows_ref[0] = fold_rows(row_sums)
    cols_ref[0] = jnp.sum(col_sums, axis=1)

    @pl.when(step == 0)
    def _():
        grad_rows = jnp.zeros((K8, W), F32)
        grad_cols = jnp.zeros((C, 8, W), F32)
        for g in range(4):
            top, bottom = halves(grad_ref[:, g * 16 : g * 16 + 16, :].astype(F32))
            grad_cols = grad_cols + top + bottom
            grad_rows = grad_rows + jnp.dot(
                stack_rows(top, bottom).astype(BF), pick_ref[g], preferred_element_type=F32
            )
        grows_ref[...] = fold_rows(grad_rows)
        gcols_ref[...] = jnp.sum(grad_cols, axis=1)

    @pl.when(step == T - 1)
    def _():
        emb_ref[...] = (total[...] * (1.0 / T)).astype(BF)


def run_gate(prod, scaled, grad, pair_sum, inv, kg, ko, pick):
    return pl.pallas_call(
        gate_kernel,
        grid=(T,),
        in_specs=[
            each_spec(C, H, W), each_spec(C, H, W), whole_spec(C, H, W), whole_spec(C, H, W),
            each_spec(H, W), whole_spec(K8, K8), whole_spec(K8, K8), whole_spec(4, 2 * W, W),
        ],
        out_specs=[
            whole_spec(C, H, W), each_spec(H, W), each_spec(C, W), each_spec(C, W),
            whole_spec(C, W), whole_spec(C, W),
        ],
        out_shape=[
            jax.ShapeDtypeStruct((C, H, W), BF),
            jax.ShapeDtypeStruct((T, H, W), F32),
            jax.ShapeDtypeStruct((T, C, W), F32),
            jax.ShapeDtypeStruct((T, C, W), F32),
            jax.ShapeDtypeStruct((C, W), F32),
            jax.ShapeDtypeStruct((C, W), F32),
        ],
        scratch_shapes=[pltpu.VMEM((C, H, W), F32)],
        compiler_params=params(),
        cost_estimate=pl.CostEstimate(flops=4 * 2**31, bytes_accessed=12 * 2**20, transcendentals=2**21),
        name="gate_and_embed",
    )(prod, scaled, grad, pair_sum, inv, kg, ko, pick)


def square_kernel(left_ref, right_ref, inv_ref, left, right, inv):
    step = pl.program_id(0)
    spread(left_ref, left.at[0])
    spread(right_ref, right.at[0])

    @pl.when(step == 0)
    def _():
        spread(inv_ref, inv)


def run_square(factors, inv):
    spec = lambda first: pl.BlockSpec((128, H, W), lambda s: (0, first + s, 0))
    out = pl.BlockSpec((1, N, N), lambda s: (s, 0, 0))
    return pl.pallas_call(
        square_kernel,
        grid=(2,),
        in_specs=[spec(0), spec(2), pl.BlockSpec((128, H, W), lambda s: (0, 0, 0))],
        out_specs=[out, out, pl.BlockSpec((N, N), lambda s: (0, 0))],
        out_shape=[pltpu.HBM((2, N, N), BF), pltpu.HBM((2, N, N), BF), pltpu.HBM((N, N), BF)],
        compiler_params=params(),
        cost_estimate=pl.CostEstimate(flops=2**20, bytes_accessed=20 * 2**20, transcendentals=0),
        name="to_matrices",
    )(factors, factors, inv)


def factor_kernel(
    core_ref, left_ref, right_ref, grad_ref, inv_ref,
    kept_ref, given_ref, cols_ref, rows_ref, grad, mean,
):
    step = pl.program_id(0)
    core = core_ref[0]
    left, right = left_ref.at[0], right_ref.at[0]
    grad[...] = matrix(grad_ref)

    @pl.when(step == 0)
    def _():
        mean[...] = jnp.zeros_like(mean)

    def finish(value, rows, factor, kind):
        mean[rows, :] += value * factor[rows, :].astype(F32)
        term = value * inv_ref[rows, :].astype(F32)
        part = jnp.sum(term.reshape(128, 8, N), axis=0)
        lanes = term[:, :W]
        for c in range(1, 8):
            lanes = lanes + term[:, c * W : (c + 1) * W]
        rows_ref[0, kind, rows, :] = lanes
        return part

    blocks = [slice(0, N)]
    total = None
    for rows in blocks:
        value = jnp.dot(grad[rows, :], right[...], preferred_element_type=F32)
        part = finish(value, rows, left, 0)
        total = part if total is None else total + part
    cols_ref[0, 0] = total
    total = None
    for rows in blocks:
        value = lax.dot_general(
            grad[:, rows], left[...], (((0,), (0,)), ((), ())), preferred_element_type=F32
        )
        part = finish(value, rows, right, 1)
        total = part if total is None else total + part
    cols_ref[0, 1] = total

    @pl.when(step == 1)
    def _():
        @pl.loop(0, 16)
        def _(r):
            mine = pl.ds(pl.multiple_of(r * H + core * 32, 32), 32)
            other = pl.ds(pl.multiple_of(r * H + (1 - core) * 32, 32), 32)
            for c in range(8):
                kept_ref[r * 8 + c] = mean[mine, c * W : (c + 1) * W].astype(BF)
                given_ref[r * 8 + c] = mean[other, c * W : (c + 1) * W].astype(BF)


def run_factor(core, left, right, grad, inv):
    matrix = pl.BlockSpec((1, N, N), lambda s: (s, 0, 0))
    return pl.pallas_call(
        factor_kernel,
        grid=(2,),
        in_specs=[
            pl.BlockSpec(memory_space=pltpu.SMEM),
            matrix,
            matrix,
            pl.BlockSpec((128, H, W), lambda s: (0, s, 0)),
            pl.BlockSpec((N, N), lambda s: (0, 0)),
        ],
        out_specs=[
            pl.BlockSpec((128, H // 2, W), lambda s: (0, 0, 0)),
            pl.BlockSpec((128, H // 2, W), lambda s: (0, 0, 0)),
            pl.BlockSpec((1, 2, 8, N), lambda s: (s, 0, 0, 0)),
            pl.BlockSpec((1, 2, N, W), lambda s: (s, 0, 0, 0)),
        ],
        out_shape=[
            jax.ShapeDtypeStruct((128, H // 2, W), BF),
            jax.ShapeDtypeStruct((128, H // 2, W), BF),
            jax.ShapeDtypeStruct((2, 2, 8, N), F32),
            jax.ShapeDtypeStruct((2, 2, N, W), F32),
        ],
        scratch_shapes=[pltpu.VMEM((N, N), BF), pltpu.VMEM((N, N), F32)],
        compiler_params=params(),
        name="factor_grads",
    )(core.reshape(1), left, right, grad, inv)


def add_kernel(left_ref, right_ref, out_ref):
    out_ref[...] = (left_ref[...].astype(F32) + right_ref[...].astype(F32)).astype(BF)


def run_add(left, right):
    spec = pl.BlockSpec((64, H // 2, W), lambda i: (i, 0, 0))
    return pl.pallas_call(
        add_kernel,
        grid=(2,),
        in_specs=[spec, spec],
        out_specs=spec,
        out_shape=pltpu.HBM((128, H // 2, W), BF),
        compiler_params=params(40),
        name="add_halves",
    )(left, right)


def close_kernel(
    recv_ref, mean_ref, inv_ref, scaled_ref, pick_ref, weight_ref, valid_ref, base_ref, out_ref
):
    got = recv_ref[0].astype(F32)
    total = got[0]
    for k in range(1, 16):
        total = total + got[k]
    weight = (total.reshape(H, W) + mean_ref[0]) * inv_ref[0] * (1.0 / C)
    row_sums = jnp.zeros((K8, W), F32)
    col_sums = jnp.zeros((C, 8, W), F32)
    for g in range(4):
        scaled = scaled_ref[0, :, g * 16 : g * 16 + 16, :].astype(F32)
        terms = []
        for part in range(2):
            first = g * 16 + part * 8
            term = scaled[:, part * 8 : part * 8 + 8, :] * weight[first : first + 8, :][None]
            col_sums = col_sums + term
            terms.append(term)
        row_sums = row_sums + jnp.dot(
            stack_rows(*terms).astype(BF), pick_ref[g], preferred_element_type=F32
        )
    for side, sums in enumerate((fold_rows(row_sums), jnp.sum(col_sums, axis=1))):
        value = jnp.dot(weight_ref[side], sums, precision=HIGHEST, preferred_element_type=F32)
        out_ref[side, 0] = (base_ref[side, 0] + value * valid_ref[side, 0]).astype(BF)


def run_close(recv, mean, inv, scaled, pick, weights, valid, base):
    both = lambda *shape: pl.BlockSpec((2, 1, *shape), lambda t: (0, t) + (0,) * len(shape))
    return pl.pallas_call(
        close_kernel,
        grid=(T,),
        in_specs=[
            each_spec(16, 2, H // 2, W), each_spec(H, W), each_spec(H, W), each_spec(C, H, W),
            whole_spec(4, 2 * W, W), whole_spec(2, C, C), both(1, W), both(C, W),
        ],
        out_specs=both(C, W),
        out_shape=jax.ShapeDtypeStruct((2, T, C, W), BF),
        compiler_params=params(58),
        name="close_sums",
    )(recv, mean, inv, scaled, pick, weights, valid, base)


def from_member(value, k):
    return lax.ppermute(value, "col", [(i, i ^ k) for i in range(8)])


def swap_cores(value):
    return from_member(value, 1)


def exchange(value):
    return lax.all_to_all(value, AXES, split_axis=0, concat_axis=0, tiled=True)


def in_order(core, mine, other, axis):
    first = jnp.where(core == 0, mine, other)
    second = jnp.where(core == 0, other, mine)
    return jnp.concatenate([first, second], axis=axis)


def by_member(value, member):
    lead, last = value.shape[:-2], value.shape[-1]
    cut = value.reshape(*lead, 2, 2, 16, last)
    cut = jnp.where(member % 2 == 1, cut[..., ::-1, :, :], cut)
    cut = jnp.where(member // 2 == 1, cut[..., ::-1, :, :, :], cut)
    return cut.reshape(*lead, 64, last)


def expand(weights):
    to = jnp.asarray(np.kron(np.eye(C), np.ones((8, 1))), BF)
    tall = jnp.einsum("ac,ncd->nad", to, weights, preferred_element_type=F32).astype(BF)
    wide = jnp.einsum("nad,bd->nab", tall, to, preferred_element_type=F32)
    index = jnp.arange(K8, dtype=jnp.int32) % 8
    return jnp.where(index[:, None] == index[None, :], wide, 0.0).astype(BF)


def per_device(
    template_pair,
    template_feat,
    block_map,
    block_count,
    residue_mask,
    row_embed,
    col_embed,
    norm_gain,
    left_proj,
    right_proj,
    gate_proj,
    out_proj,
    embed_grad,
):
    row = lax.axis_index("row")
    col = lax.axis_index("col")
    core = col % 2
    me = row * 8 + col
    own = me // 32
    pair_at = me % 32
    blocks = jnp.arange(128, dtype=jnp.int32)
    half = row % 2
    row_block = row // 2

    member = col % 4
    sent_feat = jnp.broadcast_to(template_feat.reshape(1, 4, 16, W), (32, 4, 16, W))
    pool = exchange(sent_feat.reshape(128, 16, W))
    gain = norm_gain.astype(F32)
    gain_wide = jnp.broadcast_to(gain[:, None], (C, W))
    column_ids = lambda m, at: lax.dynamic_index_in_dim(m, at, axis=1, keepdims=False)
    row_ids = column_ids(block_map, row_block)
    member_ids = [column_ids(block_map, col ^ k) for k in range(4)]
    wanted = jnp.concatenate([jnp.concatenate([ids, row_ids]) for ids in member_ids])
    choose = (wanted[:, None] == blocks[None, :]).astype(BF)
    picked = jnp.einsum(
        "eb,bx->ex", choose, pool.reshape(128, 16 * W), preferred_element_type=F32
    ).astype(BF)
    picked = picked.reshape(4, 8, 16, W)
    feats = jnp.concatenate(
        [picked[0]] + [from_member(picked[k], k) for k in range(1, 4)], axis=1
    )
    embeds = by_member(jnp.stack([row_embed, col_embed]), member)

    offsets = jnp.arange(W, dtype=jnp.int32)

    def marks(at):
        kept = lax.dynamic_slice_in_dim(residue_mask, at * W, W, axis=1) == 1
        return kept & (offsets[None, :] < column_ids(block_count, at)[:, None])

    col_valid = marks(col).astype(F32)
    row_valid = (marks(row_block) & (offsets // H == half)[None, :]).astype(F32)
    left_terms = jnp.einsum("fc,tfi->tci", embeds[0], feats[4:], preferred_element_type=F32)
    left_terms = left_terms * row_valid[:, None, :]
    right_terms = jnp.einsum("fc,tfj->tcj", embeds[1], feats[:4], preferred_element_type=F32)
    right_terms = right_terms * col_valid[:, None, :]
    kl, kr, kg, ko, kb = expand(
        jnp.stack([left_proj.T, right_proj.T, gate_proj.T, out_proj.T, out_proj])
    )
    group = 2 * np.arange(4)[:, None, None] + (np.arange(2 * W) // W)[None, :, None]
    lanes = np.arange(W)[None, None, :] % H // 8 == group
    terms_pick = jnp.asarray(np.tile(lanes.transpose(0, 2, 1), (1, 2, 1)), BF)
    sums_pick = jnp.where((offsets // H == half)[None, None, :], jnp.asarray(lanes, BF), 0)

    terms = (template_pair, left_terms, right_terms, terms_pick, gain_wide)
    sent, inv = run_norm(*terms, kl, kr)
    def center(weights):
        scaled_weights = gain[:, None] * weights.astype(F32)
        return scaled_weights - jnp.mean(scaled_weights, axis=0, keepdims=True)

    embeds = embeds.astype(F32)
    mixed = jnp.einsum(
        "efd,kdc->kefc",
        embeds,
        jnp.stack([center(left_proj), center(right_proj), center(gate_proj)]),
        precision=HIGHEST,
    )
    closing = -embeds / gain[None, None, :]
    opening = embeds * (1.0 / T)
    weights = lax.dynamic_slice_in_dim(mixed[:2], 2 * pair_at, 2, axis=3)
    own_map = lax.dynamic_index_in_dim(block_map, own, axis=0, keepdims=False)
    own_count = lax.dynamic_index_in_dim(block_count, own, axis=0, keepdims=False)
    own_marks = lax.dynamic_index_in_dim(residue_mask, own, axis=0, keepdims=False)
    own_valid = (offsets[None, :] < own_count[:, None]) & (own_marks.reshape(8, W) == 1)
    own_valid = own_valid.astype(F32)
    targets = jnp.concatenate(
        [own_map] * 4 + [jnp.concatenate([row_ids, ids]) for ids in member_ids]
    )
    place = (targets[None, :] == blocks[:, None]).astype(BF)
    factors = exchange(sent.reshape(128, ROWS, W))
    scaled, back, pair_sum = run_back(*terms, inv, embed_grad, kg, kb)
    factors, scaled, back, pair_sum, mixed, closing, opening, weights, own_valid, place = (
        lax.optimization_barrier(
            (factors, scaled, back, pair_sum, mixed, closing, opening, weights, own_valid, place)
        )
    )
    inv_part = factors[:, None, 256:]
    inv_part = in_order(member // 2, inv_part, from_member(inv_part, 2), 1)[:, :, None]
    inv_all = in_order(core, inv_part, swap_cores(inv_part), 2).reshape(128, H, W)
    prod = exchange(run_product(factors)).reshape(T, C, H, W)
    left, right, inv_matrix = run_square(factors, inv_all)
    prod, left, right, inv_matrix = lax.optimization_barrier((prod, left, right, inv_matrix))
    grads = exchange(run_grad(prod, back).reshape(128, 2 * H, W))
    embedding, gate_mean, gate_rows, gate_cols, out_rows, out_cols = run_gate(
        prod, scaled, embed_grad, pair_sum, inv, kg, ko, sums_pick
    )
    grads, embedding, gate_mean, gate_rows, gate_cols, out_rows, out_cols = (
        lax.optimization_barrier(
            (grads, embedding, gate_mean, gate_rows, gate_cols, out_rows, out_cols)
        )
    )
    kept, given, col_sums, row_sums = run_factor(core, left, right, grads, inv_matrix)
    mean_half = run_add(kept, swap_cores(given))
    col_sums, row_sums, mean_half = lax.optimization_barrier((col_sums, row_sums, mean_half))
    recv = exchange(mean_half).reshape(T, 16, 2, H // 2, W)

    valid = jnp.stack([row_valid, col_valid])[:, :, None, :]
    base = jnp.einsum(
        "efc,etcp->etfp", mixed[2], jnp.stack([gate_rows, gate_cols]), precision=HIGHEST
    )
    opened = jnp.einsum(
        "efc,ecp->efp", opening, jnp.stack([out_rows, out_cols]), precision=HIGHEST
    )
    base = (base + opened[:, None]) * valid
    owned = jnp.stack([jnp.sum(row_sums, axis=3), jnp.sum(col_sums, axis=2)], axis=2)
    grad_own = jnp.einsum("kefs,sken->fn", weights, owned, precision=HIGHEST)
    grad_own = grad_own.reshape(C, 8, W).transpose(1, 0, 2) * own_valid[:, None, :]
    grad_own = grad_own.astype(BF)
    def quarters(value):
        cut = [value[:, k * 16 : k * 16 + 16] for k in range(4)]
        return [cut[0]] + [from_member(cut[k], k) for k in range(1, 4)]

    own_parts = quarters(grad_own)
    recv, base, *own_parts = lax.optimization_barrier((recv, base, *own_parts))
    closed = run_close(recv, gate_mean, inv, scaled, sums_pick, closing, valid, base)
    parts = quarters(closed.reshape(2 * T, C, W))
    entries = jnp.concatenate([*own_parts, *parts], axis=0)
    placed = jnp.einsum(
        "be,ex->bx", place, entries.reshape(64, 16 * W), preferred_element_type=F32
    ).astype(BF)
    result = exchange(placed.reshape(128, 16, W)).reshape(32, 4 * 16, W)
    feat_grad = jnp.sum(result.astype(F32), axis=0)[None]
    return (embedding, feat_grad)


def solution(mesh):
    return jax.shard_map(
        per_device,
        mesh=mesh,
        in_specs=(
            P(None, None, "row", "col"),
            P(("row", "col"), None, None),
            P(),
            P(),
            P(),
            P(),
            P(),
            P(),
            P(),
            P(),
            P(),
            P(),
            P(None, "row", "col"),
        ),
        out_specs=(P(None, "row", "col"), P(("row", "col"), None, None)),
        check_vma=False,
    )
```

```python
import jax
import jax.numpy as jnp
import numpy as np
from jax import lax
from jax.experimental import pallas as pl
from jax.experimental.pallas import tpu as pltpu
from jax.sharding import PartitionSpec as P

EPS = 1e-05
HIGHEST = lax.Precision.HIGHEST
F32 = jnp.float32
BF = jnp.bfloat16
AXES = ("row", "col")

C = 64
T = 4
H = 64
W = 128
N = 1024
K8 = C * 8
ROWS = 272


def params(mib=60):
    return pltpu.CompilerParams(vmem_limit_bytes=mib * 2**20)


def stack_rows(top, bottom):
    return jnp.concatenate([top.reshape(K8, W), bottom.reshape(K8, W)], axis=1)


def unstack_rows(wide):
    return wide[:, :W].reshape(C, 8, W), wide[:, W:].reshape(C, 8, W)


def join_rows(top, bottom):
    return jnp.concatenate([top, bottom], axis=1)


def halves(value):
    return value[:, :8, :], value[:, 8:, :]


def mean_channels(value):
    return jnp.sum(value, axis=0, keepdims=True) * (1.0 / C)


def whole_spec(*shape):
    return pl.BlockSpec(shape, lambda t: (0,) * len(shape))


def each_spec(*shape):
    return pl.BlockSpec((1, *shape), lambda t: (t,) + (0,) * len(shape))


def row_mask(width):
    lane = lax.broadcasted_iota(jnp.int32, (8, width), 1)
    return (lane % 8 == lax.broadcasted_iota(jnp.int32, (8, width), 0)).astype(F32)


def spread_terms(left_ref, right_ref, gain_ref, right, gain):
    mask = row_mask(W)
    rows = []
    for c in range(C):
        right[c] = jnp.broadcast_to(right_ref[0, c : c + 1, :], (8, W))
        gain[c] = jnp.broadcast_to(gain_ref[c : c + 1, :], (8, W))
        rows.append(jnp.broadcast_to(left_ref[0, c : c + 1, :], (8, W)) * mask)
    value = jnp.concatenate(rows, axis=0)
    high = value.astype(BF)
    return jnp.concatenate([high, (value - high.astype(F32)).astype(BF)], axis=1)


def make_pairs(pair_ref, left, lanes_ref, right, g):
    terms = unstack_rows(jnp.dot(left, lanes_ref[g], preferred_element_type=F32))
    raw = halves(pair_ref[0, :, g * 16 : g * 16 + 16, :].astype(F32))
    return [raw[part] + terms[part] + right[...] for part in range(2)]


def norm_kernel(
    pair_ref, left_ref, right_ref, lanes_ref, gain_ref, kl_ref, kr_ref, pay_ref, inv_ref,
    right, gain, terms, wide,
):
    left = spread_terms(left_ref, right_ref, gain_ref, right, gain)
    for g in range(4):
        terms[g] = jnp.dot(left, lanes_ref[g], preferred_element_type=F32)
    for g in range(4):
        scaleds, invs = [], []
        left_terms = unstack_rows(terms[g])
        raw = halves(pair_ref[0, :, g * 16 : g * 16 + 16, :].astype(F32))
        for part in range(2):
            pair = raw[part] + left_terms[part] + right[...]
            shifted = pair - mean_channels(pair)
            inverse = lax.rsqrt(mean_channels(shifted * shifted) + EPS)
            scaleds.append(shifted * inverse * gain[...])
            invs.append(inverse[0])
        both = jnp.concatenate(invs, axis=0)
        inv_ref[0, g * 16 : g * 16 + 16, :] = both
        wide[:, g * 256 : g * 256 + 256] = stack_rows(*scaleds).astype(BF)
        for q in range(g, C // 2, 4):
            pay_ref[0, q, 256:272, :] = both.astype(BF)
    for k, weight in enumerate((kl_ref, kr_ref)):
        outs = jnp.dot(weight[...], wide[...], preferred_element_type=F32)
        for g in range(4):
            out = join_rows(*unstack_rows(outs[:, g * 256 : g * 256 + 256])).astype(BF).reshape(C // 2, 2, 16, W)
            for s in range(2):
                first = k * 128 + s * 64 + g * 16
                pay_ref[0, :, first : first + 16, :] = out[:, s]


TERM_SPECS = [
    each_spec(C, H, W),
    each_spec(C, W),
    each_spec(C, W),
    whole_spec(4, 2 * W, 2 * W),
    whole_spec(C, W),
]


def run_norm(pair, left, right, lanes, gain, kl, kr):
    return pl.pallas_call(
        norm_kernel,
        grid=(T,),
        in_specs=[*TERM_SPECS, whole_spec(K8, K8), whole_spec(K8, K8)],
        out_specs=[each_spec(C // 2, ROWS, W), each_spec(H, W)],
        out_shape=[
            pltpu.HBM((T, C // 2, ROWS, W), BF),
            jax.ShapeDtypeStruct((T, H, W), F32),
        ],
        scratch_shapes=[
            pltpu.VMEM((C, 8, W), F32),
            pltpu.VMEM((C, 8, W), F32),
            pltpu.VMEM((4, K8, 2 * W), F32),
            pltpu.VMEM((K8, N), BF),
        ],
        compiler_params=params(),
        name="pair_norm",
    )(pair, left, right, lanes, gain, kl, kr)


def spread(blocks_ref, full_ref):
    @pl.loop(0, 16)
    def _(r):
        for c in range(8):
            full_ref[pl.ds(r * H, H), c * W : (c + 1) * W] = blocks_ref[r * 8 + c]


def matrix(blocks_ref):
    rows = [
        jnp.concatenate([blocks_ref[r * 8 + c] for c in range(8)], axis=1) for r in range(16)
    ]
    return jnp.concatenate(rows, axis=0)


def product_kernel(left_ref, right_ref, out_ref):
    out = lax.dot_general(
        matrix(left_ref), matrix(right_ref), (((1,), (1,)), ((), ())), preferred_element_type=F32
    ).astype(BF)
    for r in range(16):
        for c in range(8):
            out_ref[r * 8 + c] = out[r * H : (r + 1) * H, c * W : (c + 1) * W]


def run_product(factors):
    spec = lambda first: pl.BlockSpec((128, H, W), lambda s: (0, first + s, 0))
    return pl.pallas_call(
        product_kernel,
        grid=(2,),
        in_specs=[spec(0), spec(2)],
        out_specs=pl.BlockSpec((128, H, W), lambda s: (0, s, 0)),
        out_shape=pltpu.HBM((128, 2 * H, W), BF),
        compiler_params=params(),
        name="triangle_product",
    )(factors, factors)


def back_kernel(
    pair_ref, left_ref, right_ref, lanes_ref, gain_ref, inv_ref, grad_ref, kg_ref, kb_ref,
    scaled_ref, out_ref, sum_ref, right, gain,
):
    step = pl.program_id(0)
    left = spread_terms(left_ref, right_ref, gain_ref, right, gain)

    @pl.when(step == 0)
    def _():
        sum_ref[...] = jnp.zeros_like(sum_ref)

    for g in range(4):
        rows = slice(g * 16, g * 16 + 16)
        pairs = make_pairs(pair_ref, left, lanes_ref, right, g)
        sum_ref[:, rows, :] += join_rows(*pairs)
        scaleds = []
        for part in range(2):
            first = g * 16 + part * 8
            inverse = inv_ref[0, first : first + 8, :][None]
            scaleds.append((pairs[part] - mean_channels(pairs[part])) * inverse * gain[...])
        scaled_ref[0, :, rows, :] = join_rows(*scaleds).astype(BF)
        opened = unstack_rows(
            jnp.dot(kg_ref[...], stack_rows(*scaleds).astype(BF), preferred_element_type=F32)
        )
        grads = halves(grad_ref[:, rows, :].astype(F32))
        grad_projs = [
            grads[part] * (1.0 / T) * jax.nn.sigmoid(opened[part]) for part in range(2)
        ]
        grad_norms = unstack_rows(
            jnp.dot(kb_ref[...], stack_rows(*grad_projs).astype(BF), preferred_element_type=F32)
        )
        outs = [grad_norm - mean_channels(grad_norm) for grad_norm in grad_norms]
        out_ref[0, :, rows, :] = join_rows(*outs).astype(BF)


def run_back(pair, left, right, lanes, gain, inv, grad, kg, kb):
    return pl.pallas_call(
        back_kernel,
        grid=(T,),
        in_specs=[
            *TERM_SPECS, each_spec(H, W), whole_spec(C, H, W), whole_spec(K8, K8), whole_spec(K8, K8)
        ],
        out_specs=[each_spec(C, H, W), each_spec(C, H, W), whole_spec(C, H, W)],
        out_shape=[
            pltpu.HBM((T, C, H, W), BF),
            pltpu.HBM((T, C, H, W), BF),
            jax.ShapeDtypeStruct((C, H, W), F32),
        ],
        scratch_shapes=[pltpu.VMEM((C, 8, W), F32), pltpu.VMEM((C, 8, W), F32)],
        compiler_params=params(),
        cost_estimate=pl.CostEstimate(flops=4 * 2**31, bytes_accessed=16 * 2**20, transcendentals=2**21),
        name="back_project",
    )(pair, left, right, lanes, gain, inv, grad, kg, kb)


def product_norm(product):
    shifted = product - mean_channels(product)
    return shifted, lax.rsqrt(mean_channels(shifted * shifted) + EPS)


def grad_kernel(prod_ref, back_ref, out_ref):
    for g in range(4):
        rows = slice(g * 16, g * 16 + 16)
        shifted, inverse = product_norm(prod_ref[0, :, rows, :].astype(F32))
        back = back_ref[0, :, rows, :].astype(F32)
        slope = mean_channels(back * shifted) * inverse * inverse
        out_ref[0, :, rows, :] = ((back - shifted * slope) * inverse).astype(BF)


def run_grad(prod, back):
    return pl.pallas_call(
        grad_kernel,
        grid=(T,),
        in_specs=[each_spec(C, H, W), each_spec(C, H, W)],
        out_specs=each_spec(C, H, W),
        out_shape=pltpu.HBM((T, C, H, W), BF),
        compiler_params=params(),
        cost_estimate=pl.CostEstimate(flops=2**25, bytes_accessed=12 * 2**20, transcendentals=0),
        name="product_grad",
    )(prod, back)


def fold_rows(sums):
    return jnp.sum(sums.reshape(C, 8, W) * row_mask(W)[None], axis=1)


def gate_kernel(
    prod_ref, scaled_ref, grad_ref, sum_ref, inv_ref, kg_ref, ko_ref, pick_ref,
    emb_ref, mean_ref, rows_ref, cols_ref, grows_ref, gcols_ref, total,
):
    step = pl.program_id(0)
    row_sums = jnp.zeros((K8, W), F32)
    col_sums = jnp.zeros((C, 8, W), F32)
    for g in range(4):
        rows = slice(g * 16, g * 16 + 16)
        scaled = stack_rows(*halves(scaled_ref[0, :, rows, :].astype(F32))).astype(BF)
        opened = unstack_rows(jnp.dot(kg_ref[...], scaled, preferred_element_type=F32))
        normed = []
        for product in halves(prod_ref[0, :, rows, :].astype(F32)):
            shifted, inverse = product_norm(product)
            normed.append(shifted * inverse)
        projected = unstack_rows(
            jnp.dot(ko_ref[...], stack_rows(*normed).astype(BF), preferred_element_type=F32)
        )
        grads = halves(grad_ref[:, rows, :].astype(F32))
        weighted = []
        for part in range(2):
            first = g * 16 + part * 8
            where = (slice(None), slice(first, first + 8), slice(None))
            gate = jax.nn.sigmoid(opened[part])
            gated = gate * projected[part]

            @pl.when(step == 0)
            def _():
                total[where] = sum_ref[where] + gated

            @pl.when(step > 0)
            def _():
                total[where] += gated

            grad_gate = grads[part] * (1.0 / T) * gated * (1.0 - gate)
            mean_ref[0, first : first + 8, :] = jnp.sum(grad_gate * opened[part], axis=0)
            term = grad_gate * inv_ref[0, first : first + 8, :][None]
            col_sums = col_sums + term
            weighted.append(term)
        row_sums = row_sums + jnp.dot(
            stack_rows(*weighted).astype(BF), pick_ref[g], preferred_element_type=F32
        )
    rows_ref[0] = fold_rows(row_sums)
    cols_ref[0] = jnp.sum(col_sums, axis=1)

    @pl.when(step == 0)
    def _():
        grad_rows = jnp.zeros((K8, W), F32)
        grad_cols = jnp.zeros((C, 8, W), F32)
        for g in range(4):
            top, bottom = halves(grad_ref[:, g * 16 : g * 16 + 16, :].astype(F32))
            grad_cols = grad_cols + top + bottom
            grad_rows = grad_rows + jnp.dot(
                stack_rows(top, bottom).astype(BF), pick_ref[g], preferred_element_type=F32
            )
        grows_ref[...] = fold_rows(grad_rows)
        gcols_ref[...] = jnp.sum(grad_cols, axis=1)

    @pl.when(step == T - 1)
    def _():
        emb_ref[...] = (total[...] * (1.0 / T)).astype(BF)


def run_gate(prod, scaled, grad, pair_sum, inv, kg, ko, pick):
    return pl.pallas_call(
        gate_kernel,
        grid=(T,),
        in_specs=[
            each_spec(C, H, W), each_spec(C, H, W), whole_spec(C, H, W), whole_spec(C, H, W),
            each_spec(H, W), whole_spec(K8, K8), whole_spec(K8, K8), whole_spec(4, 2 * W, W),
        ],
        out_specs=[
            whole_spec(C, H, W), each_spec(H, W), each_spec(C, W), each_spec(C, W),
            whole_spec(C, W), whole_spec(C, W),
        ],
        out_shape=[
            jax.ShapeDtypeStruct((C, H, W), BF),
            jax.ShapeDtypeStruct((T, H, W), F32),
            jax.ShapeDtypeStruct((T, C, W), F32),
            jax.ShapeDtypeStruct((T, C, W), F32),
            jax.ShapeDtypeStruct((C, W), F32),
            jax.ShapeDtypeStruct((C, W), F32),
        ],
        scratch_shapes=[pltpu.VMEM((C, H, W), F32)],
        compiler_params=params(),
        cost_estimate=pl.CostEstimate(flops=4 * 2**31, bytes_accessed=12 * 2**20, transcendentals=2**21),
        name="gate_and_embed",
    )(prod, scaled, grad, pair_sum, inv, kg, ko, pick)


def square_kernel(left_ref, right_ref, left, right):
    spread(left_ref, left.at[0])
    spread(right_ref, right.at[0])


def run_square(factors):
    spec = lambda first: pl.BlockSpec((128, H, W), lambda s: (0, first + s, 0))
    out = pl.BlockSpec((1, N, N), lambda s: (s, 0, 0))
    return pl.pallas_call(
        square_kernel,
        grid=(2,),
        in_specs=[spec(0), spec(2)],
        out_specs=[out, out],
        out_shape=[pltpu.HBM((2, N, N), BF), pltpu.HBM((2, N, N), BF)],
        compiler_params=params(),
        cost_estimate=pl.CostEstimate(flops=2**20, bytes_accessed=16 * 2**20, transcendentals=0),
        name="to_matrices",
    )(factors, factors)


def run_matrix(blocks):
    return pl.pallas_call(
        spread,
        grid=(1,),
        in_specs=[whole_spec(128, H, W)],
        out_specs=whole_spec(N, N),
        out_shape=pltpu.HBM((N, N), BF),
        compiler_params=params(),
        cost_estimate=pl.CostEstimate(flops=2**20, bytes_accessed=4 * 2**20, transcendentals=0),
        name="to_matrix",
    )(blocks)


def factor_kernel(
    core_ref, left_ref, right_ref, grad_ref, inv_ref,
    kept_ref, given_ref, cols_ref, rows_ref, grad, mean,
):
    step = pl.program_id(0)
    core = core_ref[0]
    left, right = left_ref.at[0], right_ref.at[0]
    grad[...] = matrix(grad_ref)

    @pl.when(step == 0)
    def _():
        mean[...] = jnp.zeros_like(mean)

    def finish(value, rows, factor, kind):
        mean[rows, :] += value * factor[rows, :].astype(F32)
        term = value * inv_ref[rows, :].astype(F32)
        part = jnp.sum(term.reshape(128, 8, N), axis=0)
        lanes = term[:, :W]
        for c in range(1, 8):
            lanes = lanes + term[:, c * W : (c + 1) * W]
        rows_ref[0, kind, rows, :] = lanes
        return part

    blocks = [slice(0, N)]
    total = None
    for rows in blocks:
        value = jnp.dot(grad[rows, :], right[...], preferred_element_type=F32)
        part = finish(value, rows, left, 0)
        total = part if total is None else total + part
    cols_ref[0, 0] = total
    total = None
    for rows in blocks:
        value = lax.dot_general(
            grad[:, rows], left[...], (((0,), (0,)), ((), ())), preferred_element_type=F32
        )
        part = finish(value, rows, right, 1)
        total = part if total is None else total + part
    cols_ref[0, 1] = total

    @pl.when(step == 1)
    def _():
        @pl.loop(0, 16)
        def _(r):
            mine = pl.ds(pl.multiple_of(r * H + core * 32, 32), 32)
            other = pl.ds(pl.multiple_of(r * H + (1 - core) * 32, 32), 32)
            for c in range(8):
                kept_ref[r * 8 + c] = mean[mine, c * W : (c + 1) * W].astype(BF)
                given_ref[r * 8 + c] = mean[other, c * W : (c + 1) * W].astype(BF)


def run_factor(core, left, right, grad, inv):
    matrix = pl.BlockSpec((1, N, N), lambda s: (s, 0, 0))
    return pl.pallas_call(
        factor_kernel,
        grid=(2,),
        in_specs=[
            pl.BlockSpec(memory_space=pltpu.SMEM),
            matrix,
            matrix,
            pl.BlockSpec((128, H, W), lambda s: (0, s, 0)),
            pl.BlockSpec((N, N), lambda s: (0, 0)),
        ],
        out_specs=[
            pl.BlockSpec((128, H // 2, W), lambda s: (0, 0, 0)),
            pl.BlockSpec((128, H // 2, W), lambda s: (0, 0, 0)),
            pl.BlockSpec((1, 2, 8, N), lambda s: (s, 0, 0, 0)),
            pl.BlockSpec((1, 2, N, W), lambda s: (s, 0, 0, 0)),
        ],
        out_shape=[
            jax.ShapeDtypeStruct((128, H // 2, W), BF),
            jax.ShapeDtypeStruct((128, H // 2, W), BF),
            jax.ShapeDtypeStruct((2, 2, 8, N), F32),
            jax.ShapeDtypeStruct((2, 2, N, W), F32),
        ],
        scratch_shapes=[pltpu.VMEM((N, N), BF), pltpu.VMEM((N, N), F32)],
        compiler_params=params(),
        name="factor_grads",
    )(core.reshape(1), left, right, grad, inv)


def add_kernel(left_ref, right_ref, out_ref):
    out_ref[...] = (left_ref[...].astype(F32) + right_ref[...].astype(F32)).astype(BF)


def run_add(left, right):
    spec = pl.BlockSpec((64, H // 2, W), lambda i: (i, 0, 0))
    return pl.pallas_call(
        add_kernel,
        grid=(2,),
        in_specs=[spec, spec],
        out_specs=spec,
        out_shape=pltpu.HBM((128, H // 2, W), BF),
        compiler_params=params(40),
        name="add_halves",
    )(left, right)


def close_kernel(
    recv_ref, mean_ref, inv_ref, scaled_ref, pick_ref, weight_ref, valid_ref, base_ref, out_ref
):
    got = recv_ref[0].astype(F32)
    total = got[0]
    for k in range(1, 16):
        total = total + got[k]
    weight = (total.reshape(H, W) + mean_ref[0]) * inv_ref[0] * (1.0 / C)
    row_sums = jnp.zeros((K8, W), F32)
    col_sums = jnp.zeros((C, 8, W), F32)
    for g in range(4):
        scaled = scaled_ref[0, :, g * 16 : g * 16 + 16, :].astype(F32)
        terms = []
        for part in range(2):
            first = g * 16 + part * 8
            term = scaled[:, part * 8 : part * 8 + 8, :] * weight[first : first + 8, :][None]
            col_sums = col_sums + term
            terms.append(term)
        row_sums = row_sums + jnp.dot(
            stack_rows(*terms).astype(BF), pick_ref[g], preferred_element_type=F32
        )
    for side, sums in enumerate((fold_rows(row_sums), jnp.sum(col_sums, axis=1))):
        value = jnp.dot(weight_ref[side], sums, precision=HIGHEST, preferred_element_type=F32)
        out_ref[side, 0] = (base_ref[side, 0] + value * valid_ref[side, 0]).astype(BF)


def run_close(recv, mean, inv, scaled, pick, weights, valid, base):
    both = lambda *shape: pl.BlockSpec((2, 1, *shape), lambda t: (0, t) + (0,) * len(shape))
    return pl.pallas_call(
        close_kernel,
        grid=(T,),
        in_specs=[
            each_spec(16, 2, H // 2, W), each_spec(H, W), each_spec(H, W), each_spec(C, H, W),
            whole_spec(4, 2 * W, W), whole_spec(2, C, C), both(1, W), both(C, W),
        ],
        out_specs=both(C, W),
        out_shape=jax.ShapeDtypeStruct((2, T, C, W), BF),
        compiler_params=params(58),
        name="close_sums",
    )(recv, mean, inv, scaled, pick, weights, valid, base)


def from_member(value, k):
    return lax.ppermute(value, "col", [(i, i ^ k) for i in range(8)])


def swap_cores(value):
    return from_member(value, 1)


def exchange(value):
    return lax.all_to_all(value, AXES, split_axis=0, concat_axis=0, tiled=True)


def in_order(core, mine, other, axis):
    first = jnp.where(core == 0, mine, other)
    second = jnp.where(core == 0, other, mine)
    return jnp.concatenate([first, second], axis=axis)


def by_member(value, member):
    lead, last = value.shape[:-2], value.shape[-1]
    cut = value.reshape(*lead, 2, 2, 16, last)
    cut = jnp.where(member % 2 == 1, cut[..., ::-1, :, :], cut)
    cut = jnp.where(member // 2 == 1, cut[..., ::-1, :, :, :], cut)
    return cut.reshape(*lead, 64, last)


def expand(weights):
    to = jnp.asarray(np.kron(np.eye(C), np.ones((8, 1))), BF)
    tall = jnp.einsum("ac,ncd->nad", to, weights, preferred_element_type=F32).astype(BF)
    wide = jnp.einsum("nad,bd->nab", tall, to, preferred_element_type=F32)
    index = jnp.arange(K8, dtype=jnp.int32) % 8
    return jnp.where(index[:, None] == index[None, :], wide, 0.0).astype(BF)


def per_device(
    template_pair,
    template_feat,
    block_map,
    block_count,
    residue_mask,
    row_embed,
    col_embed,
    norm_gain,
    left_proj,
    right_proj,
    gate_proj,
    out_proj,
    embed_grad,
):
    row = lax.axis_index("row")
    col = lax.axis_index("col")
    core = col % 2
    me = row * 8 + col
    own = me // 32
    pair_at = me % 32
    blocks = jnp.arange(128, dtype=jnp.int32)
    half = row % 2
    row_block = row // 2

    member = col % 4
    sent_feat = jnp.broadcast_to(template_feat.reshape(1, 4, 16, W), (32, 4, 16, W))
    pool = exchange(sent_feat.reshape(128, 16, W))
    gain = norm_gain.astype(F32)
    gain_wide = jnp.broadcast_to(gain[:, None], (C, W))
    column_ids = lambda m, at: lax.dynamic_index_in_dim(m, at, axis=1, keepdims=False)
    row_ids = column_ids(block_map, row_block)
    member_ids = [column_ids(block_map, col ^ k) for k in range(4)]
    wanted = jnp.concatenate([jnp.concatenate([ids, row_ids]) for ids in member_ids])
    choose = (wanted[:, None] == blocks[None, :]).astype(BF)
    picked = jnp.einsum(
        "eb,bx->ex", choose, pool.reshape(128, 16 * W), preferred_element_type=F32
    ).astype(BF)
    picked = picked.reshape(4, 8, 16, W)
    feats = jnp.concatenate(
        [picked[0]] + [from_member(picked[k], k) for k in range(1, 4)], axis=1
    )
    embeds = by_member(jnp.stack([row_embed, col_embed]), member)

    offsets = jnp.arange(W, dtype=jnp.int32)

    def marks(at):
        kept = lax.dynamic_slice_in_dim(residue_mask, at * W, W, axis=1) == 1
        return kept & (offsets[None, :] < column_ids(block_count, at)[:, None])

    col_valid = marks(col).astype(F32)
    row_valid = (marks(row_block) & (offsets // H == half)[None, :]).astype(F32)
    left_terms = jnp.einsum("fc,tfi->tci", embeds[0], feats[4:], preferred_element_type=F32)
    left_terms = left_terms * row_valid[:, None, :]
    right_terms = jnp.einsum("fc,tfj->tcj", embeds[1], feats[:4], preferred_element_type=F32)
    right_terms = right_terms * col_valid[:, None, :]
    kl, kr, kg, ko, kb = expand(
        jnp.stack([left_proj.T, right_proj.T, gate_proj.T, out_proj.T, out_proj])
    )
    group = 2 * np.arange(4)[:, None, None] + (np.arange(2 * W) // W)[None, :, None]
    lanes = np.arange(W)[None, None, :] % H // 8 == group
    terms_pick = jnp.asarray(np.tile(lanes.transpose(0, 2, 1), (1, 2, 1)), BF)
    sums_pick = jnp.where((offsets // H == half)[None, None, :], jnp.asarray(lanes, BF), 0)

    terms = (template_pair, left_terms, right_terms, terms_pick, gain_wide)
    sent, inv = run_norm(*terms, kl, kr)
    def center(weights):
        scaled_weights = gain[:, None] * weights.astype(F32)
        return scaled_weights - jnp.mean(scaled_weights, axis=0, keepdims=True)

    embeds = embeds.astype(F32)
    mixed = jnp.einsum(
        "efd,kdc->kefc",
        embeds,
        jnp.stack([center(left_proj), center(right_proj), center(gate_proj)]),
        precision=HIGHEST,
    )
    closing = -embeds / gain[None, None, :]
    opening = embeds * (1.0 / T)
    weights = lax.dynamic_slice_in_dim(mixed[:2], 2 * pair_at, 2, axis=3)
    own_map = lax.dynamic_index_in_dim(block_map, own, axis=0, keepdims=False)
    own_count = lax.dynamic_index_in_dim(block_count, own, axis=0, keepdims=False)
    own_marks = lax.dynamic_index_in_dim(residue_mask, own, axis=0, keepdims=False)
    own_valid = (offsets[None, :] < own_count[:, None]) & (own_marks.reshape(8, W) == 1)
    own_valid = own_valid.astype(F32)
    targets = jnp.concatenate(
        [own_map] * 4 + [jnp.concatenate([row_ids, ids]) for ids in member_ids]
    )
    place = (targets[None, :] == blocks[:, None]).astype(BF)
    factors = exchange(sent.reshape(128, ROWS, W))
    scaled, back, pair_sum = run_back(*terms, inv, embed_grad, kg, kb)
    factors, scaled, back, pair_sum, mixed, closing, opening, weights, own_valid, place = (
        lax.optimization_barrier(
            (factors, scaled, back, pair_sum, mixed, closing, opening, weights, own_valid, place)
        )
    )
    first, rest = factors[:64, None, 256:], factors[64:, None, 256:]
    first_other = from_member(first, 2)
    product, first_other = lax.optimization_barrier((run_product(factors), first_other))
    prod = exchange(product).reshape(T, C, H, W)
    left, right = run_square(factors)
    prod, left, right, first, rest = lax.optimization_barrier((prod, left, right, first, rest))
    rest_other = from_member(rest, 2)
    grad_prod = run_grad(prod, back)
    grad_prod, first, rest, rest_other = lax.optimization_barrier(
        (grad_prod, first, rest, rest_other)
    )
    grads = exchange(grad_prod.reshape(128, 2 * H, W))
    inv_part = jnp.concatenate(
        [
            in_order(member // 2, first, first_other, 1),
            in_order(member // 2, rest, rest_other, 1),
        ],
        axis=0,
    )[:, :, None]
    inv_all = in_order(core, inv_part, swap_cores(inv_part), 2).reshape(128, H, W)
    inv_matrix = run_matrix(inv_all)
    embedding, gate_mean, gate_rows, gate_cols, out_rows, out_cols = run_gate(
        prod, scaled, embed_grad, pair_sum, inv, kg, ko, sums_pick
    )
    grads, embedding, gate_mean, gate_rows, gate_cols, out_rows, out_cols, inv_matrix = (
        lax.optimization_barrier(
            (grads, embedding, gate_mean, gate_rows, gate_cols, out_rows, out_cols, inv_matrix)
        )
    )
    kept, given, col_sums, row_sums = run_factor(core, left, right, grads, inv_matrix)
    mean_half = run_add(kept, swap_cores(given))
    col_sums, row_sums, mean_half = lax.optimization_barrier((col_sums, row_sums, mean_half))
    recv = exchange(mean_half).reshape(T, 16, 2, H // 2, W)

    valid = jnp.stack([row_valid, col_valid])[:, :, None, :]
    base = jnp.einsum(
        "efc,etcp->etfp", mixed[2], jnp.stack([gate_rows, gate_cols]), precision=HIGHEST
    )
    opened = jnp.einsum(
        "efc,ecp->efp", opening, jnp.stack([out_rows, out_cols]), precision=HIGHEST
    )
    base = (base + opened[:, None]) * valid
    owned = jnp.stack([jnp.sum(row_sums, axis=3), jnp.sum(col_sums, axis=2)], axis=2)
    grad_own = jnp.einsum("kefs,sken->fn", weights, owned, precision=HIGHEST)
    grad_own = grad_own.reshape(C, 8, W).transpose(1, 0, 2) * own_valid[:, None, :]
    grad_own = grad_own.astype(BF)
    def quarters(value):
        cut = [value[:, k * 16 : k * 16 + 16] for k in range(4)]
        return [cut[0]] + [from_member(cut[k], k) for k in range(1, 4)]

    own_parts = quarters(grad_own)
    recv, base, *own_parts = lax.optimization_barrier((recv, base, *own_parts))
    closed = run_close(recv, gate_mean, inv, scaled, sums_pick, closing, valid, base)
    parts = quarters(closed.reshape(2 * T, C, W))
    entries = jnp.concatenate([*own_parts, *parts], axis=0)
    placed = jnp.einsum(
        "be,ex->bx", place, entries.reshape(64, 16 * W), preferred_element_type=F32
    ).astype(BF)
    result = exchange(placed.reshape(128, 16, W)).reshape(32, 4 * 16, W)
    feat_grad = jnp.sum(result.astype(F32), axis=0)[None]
    return (embedding, feat_grad)


def solution(mesh):
    return jax.shard_map(
        per_device,
        mesh=mesh,
        in_specs=(
            P(None, None, "row", "col"),
            P(("row", "col"), None, None),
            P(),
            P(),
            P(),
            P(),
            P(),
            P(),
            P(),
            P(),
            P(),
            P(),
            P(None, "row", "col"),
        ),
        out_specs=(P(None, "row", "col"), P(("row", "col"), None, None)),
        check_vma=False,
    )
```

```python
import jax
import jax.numpy as jnp
import numpy as np
from jax import lax
from jax.experimental import pallas as pl
from jax.experimental.pallas import tpu as pltpu
from jax.sharding import PartitionSpec as P

EPS = 1e-05
HIGHEST = lax.Precision.HIGHEST
F32 = jnp.float32
BF = jnp.bfloat16
AXES = ("row", "col")

C = 64
T = 4
H = 64
W = 128
N = 1024
K8 = C * 8
ROWS = 272


def params(mib=60):
    return pltpu.CompilerParams(vmem_limit_bytes=mib * 2**20)


def stack_rows(top, bottom):
    return jnp.concatenate([top.reshape(K8, W), bottom.reshape(K8, W)], axis=1)


def unstack_rows(wide):
    return wide[:, :W].reshape(C, 8, W), wide[:, W:].reshape(C, 8, W)


def join_rows(top, bottom):
    return jnp.concatenate([top, bottom], axis=1)


def halves(value):
    return value[:, :8, :], value[:, 8:, :]


def mean_channels(value):
    return jnp.sum(value, axis=0, keepdims=True) * (1.0 / C)


def whole_spec(*shape):
    return pl.BlockSpec(shape, lambda t: (0,) * len(shape))


def each_spec(*shape):
    return pl.BlockSpec((1, *shape), lambda t: (t,) + (0,) * len(shape))


def row_mask(width):
    lane = lax.broadcasted_iota(jnp.int32, (8, width), 1)
    return (lane % 8 == lax.broadcasted_iota(jnp.int32, (8, width), 0)).astype(F32)


def spread_terms(feats_row_ref, feats_col_ref, embeds_ref, valid_ref, gain_ref, right, gain, both):
    for side, feats in enumerate((feats_row_ref, feats_col_ref)):
        terms = jnp.dot(embeds_ref[side], feats[0], preferred_element_type=F32)
        both[side] = terms * valid_ref[side, 0]
    mask = row_mask(W)
    rows = []
    for c in range(C):
        right[c] = jnp.broadcast_to(both[1, c : c + 1, :], (8, W))
        gain[c] = jnp.broadcast_to(gain_ref[c : c + 1, :], (8, W))
        rows.append(jnp.broadcast_to(both[0, c : c + 1, :], (8, W)) * mask)
    value = jnp.concatenate(rows, axis=0)
    high = value.astype(BF)
    return jnp.concatenate([high, (value - high.astype(F32)).astype(BF)], axis=1)


def make_pairs(pair_ref, left, lanes_ref, right, g):
    terms = unstack_rows(jnp.dot(left, lanes_ref[g], preferred_element_type=F32))
    raw = halves(pair_ref[0, :, g * 16 : g * 16 + 16, :].astype(F32))
    return [raw[part] + terms[part] + right[...] for part in range(2)]


def norm_kernel(
    pair_ref, feats_row_ref, feats_col_ref, embeds_ref, valid_ref, lanes_ref, gain_ref,
    kl_ref, kr_ref, pay_ref, inv_ref, right, gain, both, terms, wide,
):
    left = spread_terms(
        feats_row_ref, feats_col_ref, embeds_ref, valid_ref, gain_ref, right, gain, both
    )
    for g in range(4):
        terms[g] = jnp.dot(left, lanes_ref[g], preferred_element_type=F32)
    for g in range(4):
        scaleds, invs = [], []
        left_terms = unstack_rows(terms[g])
        raw = halves(pair_ref[0, :, g * 16 : g * 16 + 16, :].astype(F32))
        for part in range(2):
            pair = raw[part] + left_terms[part] + right[...]
            shifted = pair - mean_channels(pair)
            inverse = lax.rsqrt(mean_channels(shifted * shifted) + EPS)
            scaleds.append(shifted * inverse * gain[...])
            invs.append(inverse[0])
        inverses = jnp.concatenate(invs, axis=0)
        inv_ref[0, g * 16 : g * 16 + 16, :] = inverses
        wide[:, g * 256 : g * 256 + 256] = stack_rows(*scaleds).astype(BF)
        for q in range(g, C // 2, 4):
            pay_ref[0, q, 256:272, :] = inverses.astype(BF)
    for k, weight in enumerate((kl_ref, kr_ref)):
        outs = jnp.dot(weight[...], wide[...], preferred_element_type=F32)
        for g in range(4):
            out = join_rows(*unstack_rows(outs[:, g * 256 : g * 256 + 256])).astype(BF).reshape(C // 2, 2, 16, W)
            for s in range(2):
                first = k * 128 + s * 64 + g * 16
                pay_ref[0, :, first : first + 16, :] = out[:, s]


TERM_SPECS = [
    each_spec(C, H, W),
    pl.BlockSpec((1, C, W), lambda t: (t + T, 0, 0)),
    each_spec(C, W),
    whole_spec(2, C, C),
    pl.BlockSpec((2, 1, 1, W), lambda t: (0, t, 0, 0)),
    whole_spec(4, 2 * W, 2 * W),
    whole_spec(C, W),
]


def run_norm(pair, feats, embeds, valid, lanes, gain, kl, kr):
    return pl.pallas_call(
        norm_kernel,
        grid=(T,),
        in_specs=[*TERM_SPECS, whole_spec(K8, K8), whole_spec(K8, K8)],
        out_specs=[each_spec(C // 2, ROWS, W), each_spec(H, W)],
        out_shape=[
            pltpu.HBM((T, C // 2, ROWS, W), BF),
            jax.ShapeDtypeStruct((T, H, W), F32),
        ],
        scratch_shapes=[
            pltpu.VMEM((C, 8, W), F32),
            pltpu.VMEM((C, 8, W), F32),
            pltpu.VMEM((2, C, W), F32),
            pltpu.VMEM((4, K8, 2 * W), F32),
            pltpu.VMEM((K8, N), BF),
        ],
        compiler_params=params(),
        name="pair_norm",
    )(pair, feats, feats, embeds, valid, lanes, gain, kl, kr)


def spread(blocks_ref, full_ref):
    @pl.loop(0, 16)
    def _(r):
        for c in range(8):
            full_ref[pl.ds(r * H, H), c * W : (c + 1) * W] = blocks_ref[r * 8 + c]


def matrix(blocks_ref):
    rows = [
        jnp.concatenate([blocks_ref[r * 8 + c] for c in range(8)], axis=1) for r in range(16)
    ]
    return jnp.concatenate(rows, axis=0)


def product_kernel(left_ref, right_ref, out_ref):
    out = lax.dot_general(
        matrix(left_ref), matrix(right_ref), (((1,), (1,)), ((), ())), preferred_element_type=F32
    ).astype(BF)
    for r in range(16):
        for c in range(8):
            out_ref[r * 8 + c] = out[r * H : (r + 1) * H, c * W : (c + 1) * W]


def run_product(factors):
    spec = lambda first: pl.BlockSpec((128, H, W), lambda s: (0, first + s, 0))
    return pl.pallas_call(
        product_kernel,
        grid=(2,),
        in_specs=[spec(0), spec(2)],
        out_specs=pl.BlockSpec((128, H, W), lambda s: (0, s, 0)),
        out_shape=pltpu.HBM((128, 2 * H, W), BF),
        compiler_params=params(),
        name="triangle_product",
    )(factors, factors)


def back_kernel(
    pair_ref, feats_row_ref, feats_col_ref, embeds_ref, valid_ref, lanes_ref, gain_ref,
    inv_ref, grad_ref, kg_ref, kb_ref, scaled_ref, out_ref, sum_ref, right, gain, both,
):
    step = pl.program_id(0)
    left = spread_terms(
        feats_row_ref, feats_col_ref, embeds_ref, valid_ref, gain_ref, right, gain, both
    )

    @pl.when(step == 0)
    def _():
        sum_ref[...] = jnp.zeros_like(sum_ref)

    for g in range(4):
        rows = slice(g * 16, g * 16 + 16)
        pairs = make_pairs(pair_ref, left, lanes_ref, right, g)
        sum_ref[:, rows, :] += join_rows(*pairs)
        scaleds = []
        for part in range(2):
            first = g * 16 + part * 8
            inverse = inv_ref[0, first : first + 8, :][None]
            scaleds.append((pairs[part] - mean_channels(pairs[part])) * inverse * gain[...])
        scaled_ref[0, :, rows, :] = join_rows(*scaleds).astype(BF)
        opened = unstack_rows(
            jnp.dot(kg_ref[...], stack_rows(*scaleds).astype(BF), preferred_element_type=F32)
        )
        grads = halves(grad_ref[:, rows, :].astype(F32))
        grad_projs = [
            grads[part] * (1.0 / T) * jax.nn.sigmoid(opened[part]) for part in range(2)
        ]
        grad_norms = unstack_rows(
            jnp.dot(kb_ref[...], stack_rows(*grad_projs).astype(BF), preferred_element_type=F32)
        )
        outs = [grad_norm - mean_channels(grad_norm) for grad_norm in grad_norms]
        out_ref[0, :, rows, :] = join_rows(*outs).astype(BF)


def run_back(pair, feats, embeds, valid, lanes, gain, inv, grad, kg, kb):
    return pl.pallas_call(
        back_kernel,
        grid=(T,),
        in_specs=[
            *TERM_SPECS, each_spec(H, W), whole_spec(C, H, W), whole_spec(K8, K8), whole_spec(K8, K8)
        ],
        out_specs=[each_spec(C, H, W), each_spec(C, H, W), whole_spec(C, H, W)],
        out_shape=[
            pltpu.HBM((T, C, H, W), BF),
            pltpu.HBM((T, C, H, W), BF),
            jax.ShapeDtypeStruct((C, H, W), F32),
        ],
        scratch_shapes=[
            pltpu.VMEM((C, 8, W), F32),
            pltpu.VMEM((C, 8, W), F32),
            pltpu.VMEM((2, C, W), F32),
        ],
        compiler_params=params(),
        cost_estimate=pl.CostEstimate(flops=4 * 2**31, bytes_accessed=16 * 2**20, transcendentals=2**21),
        name="back_project",
    )(pair, feats, feats, embeds, valid, lanes, gain, inv, grad, kg, kb)


def product_norm(product):
    shifted = product - mean_channels(product)
    return shifted, lax.rsqrt(mean_channels(shifted * shifted) + EPS)


def grad_kernel(prod_ref, back_ref, out_ref):
    for g in range(4):
        rows = slice(g * 16, g * 16 + 16)
        shifted, inverse = product_norm(prod_ref[0, :, rows, :].astype(F32))
        back = back_ref[0, :, rows, :].astype(F32)
        slope = mean_channels(back * shifted) * inverse * inverse
        out_ref[0, :, rows, :] = ((back - shifted * slope) * inverse).astype(BF)


def run_grad(prod, back):
    return pl.pallas_call(
        grad_kernel,
        grid=(T,),
        in_specs=[each_spec(C, H, W), each_spec(C, H, W)],
        out_specs=each_spec(C, H, W),
        out_shape=pltpu.HBM((T, C, H, W), BF),
        compiler_params=params(),
        cost_estimate=pl.CostEstimate(flops=2**25, bytes_accessed=12 * 2**20, transcendentals=0),
        name="product_grad",
    )(prod, back)


def fold_rows(sums):
    return jnp.sum(sums.reshape(C, 8, W) * row_mask(W)[None], axis=1)


def gate_kernel(
    prod_ref, scaled_ref, grad_ref, sum_ref, inv_ref, kg_ref, ko_ref, pick_ref,
    emb_ref, mean_ref, rows_ref, cols_ref, grows_ref, gcols_ref, total,
):
    step = pl.program_id(0)
    row_sums = jnp.zeros((K8, W), F32)
    col_sums = jnp.zeros((C, 8, W), F32)
    for g in range(4):
        rows = slice(g * 16, g * 16 + 16)
        scaled = stack_rows(*halves(scaled_ref[0, :, rows, :].astype(F32))).astype(BF)
        opened = unstack_rows(jnp.dot(kg_ref[...], scaled, preferred_element_type=F32))
        normed = []
        for product in halves(prod_ref[0, :, rows, :].astype(F32)):
            shifted, inverse = product_norm(product)
            normed.append(shifted * inverse)
        projected = unstack_rows(
            jnp.dot(ko_ref[...], stack_rows(*normed).astype(BF), preferred_element_type=F32)
        )
        grads = halves(grad_ref[:, rows, :].astype(F32))
        weighted = []
        for part in range(2):
            first = g * 16 + part * 8
            where = (slice(None), slice(first, first + 8), slice(None))
            gate = jax.nn.sigmoid(opened[part])
            gated = gate * projected[part]

            @pl.when(step == 0)
            def _():
                total[where] = sum_ref[where] + gated

            @pl.when(step > 0)
            def _():
                total[where] += gated

            grad_gate = grads[part] * (1.0 / T) * gated * (1.0 - gate)
            mean_ref[0, first : first + 8, :] = jnp.sum(grad_gate * opened[part], axis=0)
            term = grad_gate * inv_ref[0, first : first + 8, :][None]
            col_sums = col_sums + term
            weighted.append(term)
        row_sums = row_sums + jnp.dot(
            stack_rows(*weighted).astype(BF), pick_ref[g], preferred_element_type=F32
        )
    rows_ref[0] = fold_rows(row_sums)
    cols_ref[0] = jnp.sum(col_sums, axis=1)

    @pl.when(step == 0)
    def _():
        grad_rows = jnp.zeros((K8, W), F32)
        grad_cols = jnp.zeros((C, 8, W), F32)
        for g in range(4):
            top, bottom = halves(grad_ref[:, g * 16 : g * 16 + 16, :].astype(F32))
            grad_cols = grad_cols + top + bottom
            grad_rows = grad_rows + jnp.dot(
                stack_rows(top, bottom).astype(BF), pick_ref[g], preferred_element_type=F32
            )
        grows_ref[...] = fold_rows(grad_rows)
        gcols_ref[...] = jnp.sum(grad_cols, axis=1)

    @pl.when(step == T - 1)
    def _():
        emb_ref[...] = (total[...] * (1.0 / T)).astype(BF)


def run_gate(prod, scaled, grad, pair_sum, inv, kg, ko, pick):
    return pl.pallas_call(
        gate_kernel,
        grid=(T,),
        in_specs=[
            each_spec(C, H, W), each_spec(C, H, W), whole_spec(C, H, W), whole_spec(C, H, W),
            each_spec(H, W), whole_spec(K8, K8), whole_spec(K8, K8), whole_spec(4, 2 * W, W),
        ],
        out_specs=[
            whole_spec(C, H, W), each_spec(H, W), each_spec(C, W), each_spec(C, W),
            whole_spec(C, W), whole_spec(C, W),
        ],
        out_shape=[
            jax.ShapeDtypeStruct((C, H, W), BF),
            jax.ShapeDtypeStruct((T, H, W), F32),
            jax.ShapeDtypeStruct((T, C, W), F32),
            jax.ShapeDtypeStruct((T, C, W), F32),
            jax.ShapeDtypeStruct((C, W), F32),
            jax.ShapeDtypeStruct((C, W), F32),
        ],
        scratch_shapes=[pltpu.VMEM((C, H, W), F32)],
        compiler_params=params(),
        cost_estimate=pl.CostEstimate(flops=4 * 2**31, bytes_accessed=12 * 2**20, transcendentals=2**21),
        name="gate_and_embed",
    )(prod, scaled, grad, pair_sum, inv, kg, ko, pick)


def square_kernel(left_ref, right_ref, left, right):
    spread(left_ref, left.at[0])
    spread(right_ref, right.at[0])


def run_square(factors):
    spec = lambda first: pl.BlockSpec((128, H, W), lambda s: (0, first + s, 0))
    out = pl.BlockSpec((1, N, N), lambda s: (s, 0, 0))
    return pl.pallas_call(
        square_kernel,
        grid=(2,),
        in_specs=[spec(0), spec(2)],
        out_specs=[out, out],
        out_shape=[pltpu.HBM((2, N, N), BF), pltpu.HBM((2, N, N), BF)],
        compiler_params=params(),
        cost_estimate=pl.CostEstimate(flops=2**20, bytes_accessed=16 * 2**20, transcendentals=0),
        name="to_matrices",
    )(factors, factors)


def run_matrix(blocks):
    return pl.pallas_call(
        spread,
        grid=(1,),
        in_specs=[whole_spec(128, H, W)],
        out_specs=whole_spec(N, N),
        out_shape=pltpu.HBM((N, N), BF),
        compiler_params=params(),
        cost_estimate=pl.CostEstimate(flops=2**20, bytes_accessed=4 * 2**20, transcendentals=0),
        name="to_matrix",
    )(blocks)


def factor_kernel(
    core_ref, left_ref, right_ref, grad_ref, inv_ref,
    kept_ref, given_ref, cols_ref, rows_ref, grad, mean,
):
    step = pl.program_id(0)
    core = core_ref[0]
    left, right = left_ref.at[0], right_ref.at[0]
    grad[...] = matrix(grad_ref)

    @pl.when(step == 0)
    def _():
        mean[...] = jnp.zeros_like(mean)

    def finish(value, rows, factor, kind):
        mean[rows, :] += value * factor[rows, :].astype(F32)
        term = value * inv_ref[rows, :].astype(F32)
        part = jnp.sum(term.reshape(128, 8, N), axis=0)
        lanes = term[:, :W]
        for c in range(1, 8):
            lanes = lanes + term[:, c * W : (c + 1) * W]
        rows_ref[0, kind, rows, :] = lanes
        return part

    blocks = [slice(0, N)]
    total = None
    for rows in blocks:
        value = jnp.dot(grad[rows, :], right[...], preferred_element_type=F32)
        part = finish(value, rows, left, 0)
        total = part if total is None else total + part
    cols_ref[0, 0] = total
    total = None
    for rows in blocks:
        value = lax.dot_general(
            grad[:, rows], left[...], (((0,), (0,)), ((), ())), preferred_element_type=F32
        )
        part = finish(value, rows, right, 1)
        total = part if total is None else total + part
    cols_ref[0, 1] = total

    @pl.when(step == 1)
    def _():
        @pl.loop(0, 16)
        def _(r):
            mine = pl.ds(pl.multiple_of(r * H + core * 32, 32), 32)
            other = pl.ds(pl.multiple_of(r * H + (1 - core) * 32, 32), 32)
            for c in range(8):
                kept_ref[r * 8 + c] = mean[mine, c * W : (c + 1) * W].astype(BF)
                given_ref[r * 8 + c] = mean[other, c * W : (c + 1) * W].astype(BF)


def run_factor(core, left, right, grad, inv):
    matrix = pl.BlockSpec((1, N, N), lambda s: (s, 0, 0))
    return pl.pallas_call(
        factor_kernel,
        grid=(2,),
        in_specs=[
            pl.BlockSpec(memory_space=pltpu.SMEM),
            matrix,
            matrix,
            pl.BlockSpec((128, H, W), lambda s: (0, s, 0)),
            pl.BlockSpec((N, N), lambda s: (0, 0)),
        ],
        out_specs=[
            pl.BlockSpec((128, H // 2, W), lambda s: (0, 0, 0)),
            pl.BlockSpec((128, H // 2, W), lambda s: (0, 0, 0)),
            pl.BlockSpec((1, 2, 8, N), lambda s: (s, 0, 0, 0)),
            pl.BlockSpec((1, 2, N, W), lambda s: (s, 0, 0, 0)),
        ],
        out_shape=[
            jax.ShapeDtypeStruct((128, H // 2, W), BF),
            jax.ShapeDtypeStruct((128, H // 2, W), BF),
            jax.ShapeDtypeStruct((2, 2, 8, N), F32),
            jax.ShapeDtypeStruct((2, 2, N, W), F32),
        ],
        scratch_shapes=[pltpu.VMEM((N, N), BF), pltpu.VMEM((N, N), F32)],
        compiler_params=params(),
        name="factor_grads",
    )(core.reshape(1), left, right, grad, inv)


def add_kernel(left_ref, right_ref, out_ref):
    out_ref[...] = (left_ref[...].astype(F32) + right_ref[...].astype(F32)).astype(BF)


def run_add(left, right):
    spec = pl.BlockSpec((64, H // 2, W), lambda i: (i, 0, 0))
    return pl.pallas_call(
        add_kernel,
        grid=(2,),
        in_specs=[spec, spec],
        out_specs=spec,
        out_shape=pltpu.HBM((128, H // 2, W), BF),
        compiler_params=params(40),
        name="add_halves",
    )(left, right)


def close_kernel(
    recv_ref, mean_ref, inv_ref, scaled_ref, pick_ref, weight_ref, valid_ref, base_ref, *out_refs
):
    got = recv_ref[0].astype(F32)
    total = got[0]
    for k in range(1, 16):
        total = total + got[k]
    weight = (total.reshape(H, W) + mean_ref[0]) * inv_ref[0] * (1.0 / C)
    row_sums = jnp.zeros((K8, W), F32)
    col_sums = jnp.zeros((C, 8, W), F32)
    for g in range(4):
        scaled = scaled_ref[0, :, g * 16 : g * 16 + 16, :].astype(F32)
        terms = []
        for part in range(2):
            first = g * 16 + part * 8
            term = scaled[:, part * 8 : part * 8 + 8, :] * weight[first : first + 8, :][None]
            col_sums = col_sums + term
            terms.append(term)
        row_sums = row_sums + jnp.dot(
            stack_rows(*terms).astype(BF), pick_ref[g], preferred_element_type=F32
        )
    for side, sums in enumerate((fold_rows(row_sums), jnp.sum(col_sums, axis=1))):
        value = jnp.dot(weight_ref[side], sums, precision=HIGHEST, preferred_element_type=F32)
        value = (base_ref[side, 0] + value * valid_ref[side, 0]).astype(BF)
        for k, out_ref in enumerate(out_refs):
            out_ref[side, 0] = value[k * 16 : k * 16 + 16]


def run_close(recv, mean, inv, scaled, pick, weights, valid, base):
    both = lambda *shape: pl.BlockSpec((2, 1, *shape), lambda t: (0, t) + (0,) * len(shape))
    return pl.pallas_call(
        close_kernel,
        grid=(T,),
        in_specs=[
            each_spec(16, 2, H // 2, W), each_spec(H, W), each_spec(H, W), each_spec(C, H, W),
            whole_spec(4, 2 * W, W), whole_spec(2, C, C), both(1, W), both(C, W),
        ],
        out_specs=[both(16, W)] * 4,
        out_shape=[jax.ShapeDtypeStruct((2, T, 16, W), BF)] * 4,
        compiler_params=params(58),
        name="close_sums",
    )(recv, mean, inv, scaled, pick, weights, valid, base)


def from_member(value, k):
    return lax.ppermute(value, "col", [(i, i ^ k) for i in range(8)])


def swap_cores(value):
    return from_member(value, 1)


def exchange(value):
    return lax.all_to_all(value, AXES, split_axis=0, concat_axis=0, tiled=True)


def in_order(core, mine, other, axis):
    first = jnp.where(core == 0, mine, other)
    second = jnp.where(core == 0, other, mine)
    return jnp.concatenate([first, second], axis=axis)


def by_member(value, member):
    lead, last = value.shape[:-2], value.shape[-1]
    cut = value.reshape(*lead, 2, 2, 16, last)
    cut = jnp.where(member % 2 == 1, cut[..., ::-1, :, :], cut)
    cut = jnp.where(member // 2 == 1, cut[..., ::-1, :, :, :], cut)
    return cut.reshape(*lead, 64, last)


def expand(weights):
    to = jnp.asarray(np.kron(np.eye(C), np.ones((8, 1))), BF)
    tall = jnp.einsum("ac,ncd->nad", to, weights, preferred_element_type=F32).astype(BF)
    wide = jnp.einsum("nad,bd->nab", tall, to, preferred_element_type=F32)
    index = jnp.arange(K8, dtype=jnp.int32) % 8
    return jnp.where(index[:, None] == index[None, :], wide, 0.0).astype(BF)


def per_device(
    template_pair,
    template_feat,
    block_map,
    block_count,
    residue_mask,
    row_embed,
    col_embed,
    norm_gain,
    left_proj,
    right_proj,
    gate_proj,
    out_proj,
    embed_grad,
):
    row = lax.axis_index("row")
    col = lax.axis_index("col")
    core = col % 2
    me = row * 8 + col
    own = me // 32
    pair_at = me % 32
    blocks = jnp.arange(128, dtype=jnp.int32)
    half = row % 2
    row_block = row // 2

    member = col % 4
    sent_feat = jnp.broadcast_to(template_feat.reshape(1, 4, 16, W), (32, 4, 16, W))
    pool = exchange(sent_feat.reshape(128, 16, W))
    gain = norm_gain.astype(F32)
    gain_wide = jnp.broadcast_to(gain[:, None], (C, W))
    column_ids = lambda m, at: lax.dynamic_index_in_dim(m, at, axis=1, keepdims=False)
    row_ids = column_ids(block_map, row_block)
    member_ids = [column_ids(block_map, col ^ k) for k in range(4)]
    wanted = jnp.concatenate([jnp.concatenate([ids, row_ids]) for ids in member_ids])
    choose = (wanted[:, None] == blocks[None, :]).astype(BF)
    picked = jnp.einsum(
        "eb,bx->ex", choose, pool.reshape(128, 16 * W), preferred_element_type=F32
    ).astype(BF)
    picked = picked.reshape(4, 8, 16, W)
    feats = jnp.concatenate(
        [picked[0]] + [from_member(picked[k], k) for k in range(1, 4)], axis=1
    )
    embeds = by_member(jnp.stack([row_embed, col_embed]), member)

    offsets = jnp.arange(W, dtype=jnp.int32)

    def marks(at):
        kept = lax.dynamic_slice_in_dim(residue_mask, at * W, W, axis=1) == 1
        return kept & (offsets[None, :] < column_ids(block_count, at)[:, None])

    col_valid = marks(col).astype(F32)
    row_valid = (marks(row_block) & (offsets // H == half)[None, :]).astype(F32)
    valid = jnp.stack([row_valid, col_valid])[:, :, None, :]
    turned = jnp.swapaxes(embeds, 1, 2)
    kl, kr, kg, ko, kb = expand(
        jnp.stack([left_proj.T, right_proj.T, gate_proj.T, out_proj.T, out_proj])
    )
    group = 2 * np.arange(4)[:, None, None] + (np.arange(2 * W) // W)[None, :, None]
    lanes = np.arange(W)[None, None, :] % H // 8 == group
    terms_pick = jnp.asarray(np.tile(lanes.transpose(0, 2, 1), (1, 2, 1)), BF)
    sums_pick = jnp.where((offsets // H == half)[None, None, :], jnp.asarray(lanes, BF), 0)

    terms = (template_pair, feats, turned, valid, terms_pick, gain_wide)
    sent, inv = run_norm(*terms, kl, kr)
    def center(weights):
        scaled_weights = gain[:, None] * weights.astype(F32)
        return scaled_weights - jnp.mean(scaled_weights, axis=0, keepdims=True)

    embeds = embeds.astype(F32)
    mixed = jnp.einsum(
        "efd,kdc->kefc",
        embeds,
        jnp.stack([center(left_proj), center(right_proj), center(gate_proj)]),
        precision=HIGHEST,
    )
    closing = -embeds / gain[None, None, :]
    opening = embeds * (1.0 / T)
    weights = lax.dynamic_slice_in_dim(mixed[:2], 2 * pair_at, 2, axis=3)
    own_map = lax.dynamic_index_in_dim(block_map, own, axis=0, keepdims=False)
    own_count = lax.dynamic_index_in_dim(block_count, own, axis=0, keepdims=False)
    own_marks = lax.dynamic_index_in_dim(residue_mask, own, axis=0, keepdims=False)
    own_valid = (offsets[None, :] < own_count[:, None]) & (own_marks.reshape(8, W) == 1)
    own_valid = own_valid.astype(F32)
    targets = jnp.concatenate(
        [own_map] * 4 + [jnp.concatenate([row_ids, ids]) for ids in member_ids]
    )
    place = (targets[None, :] == blocks[:, None]).astype(BF)
    factors = exchange(sent.reshape(128, ROWS, W))
    scaled, back, pair_sum = run_back(*terms, inv, embed_grad, kg, kb)
    factors, scaled, back, pair_sum, mixed, closing, opening, weights, own_valid, place = (
        lax.optimization_barrier(
            (factors, scaled, back, pair_sum, mixed, closing, opening, weights, own_valid, place)
        )
    )
    first, rest = factors[:64, None, 256:], factors[64:, None, 256:]
    first_other = from_member(first, 2)
    product, first_other = lax.optimization_barrier((run_product(factors), first_other))
    prod = exchange(product).reshape(T, C, H, W)
    left, right = run_square(factors)
    prod, left, right, first, rest = lax.optimization_barrier((prod, left, right, first, rest))
    rest_other = from_member(rest, 2)
    grad_prod = run_grad(prod, back)
    grad_prod, first, rest, rest_other = lax.optimization_barrier(
        (grad_prod, first, rest, rest_other)
    )
    grads = exchange(grad_prod.reshape(128, 2 * H, W))
    inv_part = jnp.concatenate(
        [
            in_order(member // 2, first, first_other, 1),
            in_order(member // 2, rest, rest_other, 1),
        ],
        axis=0,
    )[:, :, None]
    inv_all = in_order(core, inv_part, swap_cores(inv_part), 2).reshape(128, H, W)
    inv_matrix = run_matrix(inv_all)
    embedding, gate_mean, gate_rows, gate_cols, out_rows, out_cols = run_gate(
        prod, scaled, embed_grad, pair_sum, inv, kg, ko, sums_pick
    )
    grads, embedding, gate_mean, gate_rows, gate_cols, out_rows, out_cols, inv_matrix = (
        lax.optimization_barrier(
            (grads, embedding, gate_mean, gate_rows, gate_cols, out_rows, out_cols, inv_matrix)
        )
    )
    kept, given, col_sums, row_sums = run_factor(core, left, right, grads, inv_matrix)
    mean_half = run_add(kept, swap_cores(given))
    col_sums, row_sums, mean_half = lax.optimization_barrier((col_sums, row_sums, mean_half))
    recv = exchange(mean_half).reshape(T, 16, 2, H // 2, W)

    base = jnp.einsum(
        "efc,etcp->etfp", mixed[2], jnp.stack([gate_rows, gate_cols]), precision=HIGHEST
    )
    opened = jnp.einsum(
        "efc,ecp->efp", opening, jnp.stack([out_rows, out_cols]), precision=HIGHEST
    )
    base = (base + opened[:, None]) * valid
    owned = jnp.stack([jnp.sum(row_sums, axis=3), jnp.sum(col_sums, axis=2)], axis=2)
    grad_own = jnp.einsum("kefs,sken->fn", weights, owned, precision=HIGHEST)
    grad_own = grad_own.reshape(C, 8, W).transpose(1, 0, 2) * own_valid[:, None, :]
    grad_own = grad_own.astype(BF)
    def quarters(value):
        cut = [value[:, k * 16 : k * 16 + 16] for k in range(4)]
        return [cut[0]] + [from_member(cut[k], k) for k in range(1, 4)]

    own_parts = quarters(grad_own)
    recv, base, *own_parts = lax.optimization_barrier((recv, base, *own_parts))
    closed = run_close(recv, gate_mean, inv, scaled, sums_pick, closing, valid, base)
    closed = [part.reshape(2 * T, 16, W) for part in closed]
    parts = [closed[0]] + [from_member(closed[k], k) for k in range(1, 4)]
    entries = jnp.concatenate([*own_parts, *parts], axis=0)
    placed = jnp.einsum(
        "be,ex->bx", place, entries.reshape(64, 16 * W), preferred_element_type=F32
    ).astype(BF)
    result = exchange(placed.reshape(128, 16, W)).reshape(32, 4 * 16, W)
    feat_grad = jnp.sum(result.astype(F32), axis=0)[None]
    return (embedding, feat_grad)


def solution(mesh):
    return jax.shard_map(
        per_device,
        mesh=mesh,
        in_specs=(
            P(None, None, "row", "col"),
            P(("row", "col"), None, None),
            P(),
            P(),
            P(),
            P(),
            P(),
            P(),
            P(),
            P(),
            P(),
            P(),
            P(None, "row", "col"),
        ),
        out_specs=(P(None, "row", "col"), P(("row", "col"), None, None)),
        check_vma=False,
    )
```

```python
import jax
import jax.numpy as jnp
import numpy as np
from jax import lax
from jax.experimental import pallas as pl
from jax.experimental.pallas import tpu as pltpu
from jax.sharding import PartitionSpec as P

EPS = 1e-05
HIGHEST = lax.Precision.HIGHEST
F32 = jnp.float32
BF = jnp.bfloat16
AXES = ("row", "col")

C = 64
T = 4
H = 64
W = 128
N = 1024
K8 = C * 8
ROWS = 272


def params(mib=60):
    return pltpu.CompilerParams(vmem_limit_bytes=mib * 2**20)


def stack_rows(top, bottom):
    return jnp.concatenate([top.reshape(K8, W), bottom.reshape(K8, W)], axis=1)


def unstack_rows(wide):
    return wide[:, :W].reshape(C, 8, W), wide[:, W:].reshape(C, 8, W)


def join_rows(top, bottom):
    return jnp.concatenate([top, bottom], axis=1)


def halves(value):
    return value[:, :8, :], value[:, 8:, :]


def mean_channels(value):
    return jnp.sum(value, axis=0, keepdims=True) * (1.0 / C)


def whole_spec(*shape):
    return pl.BlockSpec(shape, lambda t: (0,) * len(shape))


def each_spec(*shape):
    return pl.BlockSpec((1, *shape), lambda t: (t,) + (0,) * len(shape))


def row_mask(width):
    lane = lax.broadcasted_iota(jnp.int32, (8, width), 1)
    return (lane % 8 == lax.broadcasted_iota(jnp.int32, (8, width), 0)).astype(F32)


def spread_terms(feats_row_ref, feats_col_ref, embeds_ref, valid_ref, gain_ref, right, gain, both):
    for side, feats in enumerate((feats_row_ref, feats_col_ref)):
        terms = jnp.dot(embeds_ref[side], feats[0], preferred_element_type=F32)
        both[side] = terms * valid_ref[side, 0]
    mask = row_mask(W)
    same = lax.broadcasted_iota(jnp.int32, (C, C), 0) == lax.broadcasted_iota(jnp.int32, (C, C), 1)
    diagonal = jnp.where(same, jnp.broadcast_to(gain_ref[...].astype(F32), (C, C)), 0.0)
    both[2] = jnp.dot(diagonal.astype(BF), jnp.ones((C, W), BF), preferred_element_type=F32)
    rows = []
    for c in range(C):
        right[c] = jnp.broadcast_to(both[1, c : c + 1, :], (8, W))
        gain[c] = jnp.broadcast_to(both[2, c : c + 1, :], (8, W))
        rows.append(jnp.broadcast_to(both[0, c : c + 1, :], (8, W)) * mask)
    value = jnp.concatenate(rows, axis=0)
    high = value.astype(BF)
    return jnp.concatenate([high, (value - high.astype(F32)).astype(BF)], axis=1)


def make_pairs(pair_ref, left, lanes_ref, right, g):
    terms = unstack_rows(jnp.dot(left, lanes_ref[g], preferred_element_type=F32))
    raw = halves(pair_ref[0, :, g * 16 : g * 16 + 16, :].astype(F32))
    return [raw[part] + terms[part] + right[...] for part in range(2)]


def norm_kernel(
    pair_ref, feats_row_ref, feats_col_ref, embeds_ref, valid_ref, lanes_ref, gain_ref,
    kl_ref, kr_ref, pay_ref, inv_ref, right, gain, both, terms, wide,
):
    left = spread_terms(
        feats_row_ref, feats_col_ref, embeds_ref, valid_ref, gain_ref, right, gain, both
    )
    for g in range(4):
        terms[g] = jnp.dot(left, lanes_ref[g], preferred_element_type=F32)
    for g in range(4):
        scaleds, invs = [], []
        left_terms = unstack_rows(terms[g])
        raw = halves(pair_ref[0, :, g * 16 : g * 16 + 16, :].astype(F32))
        for part in range(2):
            pair = raw[part] + left_terms[part] + right[...]
            shifted = pair - mean_channels(pair)
            inverse = lax.rsqrt(mean_channels(shifted * shifted) + EPS)
            scaleds.append(shifted * inverse * gain[...])
            invs.append(inverse[0])
        inverses = jnp.concatenate(invs, axis=0)
        inv_ref[0, g * 16 : g * 16 + 16, :] = inverses
        wide[:, g * 256 : g * 256 + 256] = stack_rows(*scaleds).astype(BF)
        for q in range(g, C // 2, 4):
            pay_ref[0, q, 256:272, :] = inverses.astype(BF)
    for k, weight in enumerate((kl_ref, kr_ref)):
        outs = jnp.dot(weight[...], wide[...], preferred_element_type=F32)
        for g in range(4):
            out = join_rows(*unstack_rows(outs[:, g * 256 : g * 256 + 256])).astype(BF).reshape(C // 2, 2, 16, W)
            for s in range(2):
                first = k * 128 + s * 64 + g * 16
                pay_ref[0, :, first : first + 16, :] = out[:, s]


TERM_SPECS = [
    each_spec(C, H, W),
    pl.BlockSpec((1, C, W), lambda t: (t + T, 0, 0)),
    each_spec(C, W),
    whole_spec(2, C, C),
    pl.BlockSpec((2, 1, 1, W), lambda t: (0, t, 0, 0)),
    whole_spec(4, 2 * W, 2 * W),
    whole_spec(1, C),
]


def run_norm(pair, feats, embeds, valid, lanes, gain, kl, kr):
    return pl.pallas_call(
        norm_kernel,
        grid=(T,),
        in_specs=[*TERM_SPECS, whole_spec(K8, K8), whole_spec(K8, K8)],
        out_specs=[each_spec(C // 2, ROWS, W), each_spec(H, W)],
        out_shape=[
            pltpu.HBM((T, C // 2, ROWS, W), BF),
            jax.ShapeDtypeStruct((T, H, W), F32),
        ],
        scratch_shapes=[
            pltpu.VMEM((C, 8, W), F32),
            pltpu.VMEM((C, 8, W), F32),
            pltpu.VMEM((3, C, W), F32),
            pltpu.VMEM((4, K8, 2 * W), F32),
            pltpu.VMEM((K8, N), BF),
        ],
        compiler_params=params(),
        name="pair_norm",
    )(pair, feats, feats, embeds, valid, lanes, gain, kl, kr)


def spread(blocks_ref, full_ref):
    @pl.loop(0, 16)
    def _(r):
        for c in range(8):
            full_ref[pl.ds(r * H, H), c * W : (c + 1) * W] = blocks_ref[r * 8 + c]


def matrix(blocks_ref):
    rows = [
        jnp.concatenate([blocks_ref[r * 8 + c] for c in range(8)], axis=1) for r in range(16)
    ]
    return jnp.concatenate(rows, axis=0)


def product_kernel(left_ref, right_ref, out_ref):
    out = lax.dot_general(
        matrix(left_ref), matrix(right_ref), (((1,), (1,)), ((), ())), preferred_element_type=F32
    ).astype(BF)
    for r in range(16):
        for c in range(8):
            out_ref[r * 8 + c] = out[r * H : (r + 1) * H, c * W : (c + 1) * W]


def run_product(factors):
    spec = lambda first: pl.BlockSpec((128, H, W), lambda s: (0, first + s, 0))
    return pl.pallas_call(
        product_kernel,
        grid=(2,),
        in_specs=[spec(0), spec(2)],
        out_specs=pl.BlockSpec((128, H, W), lambda s: (0, s, 0)),
        out_shape=pltpu.HBM((128, 2 * H, W), BF),
        compiler_params=params(),
        name="triangle_product",
    )(factors, factors)


def back_kernel(
    pair_ref, feats_row_ref, feats_col_ref, embeds_ref, valid_ref, lanes_ref, gain_ref,
    inv_ref, grad_ref, kg_ref, kb_ref, scaled_ref, out_ref, sum_ref, right, gain, both,
):
    step = pl.program_id(0)
    left = spread_terms(
        feats_row_ref, feats_col_ref, embeds_ref, valid_ref, gain_ref, right, gain, both
    )

    @pl.when(step == 0)
    def _():
        sum_ref[...] = jnp.zeros_like(sum_ref)

    for g in range(4):
        rows = slice(g * 16, g * 16 + 16)
        pairs = make_pairs(pair_ref, left, lanes_ref, right, g)
        sum_ref[:, rows, :] += join_rows(*pairs)
        scaleds = []
        for part in range(2):
            first = g * 16 + part * 8
            inverse = inv_ref[0, first : first + 8, :][None]
            scaleds.append((pairs[part] - mean_channels(pairs[part])) * inverse * gain[...])
        scaled_ref[0, :, rows, :] = join_rows(*scaleds).astype(BF)
        opened = unstack_rows(
            jnp.dot(kg_ref[...], stack_rows(*scaleds).astype(BF), preferred_element_type=F32)
        )
        grads = halves(grad_ref[:, rows, :].astype(F32))
        grad_projs = [
            grads[part] * (1.0 / T) * jax.nn.sigmoid(opened[part]) for part in range(2)
        ]
        grad_norms = unstack_rows(
            jnp.dot(kb_ref[...], stack_rows(*grad_projs).astype(BF), preferred_element_type=F32)
        )
        outs = [grad_norm - mean_channels(grad_norm) for grad_norm in grad_norms]
        out_ref[0, :, rows, :] = join_rows(*outs).astype(BF)


def run_back(pair, feats, embeds, valid, lanes, gain, inv, grad, kg, kb):
    return pl.pallas_call(
        back_kernel,
        grid=(T,),
        in_specs=[
            *TERM_SPECS, each_spec(H, W), whole_spec(C, H, W), whole_spec(K8, K8), whole_spec(K8, K8)
        ],
        out_specs=[each_spec(C, H, W), each_spec(C, H, W), whole_spec(C, H, W)],
        out_shape=[
            pltpu.HBM((T, C, H, W), BF),
            pltpu.HBM((T, C, H, W), BF),
            jax.ShapeDtypeStruct((C, H, W), F32),
        ],
        scratch_shapes=[
            pltpu.VMEM((C, 8, W), F32),
            pltpu.VMEM((C, 8, W), F32),
            pltpu.VMEM((3, C, W), F32),
        ],
        compiler_params=params(),
        cost_estimate=pl.CostEstimate(flops=4 * 2**31, bytes_accessed=16 * 2**20, transcendentals=2**21),
        name="back_project",
    )(pair, feats, feats, embeds, valid, lanes, gain, inv, grad, kg, kb)


def product_norm(product):
    shifted = product - mean_channels(product)
    return shifted, lax.rsqrt(mean_channels(shifted * shifted) + EPS)


def grad_kernel(prod_ref, back_ref, out_ref):
    for g in range(4):
        rows = slice(g * 16, g * 16 + 16)
        shifted, inverse = product_norm(prod_ref[0, :, rows, :].astype(F32))
        back = back_ref[0, :, rows, :].astype(F32)
        slope = mean_channels(back * shifted) * inverse * inverse
        out_ref[0, :, rows, :] = ((back - shifted * slope) * inverse).astype(BF)


def run_grad(prod, back):
    return pl.pallas_call(
        grad_kernel,
        grid=(T,),
        in_specs=[each_spec(C, H, W), each_spec(C, H, W)],
        out_specs=each_spec(C, H, W),
        out_shape=pltpu.HBM((T, C, H, W), BF),
        compiler_params=params(),
        cost_estimate=pl.CostEstimate(flops=2**25, bytes_accessed=12 * 2**20, transcendentals=0),
        name="product_grad",
    )(prod, back)


def fold_rows(sums):
    return jnp.sum(sums.reshape(C, 8, W) * row_mask(W)[None], axis=1)


def gate_kernel(
    prod_ref, scaled_ref, grad_ref, sum_ref, inv_ref, kg_ref, ko_ref, pick_ref,
    emb_ref, mean_ref, rows_ref, cols_ref, grows_ref, gcols_ref, total,
):
    step = pl.program_id(0)
    row_sums = jnp.zeros((K8, W), F32)
    col_sums = jnp.zeros((C, 8, W), F32)
    for g in range(4):
        rows = slice(g * 16, g * 16 + 16)
        scaled = stack_rows(*halves(scaled_ref[0, :, rows, :].astype(F32))).astype(BF)
        opened = unstack_rows(jnp.dot(kg_ref[...], scaled, preferred_element_type=F32))
        normed = []
        for product in halves(prod_ref[0, :, rows, :].astype(F32)):
            shifted, inverse = product_norm(product)
            normed.append(shifted * inverse)
        projected = unstack_rows(
            jnp.dot(ko_ref[...], stack_rows(*normed).astype(BF), preferred_element_type=F32)
        )
        grads = halves(grad_ref[:, rows, :].astype(F32))
        weighted = []
        for part in range(2):
            first = g * 16 + part * 8
            where = (slice(None), slice(first, first + 8), slice(None))
            gate = jax.nn.sigmoid(opened[part])
            gated = gate * projected[part]

            @pl.when(step == 0)
            def _():
                total[where] = sum_ref[where] + gated

            @pl.when(step > 0)
            def _():
                total[where] += gated

            grad_gate = grads[part] * (1.0 / T) * gated * (1.0 - gate)
            mean_ref[0, first : first + 8, :] = jnp.sum(grad_gate * opened[part], axis=0)
            term = grad_gate * inv_ref[0, first : first + 8, :][None]
            col_sums = col_sums + term
            weighted.append(term)
        row_sums = row_sums + jnp.dot(
            stack_rows(*weighted).astype(BF), pick_ref[g], preferred_element_type=F32
        )
    rows_ref[0] = fold_rows(row_sums)
    cols_ref[0] = jnp.sum(col_sums, axis=1)

    @pl.when(step == 0)
    def _():
        grad_rows = jnp.zeros((K8, W), F32)
        grad_cols = jnp.zeros((C, 8, W), F32)
        for g in range(4):
            top, bottom = halves(grad_ref[:, g * 16 : g * 16 + 16, :].astype(F32))
            grad_cols = grad_cols + top + bottom
            grad_rows = grad_rows + jnp.dot(
                stack_rows(top, bottom).astype(BF), pick_ref[g], preferred_element_type=F32
            )
        grows_ref[...] = fold_rows(grad_rows)
        gcols_ref[...] = jnp.sum(grad_cols, axis=1)

    @pl.when(step == T - 1)
    def _():
        emb_ref[...] = (total[...] * (1.0 / T)).astype(BF)


def run_gate(prod, scaled, grad, pair_sum, inv, kg, ko, pick):
    return pl.pallas_call(
        gate_kernel,
        grid=(T,),
        in_specs=[
            each_spec(C, H, W), each_spec(C, H, W), whole_spec(C, H, W), whole_spec(C, H, W),
            each_spec(H, W), whole_spec(K8, K8), whole_spec(K8, K8), whole_spec(4, 2 * W, W),
        ],
        out_specs=[
            whole_spec(C, H, W), each_spec(H, W), each_spec(C, W), each_spec(C, W),
            whole_spec(C, W), whole_spec(C, W),
        ],
        out_shape=[
            jax.ShapeDtypeStruct((C, H, W), BF),
            jax.ShapeDtypeStruct((T, H, W), F32),
            jax.ShapeDtypeStruct((T, C, W), F32),
            jax.ShapeDtypeStruct((T, C, W), F32),
            jax.ShapeDtypeStruct((C, W), F32),
            jax.ShapeDtypeStruct((C, W), F32),
        ],
        scratch_shapes=[pltpu.VMEM((C, H, W), F32)],
        compiler_params=params(),
        cost_estimate=pl.CostEstimate(flops=4 * 2**31, bytes_accessed=12 * 2**20, transcendentals=2**21),
        name="gate_and_embed",
    )(prod, scaled, grad, pair_sum, inv, kg, ko, pick)


def square_kernel(left_ref, right_ref, left, right):
    spread(left_ref, left.at[0])
    spread(right_ref, right.at[0])


def run_square(factors):
    spec = lambda first: pl.BlockSpec((128, H, W), lambda s: (0, first + s, 0))
    out = pl.BlockSpec((1, N, N), lambda s: (s, 0, 0))
    return pl.pallas_call(
        square_kernel,
        grid=(2,),
        in_specs=[spec(0), spec(2)],
        out_specs=[out, out],
        out_shape=[pltpu.HBM((2, N, N), BF), pltpu.HBM((2, N, N), BF)],
        compiler_params=params(),
        cost_estimate=pl.CostEstimate(flops=2**20, bytes_accessed=16 * 2**20, transcendentals=0),
        name="to_matrices",
    )(factors, factors)


def run_matrix(blocks):
    return pl.pallas_call(
        spread,
        grid=(1,),
        in_specs=[whole_spec(128, H, W)],
        out_specs=whole_spec(N, N),
        out_shape=pltpu.HBM((N, N), BF),
        compiler_params=params(),
        cost_estimate=pl.CostEstimate(flops=2**20, bytes_accessed=4 * 2**20, transcendentals=0),
        name="to_matrix",
    )(blocks)


def factor_kernel(
    core_ref, left_ref, right_ref, grad_ref, inv_ref,
    kept_ref, given_ref, cols_ref, rows_ref, grad, mean,
):
    step = pl.program_id(0)
    core = core_ref[0]
    left, right = left_ref.at[0], right_ref.at[0]
    grad[...] = matrix(grad_ref)

    @pl.when(step == 0)
    def _():
        mean[...] = jnp.zeros_like(mean)

    def finish(value, rows, factor, kind):
        mean[rows, :] += value * factor[rows, :].astype(F32)
        term = value * inv_ref[rows, :].astype(F32)
        part = jnp.sum(term.reshape(128, 8, N), axis=0)
        lanes = term[:, :W]
        for c in range(1, 8):
            lanes = lanes + term[:, c * W : (c + 1) * W]
        rows_ref[0, kind, rows, :] = lanes
        return part

    blocks = [slice(0, N)]
    total = None
    for rows in blocks:
        value = jnp.dot(grad[rows, :], right[...], preferred_element_type=F32)
        part = finish(value, rows, left, 0)
        total = part if total is None else total + part
    cols_ref[0, 0] = total
    total = None
    for rows in blocks:
        value = lax.dot_general(
            grad[:, rows], left[...], (((0,), (0,)), ((), ())), preferred_element_type=F32
        )
        part = finish(value, rows, right, 1)
        total = part if total is None else total + part
    cols_ref[0, 1] = total

    @pl.when(step == 1)
    def _():
        @pl.loop(0, 16)
        def _(r):
            mine = pl.ds(pl.multiple_of(r * H + core * 32, 32), 32)
            other = pl.ds(pl.multiple_of(r * H + (1 - core) * 32, 32), 32)
            for c in range(8):
                kept_ref[r * 8 + c] = mean[mine, c * W : (c + 1) * W].astype(BF)
                given_ref[r * 8 + c] = mean[other, c * W : (c + 1) * W].astype(BF)


def run_factor(core, left, right, grad, inv):
    matrix = pl.BlockSpec((1, N, N), lambda s: (s, 0, 0))
    return pl.pallas_call(
        factor_kernel,
        grid=(2,),
        in_specs=[
            pl.BlockSpec(memory_space=pltpu.SMEM),
            matrix,
            matrix,
            pl.BlockSpec((128, H, W), lambda s: (0, s, 0)),
            pl.BlockSpec((N, N), lambda s: (0, 0)),
        ],
        out_specs=[
            pl.BlockSpec((128, H // 2, W), lambda s: (0, 0, 0)),
            pl.BlockSpec((128, H // 2, W), lambda s: (0, 0, 0)),
            pl.BlockSpec((1, 2, 8, N), lambda s: (s, 0, 0, 0)),
            pl.BlockSpec((1, 2, N, W), lambda s: (s, 0, 0, 0)),
        ],
        out_shape=[
            jax.ShapeDtypeStruct((128, H // 2, W), BF),
            jax.ShapeDtypeStruct((128, H // 2, W), BF),
            jax.ShapeDtypeStruct((2, 2, 8, N), F32),
            jax.ShapeDtypeStruct((2, 2, N, W), F32),
        ],
        scratch_shapes=[pltpu.VMEM((N, N), BF), pltpu.VMEM((N, N), F32)],
        compiler_params=params(),
        name="factor_grads",
    )(core.reshape(1), left, right, grad, inv)


def add_kernel(left_ref, right_ref, out_ref):
    out_ref[...] = (left_ref[...].astype(F32) + right_ref[...].astype(F32)).astype(BF)


def run_add(left, right):
    spec = pl.BlockSpec((64, H // 2, W), lambda i: (i, 0, 0))
    return pl.pallas_call(
        add_kernel,
        grid=(2,),
        in_specs=[spec, spec],
        out_specs=spec,
        out_shape=pltpu.HBM((128, H // 2, W), BF),
        compiler_params=params(40),
        name="add_halves",
    )(left, right)


def close_kernel(
    recv_ref, mean_ref, inv_ref, scaled_ref, pick_ref, weight_ref, valid_ref, base_ref, *out_refs
):
    got = recv_ref[0].astype(F32)
    total = got[0]
    for k in range(1, 16):
        total = total + got[k]
    weight = (total.reshape(H, W) + mean_ref[0]) * inv_ref[0] * (1.0 / C)
    row_sums = jnp.zeros((K8, W), F32)
    col_sums = jnp.zeros((C, 8, W), F32)
    for g in range(4):
        scaled = scaled_ref[0, :, g * 16 : g * 16 + 16, :].astype(F32)
        terms = []
        for part in range(2):
            first = g * 16 + part * 8
            term = scaled[:, part * 8 : part * 8 + 8, :] * weight[first : first + 8, :][None]
            col_sums = col_sums + term
            terms.append(term)
        row_sums = row_sums + jnp.dot(
            stack_rows(*terms).astype(BF), pick_ref[g], preferred_element_type=F32
        )
    for side, sums in enumerate((fold_rows(row_sums), jnp.sum(col_sums, axis=1))):
        value = jnp.dot(weight_ref[side], sums, precision=HIGHEST, preferred_element_type=F32)
        value = (base_ref[side, 0] + value * valid_ref[side, 0]).astype(BF)
        for k, out_ref in enumerate(out_refs):
            out_ref[side, 0] = value[k * 16 : k * 16 + 16]


def run_close(recv, mean, inv, scaled, pick, weights, valid, base):
    both = lambda *shape: pl.BlockSpec((2, 1, *shape), lambda t: (0, t) + (0,) * len(shape))
    return pl.pallas_call(
        close_kernel,
        grid=(T,),
        in_specs=[
            each_spec(16, 2, H // 2, W), each_spec(H, W), each_spec(H, W), each_spec(C, H, W),
            whole_spec(4, 2 * W, W), whole_spec(2, C, C), both(1, W), both(C, W),
        ],
        out_specs=[both(16, W)] * 4,
        out_shape=[jax.ShapeDtypeStruct((2, T, 16, W), BF)] * 4,
        compiler_params=params(58),
        name="close_sums",
    )(recv, mean, inv, scaled, pick, weights, valid, base)


def from_member(value, k):
    return lax.ppermute(value, "col", [(i, i ^ k) for i in range(8)])


def swap_cores(value):
    return from_member(value, 1)


def exchange(value):
    return lax.all_to_all(value, AXES, split_axis=0, concat_axis=0, tiled=True)


def in_order(core, mine, other, axis):
    first = jnp.where(core == 0, mine, other)
    second = jnp.where(core == 0, other, mine)
    return jnp.concatenate([first, second], axis=axis)


def by_member(value, member):
    lead, last = value.shape[:-2], value.shape[-1]
    cut = value.reshape(*lead, 2, 2, 16, last)
    cut = jnp.where(member % 2 == 1, cut[..., ::-1, :, :], cut)
    cut = jnp.where(member // 2 == 1, cut[..., ::-1, :, :, :], cut)
    return cut.reshape(*lead, 64, last)


def expand(weights):
    to = jnp.asarray(np.kron(np.eye(C), np.ones((8, 1))), BF)
    tall = jnp.einsum("ac,ncd->nad", to, weights, preferred_element_type=F32).astype(BF)
    wide = jnp.einsum("nad,bd->nab", tall, to, preferred_element_type=F32)
    index = jnp.arange(K8, dtype=jnp.int32) % 8
    return jnp.where(index[:, None] == index[None, :], wide, 0.0).astype(BF)


def per_device(
    template_pair,
    template_feat,
    block_map,
    block_count,
    residue_mask,
    row_embed,
    col_embed,
    norm_gain,
    left_proj,
    right_proj,
    gate_proj,
    out_proj,
    embed_grad,
):
    row = lax.axis_index("row")
    col = lax.axis_index("col")
    core = col % 2
    me = row * 8 + col
    own = me // 32
    pair_at = me % 32
    blocks = jnp.arange(128, dtype=jnp.int32)
    half = row % 2
    row_block = row // 2

    member = col % 4
    sent_feat = jnp.broadcast_to(template_feat.reshape(1, 4, 16, W), (32, 4, 16, W))
    pool = exchange(sent_feat.reshape(128, 16, W))
    gain = norm_gain.astype(F32)
    column_ids = lambda m, at: lax.dynamic_index_in_dim(m, at, axis=1, keepdims=False)
    row_ids = column_ids(block_map, row_block)
    member_ids = [column_ids(block_map, col ^ k) for k in range(4)]
    wanted = jnp.concatenate([jnp.concatenate([ids, row_ids]) for ids in member_ids])
    choose = (wanted[:, None] == blocks[None, :]).astype(BF)
    picked = jnp.einsum(
        "eb,bx->ex", choose, pool.reshape(128, 16 * W), preferred_element_type=F32
    ).astype(BF)
    picked = picked.reshape(4, 8, 16, W)
    feats = jnp.concatenate(
        [picked[0]] + [from_member(picked[k], k) for k in range(1, 4)], axis=1
    )
    embeds = by_member(jnp.stack([row_embed, col_embed]), member)

    offsets = jnp.arange(W, dtype=jnp.int32)

    def marks(at):
        kept = lax.dynamic_slice_in_dim(residue_mask, at * W, W, axis=1) == 1
        return kept & (offsets[None, :] < column_ids(block_count, at)[:, None])

    col_valid = marks(col).astype(F32)
    row_valid = (marks(row_block) & (offsets // H == half)[None, :]).astype(F32)
    valid = jnp.stack([row_valid, col_valid])[:, :, None, :]
    turned = jnp.swapaxes(embeds, 1, 2)
    kl, kr = expand(jnp.stack([left_proj.T, right_proj.T]))
    group = 2 * np.arange(4)[:, None, None] + (np.arange(2 * W) // W)[None, :, None]
    lanes = np.arange(W)[None, None, :] % H // 8 == group
    terms_pick = jnp.asarray(np.tile(lanes.transpose(0, 2, 1), (1, 2, 1)), BF)
    sums_pick = jnp.where((offsets // H == half)[None, None, :], jnp.asarray(lanes, BF), 0)

    terms = (template_pair, feats, turned, valid, terms_pick, norm_gain.reshape(1, C))
    sent, inv = run_norm(*terms, kl, kr)
    sent, gate_late, out_late = lax.optimization_barrier((sent, gate_proj, out_proj))
    kg, ko, kb = expand(jnp.stack([gate_late.T, out_late.T, out_late]))
    def center(weights):
        scaled_weights = gain[:, None] * weights.astype(F32)
        return scaled_weights - jnp.mean(scaled_weights, axis=0, keepdims=True)

    embeds = embeds.astype(F32)
    mixed = jnp.einsum(
        "efd,kdc->kefc",
        embeds,
        jnp.stack([center(left_proj), center(right_proj), center(gate_proj)]),
        precision=HIGHEST,
    )
    closing = -embeds / gain[None, None, :]
    opening = embeds * (1.0 / T)
    weights = lax.dynamic_slice_in_dim(mixed[:2], 2 * pair_at, 2, axis=3)
    own_map = lax.dynamic_index_in_dim(block_map, own, axis=0, keepdims=False)
    own_count = lax.dynamic_index_in_dim(block_count, own, axis=0, keepdims=False)
    own_marks = lax.dynamic_index_in_dim(residue_mask, own, axis=0, keepdims=False)
    own_valid = (offsets[None, :] < own_count[:, None]) & (own_marks.reshape(8, W) == 1)
    own_valid = own_valid.astype(F32)
    targets = jnp.concatenate(
        [own_map] * 4 + [jnp.concatenate([row_ids, ids]) for ids in member_ids]
    )
    place = (targets[None, :] == blocks[:, None]).astype(BF)
    factors = exchange(sent.reshape(128, ROWS, W))
    scaled, back, pair_sum = run_back(*terms, inv, embed_grad, kg, kb)
    factors, scaled, back, pair_sum, mixed, closing, opening, weights, own_valid, place = (
        lax.optimization_barrier(
            (factors, scaled, back, pair_sum, mixed, closing, opening, weights, own_valid, place)
        )
    )
    first, rest = factors[:64, None, 256:], factors[64:, None, 256:]
    first_other = from_member(first, 2)
    product, first_other = lax.optimization_barrier((run_product(factors), first_other))
    prod = exchange(product).reshape(T, C, H, W)
    left, right = run_square(factors)
    prod, left, right, first, rest = lax.optimization_barrier((prod, left, right, first, rest))
    rest_other = from_member(rest, 2)
    grad_prod = run_grad(prod, back)
    grad_prod, first, rest, rest_other = lax.optimization_barrier(
        (grad_prod, first, rest, rest_other)
    )
    grads = exchange(grad_prod.reshape(128, 2 * H, W))
    inv_part = jnp.concatenate(
        [
            in_order(member // 2, first, first_other, 1),
            in_order(member // 2, rest, rest_other, 1),
        ],
        axis=0,
    )[:, :, None]
    inv_all = in_order(core, inv_part, swap_cores(inv_part), 2).reshape(128, H, W)
    inv_matrix = run_matrix(inv_all)
    embedding, gate_mean, gate_rows, gate_cols, out_rows, out_cols = run_gate(
        prod, scaled, embed_grad, pair_sum, inv, kg, ko, sums_pick
    )
    grads, embedding, gate_mean, gate_rows, gate_cols, out_rows, out_cols, inv_matrix = (
        lax.optimization_barrier(
            (grads, embedding, gate_mean, gate_rows, gate_cols, out_rows, out_cols, inv_matrix)
        )
    )
    kept, given, col_sums, row_sums = run_factor(core, left, right, grads, inv_matrix)
    mean_half = run_add(kept, swap_cores(given))
    col_sums, row_sums, mean_half = lax.optimization_barrier((col_sums, row_sums, mean_half))
    recv = exchange(mean_half).reshape(T, 16, 2, H // 2, W)

    base = jnp.einsum(
        "efc,etcp->etfp", mixed[2], jnp.stack([gate_rows, gate_cols]), precision=HIGHEST
    )
    opened = jnp.einsum(
        "efc,ecp->efp", opening, jnp.stack([out_rows, out_cols]), precision=HIGHEST
    )
    base = (base + opened[:, None]) * valid
    owned = jnp.stack([jnp.sum(row_sums, axis=3), jnp.sum(col_sums, axis=2)], axis=2)
    grad_own = jnp.einsum("kefs,sken->fn", weights, owned, precision=HIGHEST)
    grad_own = grad_own.reshape(C, 8, W).transpose(1, 0, 2) * own_valid[:, None, :]
    grad_own = grad_own.astype(BF)
    def quarters(value):
        cut = [value[:, k * 16 : k * 16 + 16] for k in range(4)]
        return [cut[0]] + [from_member(cut[k], k) for k in range(1, 4)]

    own_parts = quarters(grad_own)
    recv, base, *own_parts = lax.optimization_barrier((recv, base, *own_parts))
    closed = run_close(recv, gate_mean, inv, scaled, sums_pick, closing, valid, base)
    closed = [part.reshape(2 * T, 16, W) for part in closed]
    parts = [closed[0]] + [from_member(closed[k], k) for k in range(1, 4)]
    entries = jnp.concatenate([*own_parts, *parts], axis=0)
    placed = jnp.einsum(
        "be,ex->bx", place, entries.reshape(64, 16 * W), preferred_element_type=F32
    ).astype(BF)
    result = exchange(placed.reshape(128, 16, W)).reshape(32, 4 * 16, W)
    feat_grad = jnp.sum(result.astype(F32), axis=0)[None]
    return (embedding, feat_grad)


def solution(mesh):
    return jax.shard_map(
        per_device,
        mesh=mesh,
        in_specs=(
            P(None, None, "row", "col"),
            P(("row", "col"), None, None),
            P(),
            P(),
            P(),
            P(),
            P(),
            P(),
            P(),
            P(),
            P(),
            P(),
            P(None, "row", "col"),
        ),
        out_specs=(P(None, "row", "col"), P(("row", "col"), None, None)),
        check_vma=False,
    )
```

```python
import jax
import jax.numpy as jnp
import numpy as np
from jax import lax
from jax.experimental import pallas as pl
from jax.experimental.pallas import tpu as pltpu
from jax.sharding import PartitionSpec as P

EPS = 1e-05
HIGHEST = lax.Precision.HIGHEST
F32 = jnp.float32
BF = jnp.bfloat16
AXES = ("row", "col")

C = 64
T = 4
H = 64
W = 128
N = 1024
K8 = C * 8
ROWS = 272


def params(mib=60):
    return pltpu.CompilerParams(vmem_limit_bytes=mib * 2**20)


def stack_rows(top, bottom):
    return jnp.concatenate([top.reshape(K8, W), bottom.reshape(K8, W)], axis=1)


def unstack_rows(wide):
    return wide[:, :W].reshape(C, 8, W), wide[:, W:].reshape(C, 8, W)


def join_rows(top, bottom):
    return jnp.concatenate([top, bottom], axis=1)


def halves(value):
    return value[:, :8, :], value[:, 8:, :]


def mean_channels(value):
    return jnp.sum(value, axis=0, keepdims=True) * (1.0 / C)


def whole_spec(*shape):
    return pl.BlockSpec(shape, lambda t: (0,) * len(shape))


def each_spec(*shape):
    return pl.BlockSpec((1, *shape), lambda t: (t,) + (0,) * len(shape))


def row_mask(width):
    lane = lax.broadcasted_iota(jnp.int32, (8, width), 1)
    return (lane % 8 == lax.broadcasted_iota(jnp.int32, (8, width), 0)).astype(F32)


def spread_terms(feats_row_ref, feats_col_ref, embeds_ref, valid_ref, gain_ref, right, gain, both):
    for side, feats in enumerate((feats_row_ref, feats_col_ref)):
        terms = jnp.dot(embeds_ref[side], feats[0], preferred_element_type=F32)
        both[side] = terms * valid_ref[side, 0]
    mask = row_mask(W)
    same = lax.broadcasted_iota(jnp.int32, (C, C), 0) == lax.broadcasted_iota(jnp.int32, (C, C), 1)
    diagonal = jnp.where(same, jnp.broadcast_to(gain_ref[...].astype(F32), (C, C)), 0.0)
    both[2] = jnp.dot(diagonal.astype(BF), jnp.ones((C, W), BF), preferred_element_type=F32)
    rows = []
    for c in range(C):
        right[c] = jnp.broadcast_to(both[1, c : c + 1, :], (8, W))
        gain[c] = jnp.broadcast_to(both[2, c : c + 1, :], (8, W))
        rows.append(jnp.broadcast_to(both[0, c : c + 1, :], (8, W)) * mask)
    value = jnp.concatenate(rows, axis=0)
    high = value.astype(BF)
    return jnp.concatenate([high, (value - high.astype(F32)).astype(BF)], axis=1)


def make_pairs(pair_ref, left, lanes_ref, right, g):
    terms = unstack_rows(jnp.dot(left, lanes_ref[g], preferred_element_type=F32))
    raw = halves(pair_ref[0, :, g * 16 : g * 16 + 16, :].astype(F32))
    return [raw[part] + terms[part] + right[...] for part in range(2)]


def norm_kernel(
    pair_ref, feats_row_ref, feats_col_ref, embeds_ref, valid_ref, lanes_ref, gain_ref,
    kl_ref, kr_ref, pay_ref, inv_ref, right, gain, both, terms, wide,
):
    left = spread_terms(
        feats_row_ref, feats_col_ref, embeds_ref, valid_ref, gain_ref, right, gain, both
    )
    for g in range(4):
        terms[g] = jnp.dot(left, lanes_ref[g], preferred_element_type=F32)
    for g in range(4):
        scaleds, invs = [], []
        left_terms = unstack_rows(terms[g])
        raw = halves(pair_ref[0, :, g * 16 : g * 16 + 16, :].astype(F32))
        for part in range(2):
            pair = raw[part] + left_terms[part] + right[...]
            shifted = pair - mean_channels(pair)
            inverse = lax.rsqrt(mean_channels(shifted * shifted) + EPS)
            scaleds.append(shifted * inverse * gain[...])
            invs.append(inverse[0])
        inverses = jnp.concatenate(invs, axis=0)
        inv_ref[0, g * 16 : g * 16 + 16, :] = inverses
        wide[:, g * 256 : g * 256 + 256] = stack_rows(*scaleds).astype(BF)
        for q in range(g, C // 2, 4):
            pay_ref[0, q, 256:272, :] = inverses.astype(BF)
    for k, weight in enumerate((kl_ref, kr_ref)):
        outs = jnp.dot(weight[...], wide[...], preferred_element_type=F32)
        for g in range(4):
            out = join_rows(*unstack_rows(outs[:, g * 256 : g * 256 + 256])).astype(BF).reshape(C // 2, 2, 16, W)
            for s in range(2):
                first = k * 128 + s * 64 + g * 16
                pay_ref[0, :, first : first + 16, :] = out[:, s]


TERM_SPECS = [
    each_spec(C, H, W),
    pl.BlockSpec((1, C, W), lambda t: (t + T, 0, 0)),
    each_spec(C, W),
    whole_spec(2, C, C),
    pl.BlockSpec((2, 1, 1, W), lambda t: (0, t, 0, 0)),
    whole_spec(4, 2 * W, 2 * W),
    whole_spec(1, C),
]


def run_norm(pair, feats, embeds, valid, lanes, gain, kl, kr):
    return pl.pallas_call(
        norm_kernel,
        grid=(T,),
        in_specs=[*TERM_SPECS, whole_spec(K8, K8), whole_spec(K8, K8)],
        out_specs=[each_spec(C // 2, ROWS, W), each_spec(H, W)],
        out_shape=[
            pltpu.HBM((T, C // 2, ROWS, W), BF),
            jax.ShapeDtypeStruct((T, H, W), F32),
        ],
        scratch_shapes=[
            pltpu.VMEM((C, 8, W), F32),
            pltpu.VMEM((C, 8, W), F32),
            pltpu.VMEM((3, C, W), F32),
            pltpu.VMEM((4, K8, 2 * W), F32),
            pltpu.VMEM((K8, N), BF),
        ],
        compiler_params=params(),
        name="pair_norm",
    )(pair, feats, feats, embeds, valid, lanes, gain, kl, kr)


def spread(blocks_ref, full_ref):
    @pl.loop(0, 16)
    def _(r):
        for c in range(8):
            full_ref[pl.ds(r * H, H), c * W : (c + 1) * W] = blocks_ref[r * 8 + c]


def matrix(blocks_ref):
    rows = [
        jnp.concatenate([blocks_ref[r * 8 + c] for c in range(8)], axis=1) for r in range(16)
    ]
    return jnp.concatenate(rows, axis=0)


def product_kernel(left_ref, right_ref, out_ref):
    out = lax.dot_general(
        matrix(left_ref), matrix(right_ref), (((1,), (1,)), ((), ())), preferred_element_type=F32
    ).astype(BF)
    for r in range(16):
        for c in range(8):
            out_ref[r * 8 + c] = out[r * H : (r + 1) * H, c * W : (c + 1) * W]


def run_product(factors):
    spec = lambda first: pl.BlockSpec((128, H, W), lambda s: (0, first + s, 0))
    return pl.pallas_call(
        product_kernel,
        grid=(2,),
        in_specs=[spec(0), spec(2)],
        out_specs=pl.BlockSpec((128, H, W), lambda s: (0, s, 0)),
        out_shape=pltpu.HBM((128, 2 * H, W), BF),
        compiler_params=params(),
        name="triangle_product",
    )(factors, factors)


def back_kernel(
    pair_ref, feats_row_ref, feats_col_ref, embeds_ref, valid_ref, lanes_ref, gain_ref,
    inv_ref, grad_ref, kg_ref, kb_ref, scaled_ref, out_ref, sum_ref, right, gain, both,
):
    step = pl.program_id(0)
    left = spread_terms(
        feats_row_ref, feats_col_ref, embeds_ref, valid_ref, gain_ref, right, gain, both
    )

    @pl.when(step == 0)
    def _():
        sum_ref[...] = jnp.zeros_like(sum_ref)

    for g in range(4):
        rows = slice(g * 16, g * 16 + 16)
        pairs = make_pairs(pair_ref, left, lanes_ref, right, g)
        sum_ref[:, rows, :] += join_rows(*pairs)
        scaleds = []
        for part in range(2):
            first = g * 16 + part * 8
            inverse = inv_ref[0, first : first + 8, :][None]
            scaleds.append((pairs[part] - mean_channels(pairs[part])) * inverse * gain[...])
        scaled_ref[0, :, rows, :] = join_rows(*scaleds).astype(BF)
        opened = unstack_rows(
            jnp.dot(kg_ref[...], stack_rows(*scaleds).astype(BF), preferred_element_type=F32)
        )
        grads = halves(grad_ref[:, rows, :].astype(F32))
        grad_projs = [
            grads[part] * (1.0 / T) * jax.nn.sigmoid(opened[part]) for part in range(2)
        ]
        grad_norms = unstack_rows(
            jnp.dot(kb_ref[...], stack_rows(*grad_projs).astype(BF), preferred_element_type=F32)
        )
        outs = [grad_norm - mean_channels(grad_norm) for grad_norm in grad_norms]
        out_ref[0, :, rows, :] = join_rows(*outs).astype(BF)


def run_back(pair, feats, embeds, valid, lanes, gain, inv, grad, kg, kb):
    return pl.pallas_call(
        back_kernel,
        grid=(T,),
        in_specs=[
            *TERM_SPECS, each_spec(H, W), whole_spec(C, H, W), whole_spec(K8, K8), whole_spec(K8, K8)
        ],
        out_specs=[each_spec(C, H, W), each_spec(C, H, W), whole_spec(C, H, W)],
        out_shape=[
            pltpu.HBM((T, C, H, W), BF),
            pltpu.HBM((T, C, H, W), BF),
            jax.ShapeDtypeStruct((C, H, W), F32),
        ],
        scratch_shapes=[
            pltpu.VMEM((C, 8, W), F32),
            pltpu.VMEM((C, 8, W), F32),
            pltpu.VMEM((3, C, W), F32),
        ],
        compiler_params=params(),
        cost_estimate=pl.CostEstimate(flops=4 * 2**31, bytes_accessed=16 * 2**20, transcendentals=2**21),
        name="back_project",
    )(pair, feats, feats, embeds, valid, lanes, gain, inv, grad, kg, kb)


def product_norm(product):
    shifted = product - mean_channels(product)
    return shifted, lax.rsqrt(mean_channels(shifted * shifted) + EPS)


def grad_kernel(prod_ref, back_ref, out_ref):
    for g in range(4):
        rows = slice(g * 16, g * 16 + 16)
        shifted, inverse = product_norm(prod_ref[0, :, rows, :].astype(F32))
        back = back_ref[0, :, rows, :].astype(F32)
        slope = mean_channels(back * shifted) * inverse * inverse
        out_ref[0, :, rows, :] = ((back - shifted * slope) * inverse).astype(BF)


def run_grad(prod, back):
    return pl.pallas_call(
        grad_kernel,
        grid=(T,),
        in_specs=[each_spec(C, H, W), each_spec(C, H, W)],
        out_specs=each_spec(C, H, W),
        out_shape=pltpu.HBM((T, C, H, W), BF),
        compiler_params=params(),
        cost_estimate=pl.CostEstimate(flops=2**25, bytes_accessed=12 * 2**20, transcendentals=0),
        name="product_grad",
    )(prod, back)


def fold_rows(sums):
    return jnp.sum(sums.reshape(C, 8, W) * row_mask(W)[None], axis=1)


def gate_kernel(
    prod_ref, scaled_ref, grad_ref, sum_ref, inv_ref, kg_ref, ko_ref, pick_ref,
    emb_ref, mean_ref, rows_ref, cols_ref, grows_ref, gcols_ref, total,
):
    step = pl.program_id(0)
    row_sums = jnp.zeros((K8, W), F32)
    col_sums = jnp.zeros((C, 8, W), F32)
    for g in range(4):
        rows = slice(g * 16, g * 16 + 16)
        scaled = stack_rows(*halves(scaled_ref[0, :, rows, :].astype(F32))).astype(BF)
        opened = unstack_rows(jnp.dot(kg_ref[...], scaled, preferred_element_type=F32))
        normed = []
        for product in halves(prod_ref[0, :, rows, :].astype(F32)):
            shifted, inverse = product_norm(product)
            normed.append(shifted * inverse)
        projected = unstack_rows(
            jnp.dot(ko_ref[...], stack_rows(*normed).astype(BF), preferred_element_type=F32)
        )
        grads = halves(grad_ref[:, rows, :].astype(F32))
        weighted = []
        for part in range(2):
            first = g * 16 + part * 8
            where = (slice(None), slice(first, first + 8), slice(None))
            gate = jax.nn.sigmoid(opened[part])
            gated = gate * projected[part]

            @pl.when(step == 0)
            def _():
                total[where] = sum_ref[where] + gated

            @pl.when(step > 0)
            def _():
                total[where] += gated

            grad_gate = grads[part] * (1.0 / T) * gated * (1.0 - gate)
            mean_ref[0, first : first + 8, :] = jnp.sum(grad_gate * opened[part], axis=0)
            term = grad_gate * inv_ref[0, first : first + 8, :][None]
            col_sums = col_sums + term
            weighted.append(term)
        row_sums = row_sums + jnp.dot(
            stack_rows(*weighted).astype(BF), pick_ref[g], preferred_element_type=F32
        )
    rows_ref[0] = fold_rows(row_sums)
    cols_ref[0] = jnp.sum(col_sums, axis=1)

    @pl.when(step == 0)
    def _():
        grad_rows = jnp.zeros((K8, W), F32)
        grad_cols = jnp.zeros((C, 8, W), F32)
        for g in range(4):
            top, bottom = halves(grad_ref[:, g * 16 : g * 16 + 16, :].astype(F32))
            grad_cols = grad_cols + top + bottom
            grad_rows = grad_rows + jnp.dot(
                stack_rows(top, bottom).astype(BF), pick_ref[g], preferred_element_type=F32
            )
        grows_ref[...] = fold_rows(grad_rows)
        gcols_ref[...] = jnp.sum(grad_cols, axis=1)

    @pl.when(step == T - 1)
    def _():
        emb_ref[...] = (total[...] * (1.0 / T)).astype(BF)


def run_gate(prod, scaled, grad, pair_sum, inv, kg, ko, pick):
    return pl.pallas_call(
        gate_kernel,
        grid=(T,),
        in_specs=[
            each_spec(C, H, W), each_spec(C, H, W), whole_spec(C, H, W), whole_spec(C, H, W),
            each_spec(H, W), whole_spec(K8, K8), whole_spec(K8, K8), whole_spec(4, 2 * W, W),
        ],
        out_specs=[
            whole_spec(C, H, W), each_spec(H, W), each_spec(C, W), each_spec(C, W),
            whole_spec(C, W), whole_spec(C, W),
        ],
        out_shape=[
            jax.ShapeDtypeStruct((C, H, W), BF),
            jax.ShapeDtypeStruct((T, H, W), F32),
            jax.ShapeDtypeStruct((T, C, W), F32),
            jax.ShapeDtypeStruct((T, C, W), F32),
            jax.ShapeDtypeStruct((C, W), F32),
            jax.ShapeDtypeStruct((C, W), F32),
        ],
        scratch_shapes=[pltpu.VMEM((C, H, W), F32)],
        compiler_params=params(),
        cost_estimate=pl.CostEstimate(flops=4 * 2**31, bytes_accessed=12 * 2**20, transcendentals=2**21),
        name="gate_and_embed",
    )(prod, scaled, grad, pair_sum, inv, kg, ko, pick)


def square_kernel(left_ref, right_ref, left, right):
    spread(left_ref, left.at[0])
    spread(right_ref, right.at[0])


def run_square(factors):
    spec = lambda first: pl.BlockSpec((128, H, W), lambda s: (0, first + s, 0))
    out = pl.BlockSpec((1, N, N), lambda s: (s, 0, 0))
    return pl.pallas_call(
        square_kernel,
        grid=(2,),
        in_specs=[spec(0), spec(2)],
        out_specs=[out, out],
        out_shape=[pltpu.HBM((2, N, N), BF), pltpu.HBM((2, N, N), BF)],
        compiler_params=params(),
        cost_estimate=pl.CostEstimate(flops=2**20, bytes_accessed=16 * 2**20, transcendentals=0),
        name="to_matrices",
    )(factors, factors)


def run_matrix(blocks):
    return pl.pallas_call(
        spread,
        grid=(1,),
        in_specs=[whole_spec(128, H, W)],
        out_specs=whole_spec(N, N),
        out_shape=pltpu.HBM((N, N), BF),
        compiler_params=params(),
        cost_estimate=pl.CostEstimate(flops=2**20, bytes_accessed=4 * 2**20, transcendentals=0),
        name="to_matrix",
    )(blocks)


def factor_kernel(
    core_ref, left_ref, right_ref, grad_ref, inv_ref,
    kept_ref, given_ref, cols_ref, rows_ref, grad, mean,
):
    step = pl.program_id(0)
    core = core_ref[0]
    left, right = left_ref.at[0], right_ref.at[0]
    grad[...] = matrix(grad_ref)

    @pl.when(step == 0)
    def _():
        mean[...] = jnp.zeros_like(mean)

    def finish(value, rows, factor, kind):
        mean[rows, :] += value * factor[rows, :].astype(F32)
        term = value * inv_ref[rows, :].astype(F32)
        part = jnp.sum(term.reshape(128, 8, N), axis=0)
        lanes = term[:, :W]
        for c in range(1, 8):
            lanes = lanes + term[:, c * W : (c + 1) * W]
        rows_ref[0, kind, rows, :] = lanes
        return part

    blocks = [slice(0, N)]
    total = None
    for rows in blocks:
        value = jnp.dot(grad[rows, :], right[...], preferred_element_type=F32)
        part = finish(value, rows, left, 0)
        total = part if total is None else total + part
    cols_ref[0, 0] = total
    total = None
    for rows in blocks:
        value = lax.dot_general(
            grad[:, rows], left[...], (((0,), (0,)), ((), ())), preferred_element_type=F32
        )
        part = finish(value, rows, right, 1)
        total = part if total is None else total + part
    cols_ref[0, 1] = total

    @pl.when(step == 1)
    def _():
        @pl.loop(0, 16)
        def _(r):
            mine = pl.ds(pl.multiple_of(r * H + core * 32, 32), 32)
            other = pl.ds(pl.multiple_of(r * H + (1 - core) * 32, 32), 32)
            for c in range(8):
                kept_ref[r * 8 + c] = mean[mine, c * W : (c + 1) * W].astype(BF)
                given_ref[r * 8 + c] = mean[other, c * W : (c + 1) * W].astype(BF)


def run_factor(core, left, right, grad, inv):
    matrix = pl.BlockSpec((1, N, N), lambda s: (s, 0, 0))
    return pl.pallas_call(
        factor_kernel,
        grid=(2,),
        in_specs=[
            pl.BlockSpec(memory_space=pltpu.SMEM),
            matrix,
            matrix,
            pl.BlockSpec((128, H, W), lambda s: (0, s, 0)),
            pl.BlockSpec((N, N), lambda s: (0, 0)),
        ],
        out_specs=[
            pl.BlockSpec((128, H // 2, W), lambda s: (0, 0, 0)),
            pl.BlockSpec((128, H // 2, W), lambda s: (0, 0, 0)),
            pl.BlockSpec((1, 2, 8, N), lambda s: (s, 0, 0, 0)),
            pl.BlockSpec((1, 2, N, W), lambda s: (s, 0, 0, 0)),
        ],
        out_shape=[
            jax.ShapeDtypeStruct((128, H // 2, W), BF),
            jax.ShapeDtypeStruct((128, H // 2, W), BF),
            jax.ShapeDtypeStruct((2, 2, 8, N), F32),
            jax.ShapeDtypeStruct((2, 2, N, W), F32),
        ],
        scratch_shapes=[pltpu.VMEM((N, N), BF), pltpu.VMEM((N, N), F32)],
        compiler_params=params(),
        name="factor_grads",
    )(core.reshape(1), left, right, grad, inv)


def add_kernel(left_ref, right_ref, out_ref):
    out_ref[...] = (left_ref[...].astype(F32) + right_ref[...].astype(F32)).astype(BF)


def run_add(left, right):
    spec = pl.BlockSpec((64, H // 2, W), lambda i: (i, 0, 0))
    return pl.pallas_call(
        add_kernel,
        grid=(2,),
        in_specs=[spec, spec],
        out_specs=spec,
        out_shape=pltpu.HBM((128, H // 2, W), BF),
        compiler_params=params(40),
        name="add_halves",
    )(left, right)


def close_kernel(
    recv_ref, mean_ref, inv_ref, scaled_ref, pick_ref, weight_ref, valid_ref, base_ref, *out_refs
):
    got = recv_ref[0].astype(F32)
    total = got[0]
    for k in range(1, 16):
        total = total + got[k]
    weight = (total.reshape(H, W) + mean_ref[0]) * inv_ref[0] * (1.0 / C)
    row_sums = jnp.zeros((K8, W), F32)
    col_sums = jnp.zeros((C, 8, W), F32)
    for g in range(4):
        scaled = scaled_ref[0, :, g * 16 : g * 16 + 16, :].astype(F32)
        terms = []
        for part in range(2):
            first = g * 16 + part * 8
            term = scaled[:, part * 8 : part * 8 + 8, :] * weight[first : first + 8, :][None]
            col_sums = col_sums + term
            terms.append(term)
        row_sums = row_sums + jnp.dot(
            stack_rows(*terms).astype(BF), pick_ref[g], preferred_element_type=F32
        )
    for side, sums in enumerate((fold_rows(row_sums), jnp.sum(col_sums, axis=1))):
        value = jnp.dot(weight_ref[side], sums, precision=HIGHEST, preferred_element_type=F32)
        value = (base_ref[side, 0] + value * valid_ref[side, 0]).astype(BF)
        for k, out_ref in enumerate(out_refs):
            out_ref[side, 0] = value[k * 16 : k * 16 + 16]


def run_close(recv, mean, inv, scaled, pick, weights, valid, base):
    both = lambda *shape: pl.BlockSpec((2, 1, *shape), lambda t: (0, t) + (0,) * len(shape))
    return pl.pallas_call(
        close_kernel,
        grid=(T,),
        in_specs=[
            each_spec(16, 2, H // 2, W), each_spec(H, W), each_spec(H, W), each_spec(C, H, W),
            whole_spec(4, 2 * W, W), whole_spec(2, C, C), both(1, W), both(C, W),
        ],
        out_specs=[both(16, W)] * 4,
        out_shape=[jax.ShapeDtypeStruct((2, T, 16, W), BF)] * 4,
        compiler_params=params(58),
        name="close_sums",
    )(recv, mean, inv, scaled, pick, weights, valid, base)


def from_member(value, k):
    return lax.ppermute(value, "col", [(i, i ^ k) for i in range(8)])


def swap_cores(value):
    return from_member(value, 1)


def exchange(value):
    return lax.all_to_all(value, AXES, split_axis=0, concat_axis=0, tiled=True)


def in_order(core, mine, other, axis):
    first = jnp.where(core == 0, mine, other)
    second = jnp.where(core == 0, other, mine)
    return jnp.concatenate([first, second], axis=axis)


def by_member(value, member):
    lead, last = value.shape[:-2], value.shape[-1]
    cut = value.reshape(*lead, 2, 2, 16, last)
    cut = jnp.where(member % 2 == 1, cut[..., ::-1, :, :], cut)
    cut = jnp.where(member // 2 == 1, cut[..., ::-1, :, :, :], cut)
    return cut.reshape(*lead, 64, last)


def expand(weights):
    to = jnp.asarray(np.kron(np.eye(C), np.ones((8, 1))), BF)
    tall = jnp.einsum("ac,ncd->nad", to, weights, preferred_element_type=F32).astype(BF)
    wide = jnp.einsum("nad,bd->nab", tall, to, preferred_element_type=F32)
    index = jnp.arange(K8, dtype=jnp.int32) % 8
    return jnp.where(index[:, None] == index[None, :], wide, 0.0).astype(BF)


def per_device(
    template_pair,
    template_feat,
    block_map,
    block_count,
    residue_mask,
    row_embed,
    col_embed,
    norm_gain,
    left_proj,
    right_proj,
    gate_proj,
    out_proj,
    embed_grad,
):
    row = lax.axis_index("row")
    col = lax.axis_index("col")
    core = col % 2
    me = row * 8 + col
    own = me // 32
    pair_at = me % 32
    blocks = jnp.arange(128, dtype=jnp.int32)
    half = row % 2
    row_block = row // 2

    member = col % 4
    sent_feat = jnp.broadcast_to(template_feat.reshape(1, 4, 16, W), (32, 4, 16, W))
    pool = exchange(sent_feat.reshape(128, 16, W))
    gain = norm_gain.astype(F32)
    column_ids = lambda m, at: lax.dynamic_index_in_dim(m, at, axis=1, keepdims=False)
    row_ids = column_ids(block_map, row_block)
    member_ids = [column_ids(block_map, col ^ k) for k in range(4)]
    wanted = jnp.concatenate([jnp.concatenate([ids, row_ids]) for ids in member_ids])
    choose = (wanted[:, None] == blocks[None, :]).astype(BF)
    picked = jnp.einsum(
        "eb,bx->ex", choose, pool.reshape(128, 16 * W), preferred_element_type=F32
    ).astype(BF)
    picked = picked.reshape(4, 8, 16, W)
    feats = jnp.concatenate(
        [picked[0]] + [from_member(picked[k], k) for k in range(1, 4)], axis=1
    )
    embeds = by_member(jnp.stack([row_embed, col_embed]), member)

    offsets = jnp.arange(W, dtype=jnp.int32)

    def marks(at):
        kept = lax.dynamic_slice_in_dim(residue_mask, at * W, W, axis=1) == 1
        return kept & (offsets[None, :] < column_ids(block_count, at)[:, None])

    col_valid = marks(col).astype(F32)
    row_valid = (marks(row_block) & (offsets // H == half)[None, :]).astype(F32)
    valid = jnp.stack([row_valid, col_valid])[:, :, None, :]
    turned = jnp.swapaxes(embeds, 1, 2)
    kl, kr = expand(jnp.stack([left_proj.T, right_proj.T]))
    group = 2 * np.arange(4)[:, None, None] + (np.arange(2 * W) // W)[None, :, None]
    lanes = np.arange(W)[None, None, :] % H // 8 == group
    terms_pick = jnp.asarray(np.tile(lanes.transpose(0, 2, 1), (1, 2, 1)), BF)
    sums_pick = jnp.where((offsets // H == half)[None, None, :], jnp.asarray(lanes, BF), 0)

    terms = (template_pair, feats, turned, valid, terms_pick, norm_gain.reshape(1, C))
    sent, inv = run_norm(*terms, kl, kr)
    sent, gate_late, out_late = lax.optimization_barrier((sent, gate_proj, out_proj))
    kg, ko, kb = expand(jnp.stack([gate_late.T, out_late.T, out_late]))
    def center(weights):
        scaled_weights = gain[:, None] * weights.astype(F32)
        return scaled_weights - jnp.mean(scaled_weights, axis=0, keepdims=True)

    embeds = embeds.astype(F32)
    mixed = jnp.einsum(
        "efd,kdc->kefc",
        embeds,
        jnp.stack([center(left_proj), center(right_proj), center(gate_proj)]),
        precision=HIGHEST,
    )
    closing = -embeds / gain[None, None, :]
    opening = embeds * (1.0 / T)
    weights = lax.dynamic_slice_in_dim(mixed[:2], 2 * pair_at, 2, axis=3)
    own_map = lax.dynamic_index_in_dim(block_map, own, axis=0, keepdims=False)
    own_count = lax.dynamic_index_in_dim(block_count, own, axis=0, keepdims=False)
    own_marks = lax.dynamic_index_in_dim(residue_mask, own, axis=0, keepdims=False)
    own_valid = (offsets[None, :] < own_count[:, None]) & (own_marks.reshape(8, W) == 1)
    own_valid = own_valid.astype(F32)
    targets = jnp.concatenate(
        [own_map] * 4 + [jnp.concatenate([row_ids, ids]) for ids in member_ids]
    )
    place = (targets[None, :] == blocks[:, None]).astype(BF)
    factors = exchange(sent.reshape(128, ROWS, W))
    scaled, back, pair_sum = run_back(*terms, inv, embed_grad, kg, kb)
    factors, scaled, back, pair_sum, mixed, closing, opening, weights, own_valid, place = (
        lax.optimization_barrier(
            (factors, scaled, back, pair_sum, mixed, closing, opening, weights, own_valid, place)
        )
    )
    first = factors[:64, None, 256:]
    first_other = from_member(first, 2)
    product, first_other, factors = lax.optimization_barrier(
        (run_product(factors), first_other, factors)
    )
    rest = factors[64:, None, 256:]
    prod = exchange(product).reshape(T, C, H, W)
    left, right = run_square(factors)
    prod, left, right, first, rest = lax.optimization_barrier((prod, left, right, first, rest))
    rest_other = from_member(rest, 2)
    grad_prod = run_grad(prod, back)
    grad_prod, first, rest, rest_other = lax.optimization_barrier(
        (grad_prod, first, rest, rest_other)
    )
    grads = exchange(grad_prod.reshape(128, 2 * H, W))
    inv_part = jnp.concatenate(
        [
            in_order(member // 2, first, first_other, 1),
            in_order(member // 2, rest, rest_other, 1),
        ],
        axis=0,
    )[:, :, None]
    inv_all = in_order(core, inv_part, swap_cores(inv_part), 2).reshape(128, H, W)
    inv_matrix = run_matrix(inv_all)
    embedding, gate_mean, gate_rows, gate_cols, out_rows, out_cols = run_gate(
        prod, scaled, embed_grad, pair_sum, inv, kg, ko, sums_pick
    )
    grads, embedding, gate_mean, gate_rows, gate_cols, out_rows, out_cols, inv_matrix = (
        lax.optimization_barrier(
            (grads, embedding, gate_mean, gate_rows, gate_cols, out_rows, out_cols, inv_matrix)
        )
    )
    kept, given, col_sums, row_sums = run_factor(core, left, right, grads, inv_matrix)
    mean_half = run_add(kept, swap_cores(given))
    col_sums, row_sums, mean_half = lax.optimization_barrier((col_sums, row_sums, mean_half))
    recv = exchange(mean_half).reshape(T, 16, 2, H // 2, W)

    base = jnp.einsum(
        "efc,etcp->etfp", mixed[2], jnp.stack([gate_rows, gate_cols]), precision=HIGHEST
    )
    opened = jnp.einsum(
        "efc,ecp->efp", opening, jnp.stack([out_rows, out_cols]), precision=HIGHEST
    )
    base = (base + opened[:, None]) * valid
    owned = jnp.stack([jnp.sum(row_sums, axis=3), jnp.sum(col_sums, axis=2)], axis=2)
    grad_own = jnp.einsum("kefs,sken->fn", weights, owned, precision=HIGHEST)
    grad_own = grad_own.reshape(C, 8, W).transpose(1, 0, 2) * own_valid[:, None, :]
    grad_own = grad_own.astype(BF)
    def quarters(value):
        cut = [value[:, k * 16 : k * 16 + 16] for k in range(4)]
        return [cut[0]] + [from_member(cut[k], k) for k in range(1, 4)]

    own_parts = quarters(grad_own)
    recv, base, *own_parts = lax.optimization_barrier((recv, base, *own_parts))
    closed = run_close(recv, gate_mean, inv, scaled, sums_pick, closing, valid, base)
    closed = [part.reshape(2 * T, 16, W) for part in closed]
    parts = [closed[0]] + [from_member(closed[k], k) for k in range(1, 4)]
    entries = jnp.concatenate([*own_parts, *parts], axis=0)
    placed = jnp.einsum(
        "be,ex->bx", place, entries.reshape(64, 16 * W), preferred_element_type=F32
    ).astype(BF)
    result = exchange(placed.reshape(128, 16, W)).reshape(32, 4 * 16, W)
    feat_grad = jnp.sum(result.astype(F32), axis=0)[None]
    return (embedding, feat_grad)


def solution(mesh):
    return jax.shard_map(
        per_device,
        mesh=mesh,
        in_specs=(
            P(None, None, "row", "col"),
            P(("row", "col"), None, None),
            P(),
            P(),
            P(),
            P(),
            P(),
            P(),
            P(),
            P(),
            P(),
            P(),
            P(None, "row", "col"),
        ),
        out_specs=(P(None, "row", "col"), P(("row", "col"), None, None)),
        check_vma=False,
    )
```
